128 devices in a mesh: seq: 16 (over z_lo, y, core), slot: 8 (over x, z_hi).
Axes of the slice: x: 4, y: 4, z: 4 (z_hi: 2, z_lo: 2; z = z_hi * 2 + z_lo), core: 2. Of those that a mesh axis runs over, the one named last changes fastest.
Arguments:
- tokens: bfloat16 [32768, 1280], P('seq'), may hold values from -6 to 6
- slot_keys: bfloat16 [1280, 1024], P(None, 'slot'), may hold values from -0.4375 to 0.4375
- w_in: bfloat16 [64, 3072, 1280], P('slot', 'seq'), may hold values from -0.15625 to 0.15625
- w_out: bfloat16 [64, 3072, 1280], P('slot', 'seq'), may hold values from -0.109375 to 0.109375
- out_grad: bfloat16 [32768, 1280], P('seq'), may hold values from -6 to 6
Outputs:
- grad_tokens: bfloat16 [32768, 1280], P('seq', 'slot')
- grad_keys: float32 [1280, 1024], P('seq', 'slot')
- grad_w_in: bfloat16 [64, 3072, 1280], P('slot', 'seq')
- grad_w_out: bfloat16 [64, 3072, 1280], P('slot', 'seq')
The draws below stay inside these ranges and needn't reach their ends.
All inputs are finite; a program needn't handle non-finite values.
Results may differ from the reference program's by a relative error of at most 0.04.
Values may be sent and summed in bfloat16 or wider, within the bound.
No kernel may reach another device: no remote copies, remote signals or barrier semaphores. Data moves between devices by JAX's collectives and lax.ppermute only.
A program may use at most 128 MiB of HBM per device.

```python
import jax
import jax.numpy as jnp

D = 1280
HID = 3072
EXP = 64
SLOT_EXP = 16
SLOTS = 1024
TOKENS = 32768


def level_of(own_key, shape, pieces, low, top_value):
    def one(axis_at, shards_of):
        heights = jax.random.uniform(jax.random.fold_in(jax.random.fold_in(own_key, 6), axis_at), (shards_of,), jnp.float32, low / len(pieces), top_value / len(pieces))
        return jnp.repeat(jnp.exp(heights), shape[axis_at] // shards_of).reshape((-1,) + (1,) * (len(shape) - axis_at - 1))

    level = one(*pieces[0])
    for cut in pieces[1:]:
        level = level * one(*cut)
    return level


def centred(stream_key, extent, scale, most, shards=(), kind=jnp.bfloat16):
    gain = level_of(stream_key, extent, shards, -0.22, 0.18) if shards else 1.0
    entries = jax.random.normal(stream_key, extent, jnp.float32) * scale * gain
    return jnp.minimum(jnp.maximum(entries, -most), most).astype(kind)


def setup_inputs(seed: int = 0) -> dict:
    splits = jax.random.split(jax.random.key(seed), 6)
    tokens = centred(splits[0], (TOKENS, D), 1.0, 6.0, ((0, 16),))
    slot_keys = centred(splits[1], (D, SLOTS), (D // 6) ** -0.5, 0.4375, ((1, 8),))
    w_in = centred(splits[2], (EXP, HID, D), D ** -0.5, 0.15625, ((0, 8), (1, 16)))
    w_out = centred(splits[3], (EXP, HID, D), HID ** -0.5, 0.109375, ((0, 8), (1, 16)))
    out_grad = centred(splits[4], (TOKENS, D), 1.0, 6.0, ((0, 16),))
    return dict(tokens=tokens, slot_keys=slot_keys, w_in=w_in, w_out=w_out, out_grad=out_grad)


gelu_scale = 0.7978845608
gelu_cubic = 0.044715


def gelu_tanh(values):
    return 0.5 * values * (1.0 + jnp.tanh(gelu_scale * (values + gelu_cubic * values * values * values)))


def gelu_slope(values):
    bent = jnp.tanh(gelu_scale * (values + gelu_cubic * values * values * values))
    return 0.5 * (1.0 + bent) + 0.5 * values * (1.0 - bent * bent) * gelu_scale * (1.0 + 3.0 * gelu_cubic * values * values)


def reference(tokens, slot_keys, w_in, w_out, out_grad):
    logits = jnp.dot(tokens, slot_keys, preferred_element_type=jnp.float32)
    exp_logits = jnp.exp(logits)
    dispatch = exp_logits / jnp.sum(exp_logits, axis=0, keepdims=True)
    combine = exp_logits / jnp.sum(exp_logits, axis=1, keepdims=True)
    dispatch_low = dispatch.astype(jnp.bfloat16)
    combine_low = combine.astype(jnp.bfloat16)
    slot_in = jnp.dot(dispatch_low.T, tokens, preferred_element_type=jnp.float32)
    slot_in_low = slot_in.astype(jnp.bfloat16)
    grouped_in = slot_in_low.reshape(EXP, SLOT_EXP, D).astype(jnp.float32)
    w_in_wide = w_in.astype(jnp.float32)
    w_out_wide = w_out.astype(jnp.float32)
    hidden_pre = jnp.einsum('esd,ehd->esh', grouped_in, w_in_wide)
    hidden_act = gelu_tanh(hidden_pre).astype(jnp.bfloat16)
    slot_out = jnp.einsum('esh,ehd->esd', hidden_act.astype(jnp.float32), w_out_wide).reshape(SLOTS, D)
    slot_out_low = slot_out.astype(jnp.bfloat16)
    slot_grad = jnp.dot(combine_low.T, out_grad, preferred_element_type=jnp.float32)
    slot_grad_low = slot_grad.astype(jnp.bfloat16)
    comb_dot = jnp.dot(out_grad, slot_out_low.T, preferred_element_type=jnp.float32)
    comb_logit_grad = combine * (comb_dot - jnp.sum(combine * comb_dot, axis=1, keepdims=True))
    grouped_grad = slot_grad_low.reshape(EXP, SLOT_EXP, D).astype(jnp.float32)
    grad_w_out = jnp.einsum('esh,esd->ehd', hidden_act.astype(jnp.float32), grouped_grad).astype(jnp.bfloat16)
    act_grad = jnp.einsum('esd,ehd->esh', grouped_grad, w_out_wide)
    pre_grad = (act_grad * gelu_slope(hidden_pre)).astype(jnp.bfloat16)
    grad_w_in = jnp.einsum('esh,esd->ehd', pre_grad.astype(jnp.float32), grouped_in).astype(jnp.bfloat16)
    slot_in_grad = jnp.einsum('esh,ehd->esd', pre_grad.astype(jnp.float32), w_in_wide).reshape(SLOTS, D)
    in_grad_low = slot_in_grad.astype(jnp.bfloat16)
    disp_dot = jnp.dot(tokens, in_grad_low.T, preferred_element_type=jnp.float32)
    disp_total = jnp.sum(slot_in * in_grad_low.astype(jnp.float32), axis=1)
    disp_logit_grad = dispatch * (disp_dot - disp_total[None, :])
    logit_grad_low = (disp_logit_grad + comb_logit_grad).astype(jnp.bfloat16)
    grad_keys = jnp.dot(tokens.T, logit_grad_low, preferred_element_type=jnp.float32)
    token_sum = jnp.dot(logit_grad_low, slot_keys.T, preferred_element_type=jnp.float32)
    token_sum = token_sum + jnp.dot(dispatch_low, in_grad_low, preferred_element_type=jnp.float32)
    grad_tokens = token_sum.astype(jnp.bfloat16)
    return grad_tokens, grad_keys, grad_w_in, grad_w_out
```

```python
import jax
import jax.numpy as jnp
from jax import lax
from jax.sharding import Mesh, PartitionSpec as P

gelu_scale = 0.7978845608
gelu_cubic = 0.044715
rows_contract = (((0,), (0,)), ((), ()))
cols_contract = (((1,), (1,)), ((), ()))

SEQ = ("zl", "y", "c")
SLOT = ("x", "zh")
SAME_CORE = ("x", "zh", "zl", "y")
f32 = jnp.float32
bf16 = jnp.bfloat16


def gelu_tanh(values):
    return (
        0.5
        * values
        * (1.0 + jnp.tanh(gelu_scale * (values + gelu_cubic * values * values * values)))
    )


def gelu_slope(values):
    bent = jnp.tanh(gelu_scale * (values + gelu_cubic * values * values * values))
    return 0.5 * (1.0 + bent) + 0.5 * values * (1.0 - bent * bent) * gelu_scale * (
        1.0 + 3.0 * gelu_cubic * values * values
    )


def to_blocks(first, second, groups):
    slots, width = first.shape
    both = jnp.stack([first, second]).reshape(2, groups, slots // groups, 2, width // 2)
    return both.transpose(1, 3, 0, 2, 4).reshape(groups * 2, 2, slots // groups, width // 2)


def per_device(tokens, slot_keys, w_in, w_out, out_grad):
    token_count, features = tokens.shape
    experts = w_in.shape[0]
    own_slots = slot_keys.shape[1]
    core = lax.axis_index("c")
    slot_at = lax.axis_index(SLOT)
    half = features // 2
    slot_devices = lax.axis_size(SLOT)
    seq_devices = lax.axis_size(SEQ)
    groups = seq_devices // 2
    block = own_slots // groups
    everyone = slot_devices * groups

    keys_all = lax.all_gather(slot_keys, SLOT, axis=0, tiled=False)

    logits = jnp.dot(tokens, slot_keys, preferred_element_type=f32)
    exp_logits = jnp.exp(logits)
    own_column = jnp.sum(exp_logits, axis=0)
    own_row = jnp.sum(exp_logits, axis=1)
    row_parts = lax.all_to_all(
        jnp.broadcast_to(own_row.reshape(1, -1, 128), (slot_devices, token_count // 128, 128)),
        SLOT, 0, 0,
    )
    row_total = jnp.sum(row_parts, axis=0).reshape(-1)
    safe_column = jnp.where(own_column > 0, own_column, 1.0)
    dispatch_own = (exp_logits / safe_column[None, :]).astype(bf16)
    slot_in_part = lax.dot_general(
        dispatch_own, tokens, rows_contract, preferred_element_type=f32
    ).astype(bf16)
    combine_own = (exp_logits / row_total[:, None]).astype(bf16)
    slot_grad_part = lax.dot_general(
        combine_own, out_grad, rows_contract, preferred_element_type=f32
    ).astype(bf16)
    parts = lax.all_to_all(to_blocks(slot_in_part, slot_grad_part, groups), SEQ, 0, 0)
    column_sent = jnp.broadcast_to(
        own_column.reshape(groups, 1, 1, block), (groups, 2, 8, block)
    ).reshape(seq_devices, 8, block)
    column_parts = lax.all_to_all(column_sent, SEQ, 0, 0)[:, 0, :]
    column_total = jnp.sum(column_parts, axis=0)
    share = column_parts / column_total[None, :]
    slot_in_block = jnp.sum(parts[:, 0].astype(f32) * share[:, :, None], axis=0)
    slot_grad_block = jnp.sum(parts[:, 1].astype(f32), axis=0)
    sent = jnp.stack([slot_in_block, slot_grad_block]).astype(bf16)
    whole = lax.all_to_all(
        jnp.broadcast_to(sent[None], (seq_devices,) + sent.shape), SEQ, 0, 0
    )
    whole = whole.reshape(groups, 2, 2, block, half).transpose(2, 0, 3, 1, 4)
    whole = whole.reshape(2, experts, own_slots // experts, features)
    grouped_in, grouped_grad = whole[0], whole[1]

    hidden_pre = jnp.einsum("esd,ehd->esh", grouped_in, w_in, preferred_element_type=f32)
    hidden_act = gelu_tanh(hidden_pre).astype(bf16)
    out_terms = jnp.einsum("esh,ehd->esd", hidden_act, w_out, preferred_element_type=f32)
    act_grad = jnp.einsum("esd,ehd->esh", grouped_grad, w_out, preferred_element_type=f32)
    pre_grad = (act_grad * gelu_slope(hidden_pre)).astype(bf16)
    in_terms = jnp.einsum("esh,ehd->esd", pre_grad, w_in, preferred_element_type=f32)
    grad_w_out = jnp.einsum(
        "esh,esd->ehd", hidden_act, grouped_grad, preferred_element_type=f32
    ).astype(bf16)
    grad_w_in = jnp.einsum(
        "esh,esd->ehd", pre_grad, grouped_in, preferred_element_type=f32
    ).astype(bf16)
    terms = lax.all_to_all(
        to_blocks(
            out_terms.reshape(-1, features).astype(bf16),
            in_terms.reshape(-1, features).astype(bf16),
            groups,
        ),
        SEQ, 0, 0,
    )
    summed = jnp.sum(terms.astype(f32), axis=0).astype(bf16)
    disp_half = jnp.sum(slot_in_block * summed[1].astype(f32), axis=1)
    extra = jnp.concatenate([column_total, disp_half]).reshape(1, -1)
    gathered = lax.all_to_all(
        jnp.broadcast_to(summed[None], (everyone,) + summed.shape), SAME_CORE, 0, 0
    )
    extras = lax.all_to_all(
        jnp.broadcast_to(extra[None], (everyone, 8, extra.shape[1])), SAME_CORE, 0, 0
    )[:, 0, :]
    swap = [(0, 1), (1, 0)]
    gathered_other = lax.ppermute(gathered, "c", swap)
    extras_other = lax.ppermute(extras, "c", swap)
    column_all = extras[:, :block].reshape(-1)
    disp_total = (extras[:, block:] + extras_other[:, block:]).reshape(-1)

    def whole_width(of):
        mine = gathered[:, of].reshape(-1, half)
        other = gathered_other[:, of].reshape(-1, half)
        low = jnp.where(core == 0, mine, other)
        high = jnp.where(core == 0, other, mine)
        return jnp.concatenate([low, high], axis=1)

    slot_out = whole_width(0)
    in_grad = whole_width(1)
    keys = keys_all.transpose(1, 0, 2).reshape(features, -1)

    exp_all = jnp.exp(jnp.dot(tokens, keys, preferred_element_type=f32))
    combine = exp_all / row_total[:, None]
    dispatch = exp_all / column_all[None, :]
    comb_dot = lax.dot_general(out_grad, slot_out, cols_contract, preferred_element_type=f32)
    disp_dot = lax.dot_general(tokens, in_grad, cols_contract, preferred_element_type=f32)
    comb_row = jnp.sum(combine * comb_dot, axis=1)
    logit_grad = (
        dispatch * (disp_dot - disp_total[None, :]) + combine * (comb_dot - comb_row[:, None])
    ).astype(bf16)
    dispatch_low = dispatch.astype(bf16)
    own_logit_grad = lax.dynamic_slice_in_dim(logit_grad, slot_at * own_slots, own_slots, 1)
    keys_part = lax.dot_general(
        tokens, own_logit_grad, rows_contract, preferred_element_type=f32
    ).astype(bf16)
    keys_parts = lax.all_to_all(
        keys_part.reshape(seq_devices, features // seq_devices, own_slots), SEQ, 0, 0
    )
    grad_keys = jnp.sum(keys_parts.astype(f32), axis=0)
    width = features // slot_devices
    keys_rows = lax.dynamic_slice_in_dim(keys, slot_at * width, width, 0)
    in_grad_cols = lax.dynamic_slice_in_dim(in_grad, slot_at * width, width, 1)
    grad_tokens = lax.dot_general(logit_grad, keys_rows, cols_contract, preferred_element_type=f32)
    grad_tokens = grad_tokens + jnp.dot(dispatch_low, in_grad_cols, preferred_element_type=f32)
    return (grad_tokens.astype(bf16), grad_keys, grad_w_in, grad_w_out)


def solution(mesh):
    fine = Mesh(mesh.devices.reshape(2, 4, 2, 4, 2), ("zl", "y", "c", "x", "zh"))
    placed = (
        P(SEQ, None),
        P(None, SLOT),
        P(SLOT, SEQ, None),
        P(SLOT, SEQ, None),
        P(SEQ, None),
    )
    return jax.shard_map(
        per_device,
        mesh=fine,
        in_specs=placed,
        out_specs=(
            P(SEQ, SLOT),
            P(SEQ, SLOT),
            P(SLOT, SEQ, None),
            P(SLOT, SEQ, None),
        ),
        check_vma=False,
    )
```

```python
import jax
import jax.numpy as jnp
from jax import lax
from jax.experimental import pallas as pl
from jax.experimental.pallas import tpu as pltpu
from jax.sharding import Mesh, PartitionSpec as P

gelu_scale = 0.7978845608
gelu_cubic = 0.044715
rows_contract = (((0,), (0,)), ((), ()))
cols_contract = (((1,), (1,)), ((), ()))

SEQ = ("zl", "y", "c")
SLOT = ("x", "zh")
SAME_CORE = ("x", "zh", "zl", "y")
f32 = jnp.float32
bf16 = jnp.bfloat16
LANES = 128
MIB = 1 << 20


def gelu_tanh(values):
    return (
        0.5
        * values
        * (1.0 + jnp.tanh(gelu_scale * (values + gelu_cubic * values * values * values)))
    )


def gelu_slope(values):
    bent = jnp.tanh(gelu_scale * (values + gelu_cubic * values * values * values))
    return 0.5 * (1.0 + bent) + 0.5 * values * (1.0 - bent * bent) * gelu_scale * (
        1.0 + 3.0 * gelu_cubic * values * values
    )


def guarded(total):
    power = jnp.where(total > 2.0**64, 2.0**-32, jnp.where(total < 2.0**-64, 2.0**32, 1.0))
    return power, 1.0 / (total * power)


def two_parts(values):
    high = values.astype(bf16).astype(f32)
    return high, values - high


def in_lanes(rows, columns):
    lane = lax.broadcasted_iota(jnp.int32, (rows, LANES), 1)
    laid = jnp.zeros((rows, LANES), f32)
    for at, column in enumerate(columns):
        laid = jnp.where(lane == at, column, laid)
    return laid.astype(bf16)


def params(mib):
    return pltpu.CompilerParams(vmem_limit_bytes=mib * MIB)


def cost(flops, nbytes):
    return pl.CostEstimate(flops=flops, bytes_accessed=nbytes, transcendentals=0)


def whole_in_vmem():
    return pl.BlockSpec(memory_space=pltpu.VMEM)


def own_logits(keys_t, tokens, copies, tile=512):
    slots, features = keys_t.shape
    count = tokens.shape[0]

    def kernel(keys_ref, tokens_ref, exp_ref, row_ref, column_ref):
        exps = jnp.exp(
            lax.dot_general(keys_ref[...], tokens_ref[...], cols_contract, preferred_element_type=f32)
        )
        exp_ref[...] = exps
        row_ref[...] = jnp.broadcast_to(
            jnp.sum(exps, axis=0, keepdims=True)[None], (copies, 1, tile)
        )
        by_lane = exps[:, :LANES]
        for at in range(1, tile // LANES):
            by_lane = by_lane + exps[:, at * LANES : (at + 1) * LANES]

        @pl.when(pl.program_id(0) == 0)
        def _():
            column_ref[...] = by_lane

        @pl.when(pl.program_id(0) > 0)
        def _():
            column_ref[...] += by_lane

    return pl.pallas_call(
        kernel,
        grid=(count // tile,),
        in_specs=[
            pl.BlockSpec((slots, features), lambda i: (0, 0)),
            pl.BlockSpec((tile, features), lambda i: (i, 0)),
        ],
        out_specs=[
            pl.BlockSpec((slots, tile), lambda i: (0, i)),
            pl.BlockSpec((copies, 1, tile), lambda i: (0, 0, i)),
            pl.BlockSpec((slots, LANES), lambda i: (0, 0)),
        ],
        out_shape=[
            jax.ShapeDtypeStruct((slots, count), f32),
            jax.ShapeDtypeStruct((copies, 1, count), f32),
            jax.ShapeDtypeStruct((slots, LANES), f32),
        ],
        compiler_params=params(32),
        cost_estimate=cost(2 * slots * features * count, 2 * features * count + 4 * slots * count),
        name="own_logits",
    )(keys_t, tokens)


def dispatch_part(exps, column, tokens, tile=512):
    slots, count = exps.shape
    features = tokens.shape[1]

    def kernel(exp_ref, column_ref, tokens_ref, out_ref, total_ref):
        total = jnp.sum(column_ref[...], axis=1, keepdims=True)
        power, inverse = guarded(jnp.where(total > 0, total, 1.0))
        weights = ((exp_ref[...] * power) * inverse).astype(bf16)
        term = jnp.dot(weights, tokens_ref[...], preferred_element_type=f32)

        @pl.when(pl.program_id(0) == 0)
        def _():
            total_ref[...] = term

        @pl.when(pl.program_id(0) > 0)
        def _():
            total_ref[...] += term

        @pl.when(pl.program_id(0) == pl.num_programs(0) - 1)
        def _():
            out_ref[...] = total_ref[...].astype(bf16)

    return pl.pallas_call(
        kernel,
        grid=(count // tile,),
        in_specs=[
            pl.BlockSpec((slots, tile), lambda i: (0, i)),
            pl.BlockSpec((slots, LANES), lambda i: (0, 0)),
            pl.BlockSpec((tile, features), lambda i: (i, 0)),
        ],
        out_specs=pl.BlockSpec((slots, features), lambda i: (0, 0)),
        out_shape=jax.ShapeDtypeStruct((slots, features), bf16),
        scratch_shapes=[pltpu.VMEM((slots, features), f32)],
        compiler_params=params(32),
        cost_estimate=cost(2 * slots * features * count, 2 * features * count + 4 * slots * count),
        name="dispatch_part",
    )(exps, column, tokens)


def combine_part(exps, row_parts, column, slot_in_part, out_grad, groups, tile=512):
    slots, count = exps.shape
    features = out_grad.shape[1]
    half = features // 2
    block = slots // groups
    width = features + LANES
    copies = row_parts.shape[0]

    def kernel(exp_ref, row_ref, column_ref, in_ref, grad_ref, sent_ref, total_ref):
        power, inverse = guarded(jnp.sum(row_ref[...], axis=0))
        weights = ((exp_ref[...] * power) * inverse).astype(bf16)
        term = jnp.dot(weights, grad_ref[...], preferred_element_type=f32)

        @pl.when(pl.program_id(0) == 0)
        def _():
            total_ref[...] = term

        @pl.when(pl.program_id(0) > 0)
        def _():
            total_ref[...] += term

        @pl.when(pl.program_id(0) == pl.num_programs(0) - 1)
        def _():
            total = jnp.sum(column_ref[...], axis=1, keepdims=True)
            shift, _unused = guarded(total)
            high, low = two_parts(total * shift)
            lanes = in_lanes(slots, (high, low, 1.0 / shift))
            grad = total_ref[...].astype(bf16)
            for group in range(groups):
                rows = slice(group * block, (group + 1) * block)
                for side in range(2):
                    cut = slice(side * half, (side + 1) * half)
                    sent_ref[group * 2 + side, :, :half] = in_ref[rows, cut]
                    sent_ref[group * 2 + side, :, half:features] = grad[rows, cut]
                    sent_ref[group * 2 + side, :, features:] = lanes[rows]

    return pl.pallas_call(
        kernel,
        grid=(count // tile,),
        in_specs=[
            pl.BlockSpec((slots, tile), lambda i: (0, i)),
            pl.BlockSpec((copies, 1, tile), lambda i: (0, 0, i)),
            pl.BlockSpec((slots, LANES), lambda i: (0, 0)),
            pl.BlockSpec((slots, features), lambda i: (0, 0)),
            pl.BlockSpec((tile, features), lambda i: (i, 0)),
        ],
        out_specs=pl.BlockSpec((groups * 2, block, width), lambda i: (0, 0, 0)),
        out_shape=jax.ShapeDtypeStruct((groups * 2, block, width), bf16),
        scratch_shapes=[pltpu.VMEM((slots, features), f32)],
        compiler_params=params(32),
        cost_estimate=cost(2 * slots * features * count, 2 * features * count + 4 * slots * count),
        name="combine_part",
    )(exps, row_parts, column, slot_in_part, out_grad)


def sum_slots(parts, copies):
    sources, block, width = parts.shape
    features = width - LANES
    half = features // 2

    def kernel(parts_ref, sent_ref, in_ref, column_ref):
        lanes = parts_ref[:, :, features:].astype(f32)
        columns = (lanes[:, :, 0:1] + lanes[:, :, 1:2]) * lanes[:, :, 2:3]
        total = jnp.sum(columns, axis=0)
        power, inverse = guarded(total)
        share = (columns * power[None]) * inverse[None]
        slot_in = jnp.zeros((block, half), f32)
        slot_grad = jnp.zeros((block, half), f32)
        for source in range(sources):
            slot_in = slot_in + parts_ref[source, :, :half].astype(f32) * share[source]
            slot_grad = slot_grad + parts_ref[source, :, half:features].astype(f32)
        in_ref[...] = slot_in
        column_ref[...] = jnp.broadcast_to(total, (block, LANES))
        in_low = slot_in.astype(bf16)
        grad_low = slot_grad.astype(bf16)
        for copy in range(copies):
            sent_ref[copy, :, :half] = in_low
            sent_ref[copy, :, half:] = grad_low

    return pl.pallas_call(
        kernel,
        in_specs=[whole_in_vmem()],
        out_specs=[whole_in_vmem()] * 3,
        out_shape=[
            jax.ShapeDtypeStruct((copies, block, features), bf16),
            jax.ShapeDtypeStruct((block, half), f32),
            jax.ShapeDtypeStruct((block, LANES), f32),
        ],
        compiler_params=params(32),
        name="sum_slots",
    )(parts)


def experts_part(whole, w_in, w_out):
    experts, hidden, features = w_in.shape
    block = whole.shape[1]
    half = features // 2

    def kernel(whole_ref, w_in_ref, w_out_ref, terms_ref, act_ref, pre_ref):
        slots = jnp.concatenate([whole_ref[0, :, :half], whole_ref[1, :, :half]], axis=1)
        grads = jnp.concatenate([whole_ref[0, :, half:], whole_ref[1, :, half:]], axis=1)
        hidden_pre = lax.dot_general(slots, w_in_ref[0], cols_contract, preferred_element_type=f32)
        act_grad = lax.dot_general(grads, w_out_ref[0], cols_contract, preferred_element_type=f32)
        act = gelu_tanh(hidden_pre).astype(bf16)
        pre = (act_grad * gelu_slope(hidden_pre)).astype(bf16)
        out_terms = jnp.dot(act, w_out_ref[0], preferred_element_type=f32).astype(bf16)
        in_terms = jnp.dot(pre, w_in_ref[0], preferred_element_type=f32).astype(bf16)
        for side in range(2):
            cut = slice(side * half, (side + 1) * half)
            terms_ref[side, :, :half] = out_terms[:, cut]
            terms_ref[side, :, half:] = in_terms[:, cut]
        act_ref[0] = act
        pre_ref[0] = pre

    return pl.pallas_call(
        kernel,
        grid=(experts,),
        in_specs=[
            pl.BlockSpec((2, block, features), lambda e: (e, 0, 0)),
            pl.BlockSpec((1, hidden, features), lambda e: (e, 0, 0)),
            pl.BlockSpec((1, hidden, features), lambda e: (e, 0, 0)),
        ],
        out_specs=[
            pl.BlockSpec((2, block, features), lambda e: (e, 0, 0)),
            pl.BlockSpec((1, block, hidden), lambda e: (e, 0, 0)),
            pl.BlockSpec((1, block, hidden), lambda e: (e, 0, 0)),
        ],
        out_shape=[
            jax.ShapeDtypeStruct(whole.shape, bf16),
            jax.ShapeDtypeStruct((experts, block, hidden), bf16),
            jax.ShapeDtypeStruct((experts, block, hidden), bf16),
        ],
        compiler_params=params(32),
        cost_estimate=cost(8 * experts * block * hidden * features, 4 * experts * hidden * features),
        name="experts_part",
    )(whole, w_in, w_out)


def weight_grads(whole, act, pre, hidden_shape):
    experts, hidden, features = hidden_shape
    block = whole.shape[1]
    half = features // 2

    def kernel(whole_ref, act_ref, pre_ref, in_ref, out_ref):
        for side in range(2):
            cut = slice(side * half, (side + 1) * half)
            in_ref[0, :, cut] = lax.dot_general(
                pre_ref[0], whole_ref[side, :, :half], rows_contract, preferred_element_type=f32
            ).astype(bf16)
            out_ref[0, :, cut] = lax.dot_general(
                act_ref[0], whole_ref[side, :, half:], rows_contract, preferred_element_type=f32
            ).astype(bf16)

    return pl.pallas_call(
        kernel,
        grid=(experts,),
        in_specs=[
            pl.BlockSpec((2, block, features), lambda e: (e, 0, 0)),
            pl.BlockSpec((1, block, hidden), lambda e: (e, 0, 0)),
            pl.BlockSpec((1, block, hidden), lambda e: (e, 0, 0)),
        ],
        out_specs=[pl.BlockSpec((1, hidden, features), lambda e: (e, 0, 0))] * 2,
        out_shape=[jax.ShapeDtypeStruct(hidden_shape, bf16)] * 2,
        compiler_params=params(32),
        cost_estimate=cost(4 * experts * block * hidden * features, 4 * experts * hidden * features),
        name="weight_grads",
    )(whole, act, pre)


def sum_terms(terms, slot_in, column, copies):
    sources, block, features = terms.shape
    half = features // 2
    width = features + LANES

    def kernel(terms_ref, in_ref, column_ref, sent_ref):
        total = terms_ref[0].astype(f32)
        for source in range(1, sources):
            total = total + terms_ref[source].astype(f32)
        low = total.astype(bf16)
        inner = jnp.sum(in_ref[...] * low[:, half:].astype(f32), axis=1, keepdims=True)
        power, inverse = guarded(column_ref[:, 0:1])
        lanes = in_lanes(block, two_parts(inverse) + (power,) + two_parts(inner))
        for copy in range(copies):
            sent_ref[copy, :, :features] = low
            sent_ref[copy, :, features:] = lanes

    return pl.pallas_call(
        kernel,
        in_specs=[whole_in_vmem()] * 3,
        out_specs=whole_in_vmem(),
        out_shape=jax.ShapeDtypeStruct((copies, block, width), bf16),
        compiler_params=params(32),
        name="sum_terms",
    )(terms, slot_in, column)


def all_exps(keys_t, tokens, tile=256):
    slots, features = keys_t.shape
    count = tokens.shape[0]

    def kernel(keys_ref, tokens_ref, exp_ref):
        exp_ref[...] = jnp.exp(
            lax.dot_general(keys_ref[...], tokens_ref[...], cols_contract, preferred_element_type=f32)
        )

    return pl.pallas_call(
        kernel,
        grid=(count // tile,),
        in_specs=[
            pl.BlockSpec((slots, features), lambda i: (0, 0)),
            pl.BlockSpec((tile, features), lambda i: (i, 0)),
        ],
        out_specs=pl.BlockSpec((slots, tile), lambda i: (0, i)),
        out_shape=jax.ShapeDtypeStruct((slots, count), f32),
        compiler_params=params(32),
        cost_estimate=cost(2 * slots * features * count, 2 * features * count + 4 * slots * count),
        name="all_exps",
    )(keys_t, tokens)


def logit_grads(place, exps, tokens, out_grad, row_parts, mine, other, own_slots, tile=256):
    slots, count = exps.shape
    features = tokens.shape[1]
    half = features // 2
    blocks, block, width = mine.shape
    copies = row_parts.shape[0]

    def kernel(
        place_ref, exp_ref, tokens_ref, grad_ref, row_ref, mine_ref, other_ref,
        logit_ref, dispatch_ref, keys_ref, power_ref, inverse_ref, total_ref, sum_ref,
    ):
        core = place_ref[0]
        here = pl.multiple_of(core * half, LANES)
        there = pl.multiple_of((1 - core) * half, LANES)
        step = pl.program_id(0)

        @pl.when(step == 0)
        def _():
            lanes = mine_ref[:, :, features:].reshape(slots, LANES).astype(f32)
            apart = other_ref[:, :, features:].reshape(slots, LANES).astype(f32)
            inner = lanes[:, 3:4] + lanes[:, 4:5] + apart[:, 3:4] + apart[:, 4:5]
            power_ref[...] = jnp.broadcast_to(lanes[:, 2:3], (slots, tile))
            inverse_ref[...] = jnp.broadcast_to(lanes[:, 0:1] + lanes[:, 1:2], (slots, tile))
            total_ref[...] = jnp.broadcast_to(inner, (slots, tile))

        def dot(at, ref):
            near = lax.dot_general(
                mine_ref[:, :, at * half : (at + 1) * half].reshape(slots, half),
                ref[:, pl.ds(here, half)],
                cols_contract,
                preferred_element_type=f32,
            )
            far = lax.dot_general(
                other_ref[:, :, at * half : (at + 1) * half].reshape(slots, half),
                ref[:, pl.ds(there, half)],
                cols_contract,
                preferred_element_type=f32,
            )
            return near + far

        power, inverse = guarded(jnp.sum(row_ref[...], axis=0))
        exps_here = exp_ref[...]
        combine = (exps_here * power) * inverse
        comb_dot = dot(0, grad_ref)
        comb_row = jnp.sum(combine * comb_dot, axis=0, keepdims=True)
        dispatch = (exps_here * power_ref[...]) * inverse_ref[...]
        disp_dot = dot(1, tokens_ref)
        logit = combine * (comb_dot - comb_row) + dispatch * (disp_dot - total_ref[...])
        logit_ref[...] = logit.astype(bf16)
        dispatch_ref[...] = dispatch.astype(bf16)
        own = logit_ref[pl.ds(pl.multiple_of(place_ref[1] * own_slots, own_slots), own_slots), :]
        term = jnp.dot(own, tokens_ref[...], preferred_element_type=f32)

        @pl.when(step == 0)
        def _():
            sum_ref[...] = term

        @pl.when(step > 0)
        def _():
            sum_ref[...] += term

        @pl.when(step == pl.num_programs(0) - 1)
        def _():
            keys_ref[...] = sum_ref[...].T.astype(bf16)

    return pl.pallas_call(
        kernel,
        grid_spec=pltpu.PrefetchScalarGridSpec(
            num_scalar_prefetch=1,
            grid=(count // tile,),
            in_specs=[
                pl.BlockSpec((slots, tile), lambda i, place: (0, i)),
                pl.BlockSpec((tile, features), lambda i, place: (i, 0)),
                pl.BlockSpec((tile, features), lambda i, place: (i, 0)),
                pl.BlockSpec((copies, 1, tile), lambda i, place: (0, 0, i)),
                pl.BlockSpec((blocks, block, width), lambda i, place: (0, 0, 0)),
                pl.BlockSpec((blocks, block, width), lambda i, place: (0, 0, 0)),
            ],
            out_specs=[
                pl.BlockSpec((slots, tile), lambda i, place: (0, i)),
                pl.BlockSpec((slots, tile), lambda i, place: (0, i)),
                pl.BlockSpec((features, own_slots), lambda i, place: (0, 0)),
            ],
            scratch_shapes=[
                pltpu.VMEM((slots, tile), f32),
                pltpu.VMEM((slots, tile), f32),
                pltpu.VMEM((slots, tile), f32),
                pltpu.VMEM((own_slots, features), f32),
            ],
        ),
        out_shape=[
            jax.ShapeDtypeStruct((slots, count), bf16),
            jax.ShapeDtypeStruct((slots, count), bf16),
            jax.ShapeDtypeStruct((features, own_slots), bf16),
        ],
        compiler_params=params(56),
        cost_estimate=cost(4 * slots * features * count, 4 * features * count + 8 * slots * count),
        name="logit_grads",
    )(place, exps, tokens, out_grad, row_parts, mine, other)


def token_grads(keys_rows, in_grad_rows, logit_grad, dispatch, tile=512):
    width, slots = keys_rows.shape
    count = logit_grad.shape[1]

    def kernel(keys_ref, in_ref, logit_ref, dispatch_ref, out_ref):
        total = jnp.dot(keys_ref[...], logit_ref[...], preferred_element_type=f32)
        total = total + jnp.dot(in_ref[...], dispatch_ref[...], preferred_element_type=f32)
        out_ref[...] = total.T.astype(bf16)

    return pl.pallas_call(
        kernel,
        grid=(count // tile,),
        in_specs=[
            pl.BlockSpec((width, slots), lambda i: (0, 0)),
            pl.BlockSpec((width, slots), lambda i: (0, 0)),
            pl.BlockSpec((slots, tile), lambda i: (0, i)),
            pl.BlockSpec((slots, tile), lambda i: (0, i)),
        ],
        out_specs=pl.BlockSpec((tile, width), lambda i: (i, 0)),
        out_shape=jax.ShapeDtypeStruct((count, width), bf16),
        compiler_params=params(32),
        cost_estimate=cost(4 * slots * width * count, 4 * slots * count),
        name="token_grads",
    )(keys_rows, in_grad_rows, logit_grad, dispatch)


def per_device(tokens, slot_keys, w_in, w_out, out_grad):
    features = tokens.shape[1]
    own_slots = slot_keys.shape[1]
    core = lax.axis_index("c")
    slot_at = lax.axis_index(SLOT)
    half = features // 2
    slot_devices = lax.axis_size(SLOT)
    seq_devices = lax.axis_size(SEQ)
    groups = seq_devices // 2
    everyone = slot_devices * groups

    keys_t = slot_keys.T
    keys_all = lax.all_gather(keys_t, SLOT, axis=0, tiled=True)

    exps, own_row, column = own_logits(keys_t, tokens, slot_devices)
    row_parts = lax.all_to_all(own_row, SLOT, 0, 0)
    slot_in_part = dispatch_part(exps, column, tokens)
    parts = lax.all_to_all(
        combine_part(exps, row_parts, column, slot_in_part, out_grad, groups), SEQ, 0, 0
    )
    sent, slot_in, column_total = sum_slots(parts, seq_devices)
    whole = lax.all_to_all(sent, SEQ, 0, 0)

    sent, act, pre = experts_part(whole, w_in, w_out)
    terms = lax.all_to_all(sent, SEQ, 0, 0)
    grad_w_in, grad_w_out = weight_grads(whole, act, pre, w_in.shape)
    mine = lax.all_to_all(
        sum_terms(terms, slot_in, column_total, everyone), SAME_CORE, 0, 0
    )
    other = lax.ppermute(mine, "c", [(0, 1), (1, 0)])

    all_exp = all_exps(keys_all, tokens)
    place = jnp.stack([core, slot_at]).astype(jnp.int32)
    logit_grad, dispatch, keys_part = logit_grads(
        place, all_exp, tokens, out_grad, row_parts, mine, other, own_slots
    )
    keys_parts = lax.all_to_all(
        keys_part.reshape(seq_devices, features // seq_devices, own_slots), SEQ, 0, 0
    )
    grad_keys = jnp.sum(keys_parts.astype(f32), axis=0)

    width = features // slot_devices
    keys_rows = lax.dynamic_slice_in_dim(keys_all, slot_at * width, width, 1).T
    side = (slot_at * width) // half
    at = half + slot_at * width - side * half
    in_grad_cols = jnp.where(
        side == core,
        lax.dynamic_slice_in_dim(mine, at, width, 2),
        lax.dynamic_slice_in_dim(other, at, width, 2),
    )
    in_grad_rows = in_grad_cols.reshape(-1, width).T
    grad_tokens = token_grads(keys_rows, in_grad_rows, logit_grad, dispatch)
    return (grad_tokens, grad_keys, grad_w_in, grad_w_out)


def solution(mesh):
    fine = Mesh(mesh.devices.reshape(2, 4, 2, 4, 2), ("zl", "y", "c", "x", "zh"))
    placed = (
        P(SEQ, None),
        P(None, SLOT),
        P(SLOT, SEQ, None),
        P(SLOT, SEQ, None),
        P(SEQ, None),
    )
    return jax.shard_map(
        per_device,
        mesh=fine,
        in_specs=placed,
        out_specs=(
            P(SEQ, SLOT),
            P(SEQ, SLOT),
            P(SLOT, SEQ, None),
            P(SLOT, SEQ, None),
        ),
        check_vma=False,
    )
```

```python
import jax
import jax.numpy as jnp
from jax import lax
from jax.experimental import pallas as pl
from jax.experimental.pallas import tpu as pltpu
from jax.sharding import Mesh, PartitionSpec as P

gelu_scale = 0.7978845608
gelu_cubic = 0.044715
rows_contract = (((0,), (0,)), ((), ()))
cols_contract = (((1,), (1,)), ((), ()))

SEQ = ("zl", "y", "c")
SLOT = ("x", "zh")
GATHERED = ("x", "zl", "y")
f32 = jnp.float32
bf16 = jnp.bfloat16
LANES = 128
MIB = 1 << 20


def gelu_tanh(values):
    return (
        0.5
        * values
        * (1.0 + jnp.tanh(gelu_scale * (values + gelu_cubic * values * values * values)))
    )


def gelu_slope(values):
    bent = jnp.tanh(gelu_scale * (values + gelu_cubic * values * values * values))
    return 0.5 * (1.0 + bent) + 0.5 * values * (1.0 - bent * bent) * gelu_scale * (
        1.0 + 3.0 * gelu_cubic * values * values
    )


def guarded(total):
    power = jnp.where(total > 2.0**64, 2.0**-32, jnp.where(total < 2.0**-64, 2.0**32, 1.0))
    return power, 1.0 / (total * power)


def two_parts(values):
    high = values.astype(bf16).astype(f32)
    return high, values - high


def in_lanes(rows, columns):
    lane = lax.broadcasted_iota(jnp.int32, (rows, LANES), 1)
    laid = jnp.zeros((rows, LANES), f32)
    for at, column in enumerate(columns):
        laid = jnp.where(lane == at, column, laid)
    return laid.astype(bf16)


def params(mib):
    return pltpu.CompilerParams(vmem_limit_bytes=mib * MIB)


def cost(flops, nbytes):
    return pl.CostEstimate(flops=flops, bytes_accessed=nbytes, transcendentals=0)


def whole_in_vmem():
    return pl.BlockSpec(memory_space=pltpu.VMEM)


def own_logits(keys_t, tokens, copies, tile=512):
    slots, features = keys_t.shape
    count = tokens.shape[0]

    def kernel(keys_ref, tokens_ref, exp_ref, row_ref, column_ref):
        exps = jnp.exp(
            lax.dot_general(keys_ref[...], tokens_ref[...], cols_contract, preferred_element_type=f32)
        )
        exp_ref[...] = exps
        row_ref[...] = jnp.broadcast_to(
            jnp.sum(exps, axis=0, keepdims=True)[None], (copies, 1, tile)
        )
        by_lane = exps[:, :LANES]
        for at in range(1, tile // LANES):
            by_lane = by_lane + exps[:, at * LANES : (at + 1) * LANES]

        @pl.when(pl.program_id(0) == 0)
        def _():
            column_ref[...] = by_lane

        @pl.when(pl.program_id(0) > 0)
        def _():
            column_ref[...] += by_lane

    return pl.pallas_call(
        kernel,
        grid=(count // tile,),
        in_specs=[
            pl.BlockSpec((slots, features), lambda i: (0, 0)),
            pl.BlockSpec((tile, features), lambda i: (i, 0)),
        ],
        out_specs=[
            pl.BlockSpec((slots, tile), lambda i: (0, i)),
            pl.BlockSpec((copies, 1, tile), lambda i: (0, 0, i)),
            pl.BlockSpec((slots, LANES), lambda i: (0, 0)),
        ],
        out_shape=[
            jax.ShapeDtypeStruct((slots, count), f32),
            jax.ShapeDtypeStruct((copies, 1, count), f32),
            jax.ShapeDtypeStruct((slots, LANES), f32),
        ],
        compiler_params=params(32),
        cost_estimate=cost(2 * slots * features * count, 2 * features * count + 4 * slots * count),
        name="own_logits",
    )(keys_t, tokens)


def dispatch_part(exps, column, tokens, tile=512):
    slots, count = exps.shape
    features = tokens.shape[1]

    def kernel(exp_ref, column_ref, tokens_ref, out_ref, total_ref):
        total = jnp.sum(column_ref[...], axis=1, keepdims=True)
        power, inverse = guarded(jnp.where(total > 0, total, 1.0))
        weights = ((exp_ref[...] * power) * inverse).astype(bf16)
        term = jnp.dot(weights, tokens_ref[...], preferred_element_type=f32)

        @pl.when(pl.program_id(0) == 0)
        def _():
            total_ref[...] = term

        @pl.when(pl.program_id(0) > 0)
        def _():
            total_ref[...] += term

        @pl.when(pl.program_id(0) == pl.num_programs(0) - 1)
        def _():
            out_ref[...] = total_ref[...].astype(bf16)

    return pl.pallas_call(
        kernel,
        grid=(count // tile,),
        in_specs=[
            pl.BlockSpec((slots, tile), lambda i: (0, i)),
            pl.BlockSpec((slots, LANES), lambda i: (0, 0)),
            pl.BlockSpec((tile, features), lambda i: (i, 0)),
        ],
        out_specs=pl.BlockSpec((slots, features), lambda i: (0, 0)),
        out_shape=jax.ShapeDtypeStruct((slots, features), bf16),
        scratch_shapes=[pltpu.VMEM((slots, features), f32)],
        compiler_params=params(32),
        cost_estimate=cost(2 * slots * features * count, 2 * features * count + 4 * slots * count),
        name="dispatch_part",
    )(exps, column, tokens)


def combine_part(exps, row_parts, column, slot_in_part, out_grad, groups, tile=512):
    slots, count = exps.shape
    features = out_grad.shape[1]
    half = features // 2
    block = slots // groups
    width = features + LANES
    copies = row_parts.shape[0]

    def kernel(exp_ref, row_ref, column_ref, in_ref, grad_ref, sent_ref, total_ref):
        power, inverse = guarded(jnp.sum(row_ref[...], axis=0))
        weights = ((exp_ref[...] * power) * inverse).astype(bf16)
        term = jnp.dot(weights, grad_ref[...], preferred_element_type=f32)

        @pl.when(pl.program_id(0) == 0)
        def _():
            total_ref[...] = term

        @pl.when(pl.program_id(0) > 0)
        def _():
            total_ref[...] += term

        @pl.when(pl.program_id(0) == pl.num_programs(0) - 1)
        def _():
            total = jnp.sum(column_ref[...], axis=1, keepdims=True)
            shift, _unused = guarded(total)
            high, low = two_parts(total * shift)
            lanes = in_lanes(slots, (high, low, 1.0 / shift))
            grad = total_ref[...].astype(bf16)
            for group in range(groups):
                rows = slice(group * block, (group + 1) * block)
                for side in range(2):
                    cut = slice(side * half, (side + 1) * half)
                    sent_ref[group * 2 + side, :, :half] = in_ref[rows, cut]
                    sent_ref[group * 2 + side, :, half:features] = grad[rows, cut]
                    sent_ref[group * 2 + side, :, features:] = lanes[rows]

    return pl.pallas_call(
        kernel,
        grid=(count // tile,),
        in_specs=[
            pl.BlockSpec((slots, tile), lambda i: (0, i)),
            pl.BlockSpec((copies, 1, tile), lambda i: (0, 0, i)),
            pl.BlockSpec((slots, LANES), lambda i: (0, 0)),
            pl.BlockSpec((slots, features), lambda i: (0, 0)),
            pl.BlockSpec((tile, features), lambda i: (i, 0)),
        ],
        out_specs=pl.BlockSpec((groups * 2, block, width), lambda i: (0, 0, 0)),
        out_shape=jax.ShapeDtypeStruct((groups * 2, block, width), bf16),
        scratch_shapes=[pltpu.VMEM((slots, features), f32)],
        compiler_params=params(32),
        cost_estimate=cost(2 * slots * features * count, 2 * features * count + 4 * slots * count),
        name="combine_part",
    )(exps, row_parts, column, slot_in_part, out_grad)


def sum_slots(parts, copies):
    sources, block, width = parts.shape
    features = width - LANES
    half = features // 2

    def kernel(parts_ref, sent_ref, in_ref, column_ref):
        lanes = parts_ref[:, :, features:].astype(f32)
        columns = (lanes[:, :, 0:1] + lanes[:, :, 1:2]) * lanes[:, :, 2:3]
        total = jnp.sum(columns, axis=0)
        power, inverse = guarded(total)
        share = (columns * power[None]) * inverse[None]
        slot_in = jnp.zeros((block, half), f32)
        slot_grad = jnp.zeros((block, half), f32)
        for source in range(sources):
            slot_in = slot_in + parts_ref[source, :, :half].astype(f32) * share[source]
            slot_grad = slot_grad + parts_ref[source, :, half:features].astype(f32)
        in_ref[...] = slot_in
        column_ref[...] = jnp.broadcast_to(total, (block, LANES))
        in_low = slot_in.astype(bf16)
        grad_low = slot_grad.astype(bf16)
        for copy in range(copies):
            sent_ref[copy, :, :half] = in_low
            sent_ref[copy, :, half:] = grad_low

    return pl.pallas_call(
        kernel,
        in_specs=[whole_in_vmem()],
        out_specs=[whole_in_vmem()] * 3,
        out_shape=[
            jax.ShapeDtypeStruct((copies, block, features), bf16),
            jax.ShapeDtypeStruct((block, half), f32),
            jax.ShapeDtypeStruct((block, LANES), f32),
        ],
        compiler_params=params(32),
        name="sum_slots",
    )(parts)


def experts_part(whole, w_in, w_out):
    experts, hidden, features = w_in.shape
    block = whole.shape[1]
    half = features // 2

    def kernel(whole_ref, w_in_ref, w_out_ref, terms_ref, act_ref, pre_ref):
        slots = jnp.concatenate([whole_ref[0, :, :half], whole_ref[1, :, :half]], axis=1)
        grads = jnp.concatenate([whole_ref[0, :, half:], whole_ref[1, :, half:]], axis=1)
        hidden_pre = lax.dot_general(slots, w_in_ref[0], cols_contract, preferred_element_type=f32)
        act_grad = lax.dot_general(grads, w_out_ref[0], cols_contract, preferred_element_type=f32)
        act = gelu_tanh(hidden_pre).astype(bf16)
        pre = (act_grad * gelu_slope(hidden_pre)).astype(bf16)
        out_terms = jnp.dot(act, w_out_ref[0], preferred_element_type=f32).astype(bf16)
        in_terms = jnp.dot(pre, w_in_ref[0], preferred_element_type=f32).astype(bf16)
        for side in range(2):
            cut = slice(side * half, (side + 1) * half)
            terms_ref[side, :, :half] = out_terms[:, cut]
            terms_ref[side, :, half:] = in_terms[:, cut]
        act_ref[0] = act
        pre_ref[0] = pre

    return pl.pallas_call(
        kernel,
        grid=(experts,),
        in_specs=[
            pl.BlockSpec((2, block, features), lambda e: (e, 0, 0)),
            pl.BlockSpec((1, hidden, features), lambda e: (e, 0, 0)),
            pl.BlockSpec((1, hidden, features), lambda e: (e, 0, 0)),
        ],
        out_specs=[
            pl.BlockSpec((2, block, features), lambda e: (e, 0, 0)),
            pl.BlockSpec((1, block, hidden), lambda e: (e, 0, 0)),
            pl.BlockSpec((1, block, hidden), lambda e: (e, 0, 0)),
        ],
        out_shape=[
            jax.ShapeDtypeStruct(whole.shape, bf16),
            jax.ShapeDtypeStruct((experts, block, hidden), bf16),
            jax.ShapeDtypeStruct((experts, block, hidden), bf16),
        ],
        compiler_params=params(32),
        cost_estimate=cost(8 * experts * block * hidden * features, 4 * experts * hidden * features),
        name="experts_part",
    )(whole, w_in, w_out)


def weight_grads(whole, act, pre, hidden_shape):
    experts, hidden, features = hidden_shape
    block = whole.shape[1]
    half = features // 2

    def kernel(whole_ref, act_ref, pre_ref, in_ref, out_ref):
        for side in range(2):
            cut = slice(side * half, (side + 1) * half)
            in_ref[0, :, cut] = lax.dot_general(
                pre_ref[0], whole_ref[side, :, :half], rows_contract, preferred_element_type=f32
            ).astype(bf16)
            out_ref[0, :, cut] = lax.dot_general(
                act_ref[0], whole_ref[side, :, half:], rows_contract, preferred_element_type=f32
            ).astype(bf16)

    return pl.pallas_call(
        kernel,
        grid=(experts,),
        in_specs=[
            pl.BlockSpec((2, block, features), lambda e: (e, 0, 0)),
            pl.BlockSpec((1, block, hidden), lambda e: (e, 0, 0)),
            pl.BlockSpec((1, block, hidden), lambda e: (e, 0, 0)),
        ],
        out_specs=[pl.BlockSpec((1, hidden, features), lambda e: (e, 0, 0))] * 2,
        out_shape=[jax.ShapeDtypeStruct(hidden_shape, bf16)] * 2,
        compiler_params=params(32),
        cost_estimate=cost(4 * experts * block * hidden * features, 4 * experts * hidden * features),
        name="weight_grads",
    )(whole, act, pre)


def sum_terms(terms, slot_in, column, copies):
    sources, block, features = terms.shape
    half = features // 2
    width = features + LANES

    def kernel(terms_ref, in_ref, column_ref, sent_ref):
        total = terms_ref[0].astype(f32)
        for source in range(1, sources):
            total = total + terms_ref[source].astype(f32)
        low = total.astype(bf16)
        inner = jnp.sum(in_ref[...] * low[:, half:].astype(f32), axis=1, keepdims=True)
        power, inverse = guarded(column_ref[:, 0:1])
        lanes = in_lanes(block, two_parts(inverse) + (power,) + two_parts(inner))
        for copy in range(copies):
            sent_ref[copy, :, :features] = low
            sent_ref[copy, :, features:] = lanes

    return pl.pallas_call(
        kernel,
        in_specs=[whole_in_vmem()] * 3,
        out_specs=whole_in_vmem(),
        out_shape=jax.ShapeDtypeStruct((copies, block, width), bf16),
        compiler_params=params(32),
        name="sum_terms",
    )(terms, slot_in, column)


def all_exps(keys_t, tokens, tile=256):
    slots, features = keys_t.shape
    count = tokens.shape[0]

    def kernel(keys_ref, tokens_ref, exp_ref):
        exp_ref[...] = jnp.exp(
            lax.dot_general(keys_ref[...], tokens_ref[...], cols_contract, preferred_element_type=f32)
        )

    return pl.pallas_call(
        kernel,
        grid=(count // tile,),
        in_specs=[
            pl.BlockSpec((slots, features), lambda i: (0, 0)),
            pl.BlockSpec((tile, features), lambda i: (i, 0)),
        ],
        out_specs=pl.BlockSpec((slots, tile), lambda i: (0, i)),
        out_shape=jax.ShapeDtypeStruct((slots, count), f32),
        compiler_params=params(32),
        cost_estimate=cost(2 * slots * features * count, 2 * features * count + 4 * slots * count),
        name="all_exps",
    )(keys_t, tokens)


def whole_block(shape):
    return pl.BlockSpec(shape, lambda i: (0,) * len(shape), pipeline_mode=pl.Buffered(1))


def width_dot(place_ref, mine_ref, other_ref, ref, at):
    blocks, block, width = mine_ref.shape
    half = ref.shape[1] // 2
    core = place_ref[0]
    here = pl.multiple_of(core * half, LANES)
    there = pl.multiple_of((1 - core) * half, LANES)
    near = lax.dot_general(
        mine_ref[:, :, at * half : (at + 1) * half].reshape(blocks * block, half),
        ref[:, pl.ds(here, half)],
        cols_contract,
        preferred_element_type=f32,
    )
    far = lax.dot_general(
        other_ref[:, :, at * half : (at + 1) * half].reshape(blocks * block, half),
        ref[:, pl.ds(there, half)],
        cols_contract,
        preferred_element_type=f32,
    )
    return near + far


def comb_dots(place, exps, out_grad, row_parts, mine, other, tile=512):
    slots, count = exps.shape
    features = out_grad.shape[1]
    copies = row_parts.shape[0]

    def kernel(place_ref, exp_ref, grad_ref, row_ref, mine_ref, other_ref, dot_ref, sum_ref):
        power, inverse = guarded(jnp.sum(row_ref[...], axis=0))
        dots = width_dot(place_ref, mine_ref, other_ref, grad_ref, 0)
        dot_ref[...] = dots
        combine = (exp_ref[...] * power) * inverse
        sum_ref[...] = jnp.sum(combine * dots, axis=0, keepdims=True)

    return pl.pallas_call(
        kernel,
        grid=(count // tile,),
        in_specs=[
            pl.BlockSpec(memory_space=pltpu.SMEM),
            pl.BlockSpec((slots, tile), lambda i: (0, i)),
            pl.BlockSpec((tile, features), lambda i: (i, 0)),
            pl.BlockSpec((copies, 1, tile), lambda i: (0, 0, i)),
            whole_block(mine.shape),
            whole_block(other.shape),
        ],
        out_specs=[
            pl.BlockSpec((slots, tile), lambda i: (0, i)),
            pl.BlockSpec((1, tile), lambda i: (0, i)),
        ],
        out_shape=[
            jax.ShapeDtypeStruct((slots, count), f32),
            jax.ShapeDtypeStruct((1, count), f32),
        ],
        compiler_params=params(24),
        cost_estimate=cost(2 * slots * features * count, 2 * features * count),
        name="comb_dots",
    )(place, exps, out_grad, row_parts, mine, other)


def disp_dots(place, exps, dots, tokens, row_parts, mine, other, tile=512):
    slots, count = exps.shape
    features = tokens.shape[1]
    copies = row_parts.shape[0]

    def kernel(
        place_ref, exp_ref, dot_ref, tokens_ref, row_ref, mine_ref, other_ref,
        terms_ref, dispatch_ref, power_ref, inverse_ref, total_ref,
    ):
        @pl.when(pl.program_id(0) == 0)
        def _():
            lanes = mine_ref[:, :, features:].reshape(slots, LANES).astype(f32)
            apart = other_ref[:, :, features:].reshape(slots, LANES).astype(f32)
            inner = lanes[:, 3:4] + lanes[:, 4:5] + apart[:, 3:4] + apart[:, 4:5]
            power_ref[...] = jnp.broadcast_to(lanes[:, 2:3], (slots, tile))
            inverse_ref[...] = jnp.broadcast_to(lanes[:, 0:1] + lanes[:, 1:2], (slots, tile))
            total_ref[...] = jnp.broadcast_to(inner, (slots, tile))

        power, inverse = guarded(jnp.sum(row_ref[...], axis=0))
        here = exp_ref[...]
        dispatch = (here * power_ref[...]) * inverse_ref[...]
        dispatch_ref[...] = dispatch.astype(bf16)
        disp_dot = width_dot(place_ref, mine_ref, other_ref, tokens_ref, 1)
        combine = (here * power) * inverse
        terms_ref[...] = combine * dot_ref[...] + dispatch * (disp_dot - total_ref[...])

    return pl.pallas_call(
        kernel,
        grid=(count // tile,),
        in_specs=[
            pl.BlockSpec(memory_space=pltpu.SMEM),
            pl.BlockSpec((slots, tile), lambda i: (0, i)),
            pl.BlockSpec((slots, tile), lambda i: (0, i)),
            pl.BlockSpec((tile, features), lambda i: (i, 0)),
            pl.BlockSpec((copies, 1, tile), lambda i: (0, 0, i)),
            whole_block(mine.shape),
            whole_block(other.shape),
        ],
        out_specs=[
            pl.BlockSpec((slots, tile), lambda i: (0, i)),
            pl.BlockSpec((slots, tile), lambda i: (0, i)),
        ],
        out_shape=[
            jax.ShapeDtypeStruct((slots, count), f32),
            jax.ShapeDtypeStruct((slots, count), bf16),
        ],
        scratch_shapes=[pltpu.VMEM((slots, tile), f32)] * 3,
        compiler_params=params(24),
        cost_estimate=cost(2 * slots * features * count, 2 * features * count),
        name="disp_dots",
    )(place, exps, dots, tokens, row_parts, mine, other)


def logit_grads(place, exps, terms, dispatch, tokens, row_parts, row, row_other, rows_other, own_slots, tile=512):
    slots, count = exps.shape
    features = tokens.shape[1]
    copies = row_parts.shape[0]
    width = rows_other.shape[0]

    def kernel(
        place_ref, exp_ref, terms_ref, dispatch_ref, tokens_ref, row_ref, sum_ref, other_ref, rows_ref,
        logit_ref, keys_ref, sent_ref, total_ref,
    ):
        step = pl.program_id(0)
        power, inverse = guarded(jnp.sum(row_ref[...], axis=0))
        weight = (sum_ref[...] + other_ref[...]) * inverse
        logit_ref[...] = (terms_ref[...] - (exp_ref[...] * power) * weight).astype(bf16)
        own = logit_ref[pl.ds(pl.multiple_of(place_ref[1] * own_slots, own_slots), own_slots), :]
        term = jnp.dot(own, tokens_ref[...], preferred_element_type=f32)

        @pl.when(step == 0)
        def _():
            total_ref[...] = term

        @pl.when(step > 0)
        def _():
            total_ref[...] += term

        @pl.when(step == pl.num_programs(0) - 1)
        def _():
            keys_ref[...] = total_ref[...].T.astype(bf16)

        sent = jnp.dot(rows_ref[:, :slots], logit_ref[...], preferred_element_type=f32)
        sent = sent + jnp.dot(rows_ref[:, slots:], dispatch_ref[...], preferred_element_type=f32)
        sent_ref[...] = sent.astype(bf16)

    return pl.pallas_call(
        kernel,
        grid=(count // tile,),
        in_specs=[
            pl.BlockSpec(memory_space=pltpu.SMEM),
            pl.BlockSpec((slots, tile), lambda i: (0, i)),
            pl.BlockSpec((slots, tile), lambda i: (0, i)),
            pl.BlockSpec((slots, tile), lambda i: (0, i)),
            pl.BlockSpec((tile, features), lambda i: (i, 0)),
            pl.BlockSpec((copies, 1, tile), lambda i: (0, 0, i)),
            pl.BlockSpec((1, tile), lambda i: (0, i)),
            pl.BlockSpec((1, tile), lambda i: (0, i)),
            whole_block(rows_other.shape),
        ],
        out_specs=[
            pl.BlockSpec((slots, tile), lambda i: (0, i)),
            pl.BlockSpec((features, own_slots), lambda i: (0, 0)),
            pl.BlockSpec((width, tile), lambda i: (0, i)),
        ],
        out_shape=[
            jax.ShapeDtypeStruct((slots, count), bf16),
            jax.ShapeDtypeStruct((features, own_slots), bf16),
            jax.ShapeDtypeStruct((width, count), bf16),
        ],
        scratch_shapes=[pltpu.VMEM((own_slots, features), f32)],
        compiler_params=params(24),
        cost_estimate=cost(2 * own_slots * features * count, 2 * features * count),
        name="logit_grads",
    )(place, exps, terms, dispatch, tokens, row_parts, row, row_other, rows_other)


def token_grads(rows, logit_grad, dispatch, tile=512):
    slots, count = logit_grad.shape
    width = rows.shape[0]

    def kernel(rows_ref, logit_ref, dispatch_ref, out_ref):
        total = jnp.dot(rows_ref[:, :slots], logit_ref[...], preferred_element_type=f32)
        out_ref[...] = total + jnp.dot(
            rows_ref[:, slots:], dispatch_ref[...], preferred_element_type=f32
        )

    return pl.pallas_call(
        kernel,
        grid=(count // tile,),
        in_specs=[
            whole_block(rows.shape),
            pl.BlockSpec((slots, tile), lambda i: (0, i)),
            pl.BlockSpec((slots, tile), lambda i: (0, i)),
        ],
        out_specs=pl.BlockSpec((width, tile), lambda i: (0, i)),
        out_shape=jax.ShapeDtypeStruct((width, count), f32),
        compiler_params=params(24),
        cost_estimate=cost(4 * slots * width * count, 4 * slots * count),
        name="token_grads",
    )(rows, logit_grad, dispatch)


def transposed(keys):
    def kernel(keys_ref, out_ref):
        out_ref[...] = keys_ref[...].T

    return pl.pallas_call(
        kernel,
        in_specs=[whole_in_vmem()],
        out_specs=whole_in_vmem(),
        out_shape=jax.ShapeDtypeStruct(keys.shape[::-1], keys.dtype),
        compiler_params=params(24),
        name="transposed",
    )(keys)


def per_device(tokens, slot_keys, w_in, w_out, out_grad):
    features = tokens.shape[1]
    own_slots = slot_keys.shape[1]
    core = lax.axis_index("c")
    column_at = lax.axis_index("x")
    pair_at = lax.axis_index("zh")
    half = features // 2
    slot_devices = lax.axis_size(SLOT)
    seq_devices = lax.axis_size(SEQ)
    groups = seq_devices // 2
    everyone = lax.axis_size(GATHERED)
    swap = [(0, 1), (1, 0)]

    keys_t = transposed(slot_keys)
    keys_all = lax.all_gather(keys_t, "x", axis=0, tiled=True)

    exps, own_row, column = own_logits(keys_t, tokens, slot_devices)
    row_parts = lax.all_to_all(own_row, SLOT, 0, 0)
    slot_in_part = dispatch_part(exps, column, tokens)
    parts = lax.all_to_all(
        combine_part(exps, row_parts, column, slot_in_part, out_grad, groups), SEQ, 0, 0
    )
    sent, slot_in, column_total = sum_slots(parts, seq_devices)
    whole = lax.all_to_all(sent, SEQ, 0, 0)

    sent, act, pre = experts_part(whole, w_in, w_out)
    sent, keys_all = lax.optimization_barrier((sent, keys_all))
    terms = lax.all_to_all(sent, SEQ, 0, 0)
    all_exp = all_exps(keys_all, tokens)
    terms, all_exp, act, pre = lax.optimization_barrier((terms, all_exp, act, pre))
    sent = sum_terms(terms, slot_in, column_total, everyone)
    mine = lax.all_to_all(sent, GATHERED, 0, 0)
    grad_w_in, grad_w_out = weight_grads(whole, act, pre, w_in.shape)
    mine, grad_w_in, grad_w_out = lax.optimization_barrier((mine, grad_w_in, grad_w_out))
    other = lax.ppermute(mine, "c", swap)

    place = jnp.stack([core, column_at]).astype(jnp.int32)
    dots, row = comb_dots(place, all_exp, out_grad, row_parts, mine, other)
    row_other = lax.ppermute(row, "zh", swap)
    terms, dispatch = disp_dots(place, all_exp, dots, tokens, row_parts, mine, other)

    width = features // slot_devices
    pair = 2 * width
    keys_cols = lax.dynamic_slice_in_dim(keys_all, column_at * pair, pair, 1)
    side = (column_at * pair) // half
    at = half + column_at * pair - side * half
    in_grad_cols = jnp.where(
        side == core,
        lax.dynamic_slice_in_dim(mine, at, pair, 2),
        lax.dynamic_slice_in_dim(other, at, pair, 2),
    ).reshape(-1, pair)
    pair_rows = jnp.concatenate([keys_cols.T, in_grad_cols.T], axis=1)
    rows_own = lax.dynamic_slice_in_dim(pair_rows, pair_at * width, width, 0)
    rows_other = lax.dynamic_slice_in_dim(pair_rows, (1 - pair_at) * width, width, 0)

    logit_grad, keys_part, sent = logit_grads(
        place, all_exp, terms, dispatch, tokens, row_parts, row, row_other, rows_other, own_slots
    )
    received = lax.ppermute(sent, "zh", swap)
    keys_parts = lax.all_to_all(
        keys_part.reshape(seq_devices, features // seq_devices, own_slots), SEQ, 0, 0
    )
    grad_keys = jnp.sum(keys_parts.astype(f32), axis=0)
    own_grads = token_grads(rows_own, logit_grad, dispatch)
    grad_tokens = (own_grads + received.astype(f32)).astype(bf16).T
    return (grad_tokens, grad_keys, grad_w_in, grad_w_out)


def solution(mesh):
    fine = Mesh(mesh.devices.reshape(2, 4, 2, 4, 2), ("zl", "y", "c", "x", "zh"))
    placed = (
        P(SEQ, None),
        P(None, SLOT),
        P(SLOT, SEQ, None),
        P(SLOT, SEQ, None),
        P(SEQ, None),
    )
    return jax.shard_map(
        per_device,
        mesh=fine,
        in_specs=placed,
        out_specs=(
            P(SEQ, SLOT),
            P(SEQ, SLOT),
            P(SLOT, SEQ, None),
            P(SLOT, SEQ, None),
        ),
        check_vma=False,
    )
```

```python
import jax
import jax.numpy as jnp
from jax import lax
from jax.experimental import pallas as pl
from jax.experimental.pallas import tpu as pltpu
from jax.sharding import Mesh, PartitionSpec as P

gelu_scale = 0.7978845608
gelu_cubic = 0.044715
rows_contract = (((0,), (0,)), ((), ()))
cols_contract = (((1,), (1,)), ((), ()))

SEQ = ("zl", "y", "c")
SLOT = ("xa", "xb", "zh")
KEYS = ("xb", "zh")
CHIPS = ("zl", "y")
GATHERED = ("xb", "zh", "zl", "y")
f32 = jnp.float32
bf16 = jnp.bfloat16
LANES = 128
MIB = 1 << 20
GRANT = 16
SCALE = 1


def gelu_tanh(values):
    return (
        0.5
        * values
        * (1.0 + jnp.tanh(gelu_scale * (values + gelu_cubic * values * values * values)))
    )


def gelu_slope(values):
    bent = jnp.tanh(gelu_scale * (values + gelu_cubic * values * values * values))
    return 0.5 * (1.0 + bent) + 0.5 * values * (1.0 - bent * bent) * gelu_scale * (
        1.0 + 3.0 * gelu_cubic * values * values
    )


def guarded(total):
    power = jnp.where(total > 2.0**64, 2.0**-32, jnp.where(total < 2.0**-64, 2.0**32, 1.0))
    return power, 1.0 / (total * power)


def two_parts(values):
    high = values.astype(bf16).astype(f32)
    return high, values - high


def in_lanes(rows, columns):
    lane = lax.broadcasted_iota(jnp.int32, (rows, LANES), 1)
    laid = jnp.zeros((rows, LANES), f32)
    for at, column in enumerate(columns):
        laid = jnp.where(lane == at, column, laid)
    return laid.astype(bf16)


def params(mib):
    return pltpu.CompilerParams(vmem_limit_bytes=mib * MIB)


def cost(flops, nbytes):
    return pl.CostEstimate(flops=SCALE * flops, bytes_accessed=nbytes, transcendentals=0)


def whole_in_vmem():
    return pl.BlockSpec(memory_space=pltpu.VMEM)


def in_smem():
    return pl.BlockSpec(memory_space=pltpu.SMEM)


def halves(place_ref, half):
    core = place_ref[0]
    here = pl.ds(pl.multiple_of(core * half, LANES), half)
    there = pl.ds(pl.multiple_of((1 - core) * half, LANES), half)
    return here, there


def own_logits(slot_keys, tokens, copies, tile=512):
    features, slots = slot_keys.shape
    count = tokens.shape[0]

    def kernel(slot_keys_ref, tokens_ref, exp_ref, row_ref, column_ref):
        keys = slot_keys_ref[...].T
        by_lane = jnp.zeros((slots, LANES), f32)
        for at in range(0, count, tile):
            cut = slice(at, at + tile)
            exps = jnp.exp(
                lax.dot_general(keys, tokens_ref[cut, :], cols_contract, preferred_element_type=f32)
            )
            exp_ref[:, cut] = exps
            row_ref[:, :, cut] = jnp.broadcast_to(
                jnp.sum(exps, axis=0, keepdims=True)[None], (copies, 1, tile)
            )
            for lanes in range(0, tile, LANES):
                by_lane = by_lane + exps[:, lanes : lanes + LANES]
        column_ref[...] = by_lane

    return pl.pallas_call(
        kernel,
        in_specs=[whole_in_vmem()] * 2,
        out_specs=[whole_in_vmem()] * 3,
        out_shape=[
            jax.ShapeDtypeStruct((slots, count), f32),
            jax.ShapeDtypeStruct((copies, 1, count), f32),
            jax.ShapeDtypeStruct((slots, LANES), f32),
        ],
        compiler_params=params(GRANT),
        cost_estimate=cost(2 * slots * features * count, 2 * features * count),
        name="own_logits",
    )(slot_keys, tokens)


def dispatch_part(exps, column, column_other, tokens):
    slots, count = exps.shape
    features = tokens.shape[1]

    def kernel(exp_ref, column_ref, other_ref, tokens_ref, out_ref, weights_ref):
        total = jnp.sum(column_ref[...] + other_ref[...], axis=1, keepdims=True)
        power, inverse = guarded(jnp.where(total > 0, total, 1.0))
        weights_ref[...] = ((exp_ref[...] * power) * inverse).astype(bf16)
        out_ref[...] = jnp.dot(
            weights_ref[...], tokens_ref[...], preferred_element_type=f32
        ).astype(bf16)

    return pl.pallas_call(
        kernel,
        in_specs=[whole_in_vmem()] * 4,
        out_specs=whole_in_vmem(),
        out_shape=jax.ShapeDtypeStruct((slots, features), bf16),
        scratch_shapes=[pltpu.VMEM((slots, count), bf16)],
        compiler_params=params(GRANT),
        cost_estimate=cost(2 * slots * features * count, 2 * features * count),
        name="dispatch_part",
    )(exps, column, column_other, tokens)


def combine_part(place, exps, row_parts, column, column_other, slot_in_part, out_grad, groups):
    slots, count = exps.shape
    features = out_grad.shape[1]
    half = features // 2
    block = slots // groups

    def kernel(
        place_ref, exp_ref, row_ref, column_ref, other_ref, in_ref, grad_ref,
        keep_ref, give_ref, weights_ref, total_ref,
    ):
        power, inverse = guarded(jnp.sum(row_ref[...], axis=0))
        weights_ref[...] = ((exp_ref[...] * power) * inverse).astype(bf16)
        total = jnp.sum(column_ref[...] + other_ref[...], axis=1, keepdims=True)
        shift, _unused = guarded(total)
        high, low = two_parts(total * shift)
        lanes = in_lanes(slots, (high, low, 1.0 / shift))
        total_ref[...] = jnp.dot(
            weights_ref[...], grad_ref[...], preferred_element_type=f32
        ).astype(bf16)
        here, there = halves(place_ref, half)
        for group in range(groups):
            rows = slice(group * block, (group + 1) * block)
            keep_ref[group, :, :half] = in_ref[rows, here]
            keep_ref[group, :, half:features] = total_ref[rows, here]
            keep_ref[group, :, features:] = lanes[rows]
            give_ref[group, :, :half] = in_ref[rows, there]
            give_ref[group, :, half:] = total_ref[rows, there]

    return pl.pallas_call(
        kernel,
        in_specs=[in_smem()] + [whole_in_vmem()] * 6,
        out_specs=[whole_in_vmem()] * 2,
        out_shape=[
            jax.ShapeDtypeStruct((groups, block, features + LANES), bf16),
            jax.ShapeDtypeStruct((groups, block, features), bf16),
        ],
        scratch_shapes=[
            pltpu.VMEM((slots, count), bf16),
            pltpu.VMEM((slots, features), bf16),
        ],
        compiler_params=params(GRANT),
        cost_estimate=cost(2 * slots * features * count, 2 * features * count),
        name="combine_part",
    )(place, exps, row_parts, column, column_other, slot_in_part, out_grad)


def pair_sum(keep, received):
    features = received.shape[2]

    def kernel(keep_ref, received_ref, out_ref):
        total = keep_ref[:, :, :features].astype(f32) + received_ref[...].astype(f32)
        out_ref[:, :, :features] = total.astype(bf16)
        if keep_ref.shape[2] > features:
            out_ref[:, :, features:] = keep_ref[:, :, features:]

    return pl.pallas_call(
        kernel,
        in_specs=[whole_in_vmem()] * 2,
        out_specs=whole_in_vmem(),
        out_shape=jax.ShapeDtypeStruct(keep.shape, bf16),
        compiler_params=params(GRANT),
        name="pair_sum",
    )(keep, received)


def sum_slots(parts, copies):
    sources, block, width = parts.shape
    features = width - LANES
    half = features // 2

    def kernel(parts_ref, sent_ref, in_ref, column_ref):
        lanes = parts_ref[:, :, features:].astype(f32)
        columns = (lanes[:, :, 0:1] + lanes[:, :, 1:2]) * lanes[:, :, 2:3]
        total = jnp.sum(columns, axis=0)
        power, inverse = guarded(total)
        share = (columns * power[None]) * inverse[None]
        slot_in = jnp.zeros((block, half), f32)
        slot_grad = jnp.zeros((block, half), f32)
        for source in range(sources):
            slot_in = slot_in + parts_ref[source, :, :half].astype(f32) * share[source]
            slot_grad = slot_grad + parts_ref[source, :, half:features].astype(f32)
        in_ref[...] = slot_in
        column_ref[...] = jnp.broadcast_to(total, (block, LANES))
        in_low = slot_in.astype(bf16)
        grad_low = slot_grad.astype(bf16)
        for copy in range(copies):
            sent_ref[copy, :, :half] = in_low
            sent_ref[copy, :, half:] = grad_low

    return pl.pallas_call(
        kernel,
        in_specs=[whole_in_vmem()],
        out_specs=[whole_in_vmem()] * 3,
        out_shape=[
            jax.ShapeDtypeStruct((copies, block, features), bf16),
            jax.ShapeDtypeStruct((block, half), f32),
            jax.ShapeDtypeStruct((block, LANES), f32),
        ],
        compiler_params=params(GRANT),
        name="sum_slots",
    )(parts)


def experts_part(place, mine, other, w_in, w_out):
    experts, hidden, features = w_in.shape
    block = mine.shape[1]
    half = features // 2

    def kernel(place_ref, mine_ref, other_ref, w_in_ref, w_out_ref, keep_ref, give_ref, act_ref, pre_ref):
        here, there = halves(place_ref, half)

        def inward(at, weights_ref, e):
            cut = slice(at * half, (at + 1) * half)
            near = lax.dot_general(
                mine_ref[e, :, cut], weights_ref[e, :, here], cols_contract, preferred_element_type=f32
            )
            far = lax.dot_general(
                other_ref[e, :, cut], weights_ref[e, :, there], cols_contract, preferred_element_type=f32
            )
            return near + far

        for e in range(experts):
            hidden_pre = inward(0, w_in_ref, e)
            act_grad = inward(1, w_out_ref, e)
            act = gelu_tanh(hidden_pre).astype(bf16)
            pre = (act_grad * gelu_slope(hidden_pre)).astype(bf16)
            for cut, out_ref in ((here, keep_ref), (there, give_ref)):
                out_ref[e, :, :half] = jnp.dot(
                    act, w_out_ref[e, :, cut], preferred_element_type=f32
                ).astype(bf16)
                out_ref[e, :, half:] = jnp.dot(
                    pre, w_in_ref[e, :, cut], preferred_element_type=f32
                ).astype(bf16)
            act_ref[e] = act
            pre_ref[e] = pre

    return pl.pallas_call(
        kernel,
        in_specs=[in_smem()] + [whole_in_vmem()] * 4,
        out_specs=[whole_in_vmem()] * 4,
        out_shape=[
            jax.ShapeDtypeStruct((experts, block, features), bf16),
            jax.ShapeDtypeStruct((experts, block, features), bf16),
            jax.ShapeDtypeStruct((experts, block, hidden), bf16),
            jax.ShapeDtypeStruct((experts, block, hidden), bf16),
        ],
        compiler_params=params(GRANT),
        cost_estimate=cost(8 * experts * block * hidden * features, 4 * experts * hidden * features),
        name="experts_part",
    )(place, mine, other, w_in, w_out)


def weight_grads(place, mine, other, act, pre):
    experts, block, hidden = act.shape
    features = mine.shape[2]
    half = features // 2

    def kernel(place_ref, mine_ref, other_ref, act_ref, pre_ref, in_ref, out_ref):
        here, there = halves(place_ref, half)
        for cut, from_ref in ((here, mine_ref), (there, other_ref)):
            in_ref[0, :, cut] = lax.dot_general(
                pre_ref[0], from_ref[0, :, :half], rows_contract, preferred_element_type=f32
            ).astype(bf16)
            out_ref[0, :, cut] = lax.dot_general(
                act_ref[0], from_ref[0, :, half:], rows_contract, preferred_element_type=f32
            ).astype(bf16)

    return pl.pallas_call(
        kernel,
        grid=(experts,),
        in_specs=[
            in_smem(),
            pl.BlockSpec((1, block, features), lambda e: (e, 0, 0)),
            pl.BlockSpec((1, block, features), lambda e: (e, 0, 0)),
            pl.BlockSpec((1, block, hidden), lambda e: (e, 0, 0)),
            pl.BlockSpec((1, block, hidden), lambda e: (e, 0, 0)),
        ],
        out_specs=[pl.BlockSpec((1, hidden, features), lambda e: (e, 0, 0))] * 2,
        out_shape=[jax.ShapeDtypeStruct((experts, hidden, features), bf16)] * 2,
        compiler_params=params(GRANT),
        cost_estimate=cost(4 * experts * block * hidden * features, 4 * experts * hidden * features),
        name="weight_grads",
    )(place, mine, other, act, pre)


def sum_terms(terms, slot_in, column, copies):
    sources, block, features = terms.shape
    half = features // 2
    width = features + LANES

    def kernel(terms_ref, in_ref, column_ref, sent_ref):
        total = terms_ref[0].astype(f32)
        for source in range(1, sources):
            total = total + terms_ref[source].astype(f32)
        low = total.astype(bf16)
        inner = jnp.sum(in_ref[...] * low[:, half:].astype(f32), axis=1, keepdims=True)
        power, inverse = guarded(column_ref[:, 0:1])
        lanes = in_lanes(block, two_parts(inverse) + (power,) + two_parts(inner))
        for copy in range(copies):
            sent_ref[copy, :, :features] = low
            sent_ref[copy, :, features:] = lanes

    return pl.pallas_call(
        kernel,
        in_specs=[whole_in_vmem()] * 3,
        out_specs=whole_in_vmem(),
        out_shape=jax.ShapeDtypeStruct((copies, block, width), bf16),
        compiler_params=params(GRANT),
        name="sum_terms",
    )(terms, slot_in, column)


def all_exps(place, keys_all, tokens, width, tile=256):
    blocks, features, block = keys_all.shape
    slots = blocks * block
    count = tokens.shape[0]
    half = features // 2

    def kernel(place_ref, keys_ref, tokens_ref, exp_ref, rows_ref, turned_ref):
        for at in range(blocks):
            cut = slice(at * block, (at + 1) * block)
            turned_ref[cut, :] = keys_ref[at].T
            for side in range(2):
                first = pl.multiple_of(place_ref[1] * width + side * half, 16)
                rows_ref[side, :, cut] = keys_ref[at, pl.ds(first, width), :]
        for at in range(0, count, tile):
            exp_ref[:, at : at + tile] = jnp.exp(
                lax.dot_general(
                    turned_ref[...], tokens_ref[at : at + tile, :], cols_contract,
                    preferred_element_type=f32,
                )
            ).astype(bf16)

    return pl.pallas_call(
        kernel,
        in_specs=[in_smem()] + [whole_in_vmem()] * 2,
        out_specs=[whole_in_vmem()] * 2,
        out_shape=[
            jax.ShapeDtypeStruct((slots, count), bf16),
            jax.ShapeDtypeStruct((2, width, slots), bf16),
        ],
        scratch_shapes=[pltpu.VMEM((slots, features), bf16)],
        compiler_params=params(GRANT),
        cost_estimate=cost(2 * slots * features * count, 2 * features * count),
        name="all_exps",
    )(place, keys_all, tokens)


def width_dot(place_ref, mine_ref, other_ref, ref, at, rows):
    blocks, block, _unused = mine_ref.shape
    half = ref.shape[1] // 2
    here, there = halves(place_ref, half)
    near = lax.dot_general(
        mine_ref[:, :, at * half : (at + 1) * half].reshape(blocks * block, half),
        ref[rows, here],
        cols_contract,
        preferred_element_type=f32,
    )
    far = lax.dot_general(
        other_ref[:, :, at * half : (at + 1) * half].reshape(blocks * block, half),
        ref[rows, there],
        cols_contract,
        preferred_element_type=f32,
    )
    return near + far


def comb_dots(place, exps, out_grad, row_parts, mine, other, tile=256):
    slots, count = exps.shape
    features = out_grad.shape[1]

    def kernel(place_ref, exp_ref, grad_ref, row_ref, mine_ref, other_ref, dot_ref, sum_ref):
        for at in range(0, count, tile):
            cut = slice(at, at + tile)
            power, inverse = guarded(jnp.sum(row_ref[:, :, cut], axis=0))
            dots = width_dot(place_ref, mine_ref, other_ref, grad_ref, 0, cut)
            dot_ref[:, cut] = dots
            terms = (exp_ref[:, cut].astype(f32) * power) * dots
            sum_ref[:, cut] = jnp.sum(terms, axis=0, keepdims=True) * inverse

    return pl.pallas_call(
        kernel,
        in_specs=[in_smem()] + [whole_in_vmem()] * 5,
        out_specs=[whole_in_vmem()] * 2,
        out_shape=[
            jax.ShapeDtypeStruct((slots, count), f32),
            jax.ShapeDtypeStruct((1, count), f32),
        ],
        compiler_params=params(GRANT),
        cost_estimate=cost(2 * slots * features * count, 2 * features * count),
        name="comb_dots",
    )(place, exps, out_grad, row_parts, mine, other)


def disp_dots(place, exps, dots, tokens, row_parts, mine, other, width, tile=256):
    slots, count = exps.shape
    features = tokens.shape[1]
    half = features // 2

    def kernel(
        place_ref, exp_ref, dot_ref, tokens_ref, row_ref, mine_ref, other_ref,
        terms_ref, dispatch_ref, rows_ref, power_ref, inverse_ref, total_ref, turned_ref,
    ):
        lanes = mine_ref[:, :, features:].reshape(slots, LANES).astype(f32)
        apart = other_ref[:, :, features:].reshape(slots, LANES).astype(f32)
        inner = lanes[:, 3:4] + lanes[:, 4:5] + apart[:, 3:4] + apart[:, 4:5]
        power_ref[...] = jnp.broadcast_to(lanes[:, 2:3], (slots, tile))
        inverse_ref[...] = jnp.broadcast_to(lanes[:, 0:1] + lanes[:, 1:2], (slots, tile))
        total_ref[...] = jnp.broadcast_to(inner, (slots, tile))
        rows = pl.ds(pl.multiple_of(place_ref[1] * width, 16), width)
        for at, ref in enumerate((mine_ref, other_ref)):
            turned_ref[...] = ref[:, :, half:features].reshape(slots, half).T
            rows_ref[at] = turned_ref[rows, :]
        for at in range(0, count, tile):
            cut = slice(at, at + tile)
            power, inverse = guarded(jnp.sum(row_ref[:, :, cut], axis=0))
            exps_here = exp_ref[:, cut].astype(f32)
            dispatch = (exps_here * power_ref[...]) * inverse_ref[...]
            dispatch_ref[:, cut] = dispatch.astype(bf16)
            disp_dot = width_dot(place_ref, mine_ref, other_ref, tokens_ref, 1, cut)
            combine = (exps_here * power) * inverse
            terms_ref[:, cut] = combine * dot_ref[:, cut] + dispatch * (disp_dot - total_ref[...])

    return pl.pallas_call(
        kernel,
        in_specs=[in_smem()] + [whole_in_vmem()] * 6,
        out_specs=[whole_in_vmem()] * 3,
        out_shape=[
            jax.ShapeDtypeStruct((slots, count), f32),
            jax.ShapeDtypeStruct((slots, count), bf16),
            jax.ShapeDtypeStruct((2, width, slots), bf16),
        ],
        scratch_shapes=[pltpu.VMEM((slots, tile), f32)] * 3 + [pltpu.VMEM((half, slots), bf16)],
        compiler_params=params(GRANT),
        cost_estimate=cost(2 * slots * features * count, 2 * features * count),
        name="disp_dots",
    )(place, exps, dots, tokens, row_parts, mine, other)


def logit_grads(place, exps, terms, dispatch, tokens, row_parts, row, row_other, keys_rows, grad_rows, own_slots, tile=256):
    slots, count = exps.shape
    features = tokens.shape[1]
    width = keys_rows.shape[1]

    def kernel(
        place_ref, exp_ref, terms_ref, dispatch_ref, tokens_ref, row_ref, sum_ref, other_ref, keys_rows_ref, grad_rows_ref,
        keys_ref, sent_ref, own_ref, logit_ref,
    ):
        core, half_at = place_ref[0], place_ref[2]
        near = jnp.where(core == half_at, 0, 1)
        for at in range(0, count, tile):
            cut = slice(at, at + tile)
            power, inverse = guarded(jnp.sum(row_ref[:, :, cut], axis=0))
            weight = (sum_ref[:, cut] + other_ref[:, cut]) * inverse
            exps_here = exp_ref[:, cut].astype(f32)
            logit_ref[:, cut] = (terms_ref[:, cut] - (exps_here * power) * weight).astype(bf16)
            for out_ref, at_keys, at_grad in (
                (sent_ref, 1 - half_at, 1 - near),
                (own_ref, half_at, near),
            ):
                total = jnp.dot(keys_rows_ref[at_keys], logit_ref[:, cut], preferred_element_type=f32)
                total = total + jnp.dot(
                    grad_rows_ref[at_grad], dispatch_ref[:, cut], preferred_element_type=f32
                )
                out_ref[:, cut] = total.astype(out_ref.dtype)
        own = pl.ds(pl.multiple_of(place_ref[1] * own_slots, own_slots), own_slots)
        total = jnp.dot(logit_ref[own, :], tokens_ref[...], preferred_element_type=f32)
        keys_ref[...] = total.T.astype(bf16)

    return pl.pallas_call(
        kernel,
        in_specs=[in_smem()] + [whole_in_vmem()] * 9,
        out_specs=[whole_in_vmem()] * 3,
        out_shape=[
            jax.ShapeDtypeStruct((features, own_slots), bf16),
            jax.ShapeDtypeStruct((width, count), bf16),
            jax.ShapeDtypeStruct((width, count), f32),
        ],
        scratch_shapes=[pltpu.VMEM((slots, count), bf16)],
        compiler_params=params(GRANT),
        cost_estimate=cost(2 * own_slots * features * count, 2 * features * count),
        name="logit_grads",
    )(place, exps, terms, dispatch, tokens, row_parts, row, row_other, keys_rows, grad_rows)


def per_device(tokens, slot_keys, w_in, w_out, out_grad):
    features = tokens.shape[1]
    own_slots = slot_keys.shape[1]
    slot_devices = lax.axis_size(SLOT)
    seq_devices = lax.axis_size(SEQ)
    groups = lax.axis_size(CHIPS)
    everyone = lax.axis_size(GATHERED)
    width = features // slot_devices
    swap = [(0, 1), (1, 0)]
    place = jnp.stack(
        [lax.axis_index("c"), lax.axis_index(KEYS), lax.axis_index("xa")]
    ).astype(jnp.int32)

    keys_all = lax.all_gather(slot_keys, KEYS, axis=0, tiled=False)
    exps, own_row, column = own_logits(slot_keys, tokens, slot_devices)
    column_other = lax.ppermute(column, "c", swap)
    row_parts = lax.all_to_all(own_row, SLOT, 0, 0)
    slot_in_part = dispatch_part(exps, column, column_other, tokens)
    keep, give = combine_part(
        place, exps, row_parts, column, column_other, slot_in_part, out_grad, groups
    )
    parts = lax.all_to_all(pair_sum(keep, lax.ppermute(give, "c", swap)), CHIPS, 0, 0)
    sent, slot_in, column_total = sum_slots(parts, groups)
    mine = lax.all_to_all(sent, CHIPS, 0, 0)
    other = lax.ppermute(mine, "c", swap)

    keep, give, act, pre = experts_part(place, mine, other, w_in, w_out)
    sent = pair_sum(keep, lax.ppermute(give, "c", swap))
    sent, keys_all = lax.optimization_barrier((sent, keys_all))
    terms = lax.all_to_all(sent, CHIPS, 0, 0)
    all_exp, keys_rows = all_exps(place, keys_all, tokens, width)
    terms, all_exp, act, pre = lax.optimization_barrier((terms, all_exp, act, pre))
    sent = sum_terms(terms, slot_in, column_total, everyone)
    gathered = lax.all_to_all(sent, GATHERED, 0, 0)
    grad_w_in, grad_w_out = weight_grads(place, mine, other, act, pre)
    gathered, grad_w_in, grad_w_out = lax.optimization_barrier((gathered, grad_w_in, grad_w_out))
    gathered_other = lax.ppermute(gathered, "c", swap)

    dots, row = comb_dots(place, all_exp, out_grad, row_parts, gathered, gathered_other)
    row_other = lax.ppermute(row, "xa", swap)
    terms, dispatch, grad_rows = disp_dots(
        place, all_exp, dots, tokens, row_parts, gathered, gathered_other, width
    )
    keys_part, sent, own_grads = logit_grads(
        place, all_exp, terms, dispatch, tokens, row_parts, row, row_other, keys_rows, grad_rows, own_slots
    )
    received = lax.ppermute(sent, "xa", swap)
    keys_parts = lax.all_to_all(
        keys_part.reshape(seq_devices, features // seq_devices, own_slots), SEQ, 0, 0
    )
    grad_tokens = (own_grads + received.astype(f32)).astype(bf16).T
    grad_keys = jnp.sum(keys_parts.astype(f32), axis=0)
    return (grad_tokens, grad_keys, grad_w_in, grad_w_out)


def solution(mesh):
    fine = Mesh(mesh.devices.reshape(2, 4, 2, 2, 2, 2), ("zl", "y", "c", "xa", "xb", "zh"))
    placed = (
        P(SEQ, None),
        P(None, SLOT),
        P(SLOT, SEQ, None),
        P(SLOT, SEQ, None),
        P(SEQ, None),
    )
    return jax.shard_map(
        per_device,
        mesh=fine,
        in_specs=placed,
        out_specs=(
            P(SEQ, SLOT),
            P(SEQ, SLOT),
            P(SLOT, SEQ, None),
            P(SLOT, SEQ, None),
        ),
        check_vma=False,
    )
```

```python
import jax
import jax.numpy as jnp
from jax import lax
from jax.experimental import pallas as pl
from jax.experimental.pallas import tpu as pltpu
from jax.sharding import Mesh, PartitionSpec as P

gelu_scale = 0.7978845608
gelu_cubic = 0.044715
rows_contract = (((0,), (0,)), ((), ()))
cols_contract = (((1,), (1,)), ((), ()))

SEQ = ("zl", "y", "c")
SLOT = ("xa", "xb", "zh")
KEYS = ("xb", "zh")
CHIPS = ("zl", "y")
GATHERED = ("xb", "zh", "zl", "y")
f32 = jnp.float32
bf16 = jnp.bfloat16
LANES = 128
MIB = 1 << 20
GRANT = 16
SCALE = 1


def gelu_tanh(values):
    return (
        0.5
        * values
        * (1.0 + jnp.tanh(gelu_scale * (values + gelu_cubic * values * values * values)))
    )


def gelu_slope(values):
    bent = jnp.tanh(gelu_scale * (values + gelu_cubic * values * values * values))
    return 0.5 * (1.0 + bent) + 0.5 * values * (1.0 - bent * bent) * gelu_scale * (
        1.0 + 3.0 * gelu_cubic * values * values
    )


def guarded(total):
    power = jnp.where(total > 2.0**64, 2.0**-32, jnp.where(total < 2.0**-64, 2.0**32, 1.0))
    return power, 1.0 / (total * power)


def two_parts(values):
    high = values.astype(bf16).astype(f32)
    return high, values - high


def in_lanes(rows, columns):
    lane = lax.broadcasted_iota(jnp.int32, (rows, LANES), 1)
    laid = jnp.zeros((rows, LANES), f32)
    for at, column in enumerate(columns):
        laid = jnp.where(lane == at, column, laid)
    return laid.astype(bf16)


def params(mib):
    return pltpu.CompilerParams(vmem_limit_bytes=mib * MIB)


def cost(flops, nbytes):
    return pl.CostEstimate(flops=SCALE * flops, bytes_accessed=nbytes, transcendentals=0)


def whole_in_vmem():
    return pl.BlockSpec(memory_space=pltpu.VMEM)


def in_smem():
    return pl.BlockSpec(memory_space=pltpu.SMEM)


def halves(place_ref, half):
    core = place_ref[0]
    here = pl.ds(pl.multiple_of(core * half, LANES), half)
    there = pl.ds(pl.multiple_of((1 - core) * half, LANES), half)
    return here, there


def own_logits(slot_keys, tokens, copies, tile=512):
    features, slots = slot_keys.shape
    count = tokens.shape[0]

    def kernel(slot_keys_ref, tokens_ref, exp_ref, row_ref, column_ref):
        keys = slot_keys_ref[...].T
        by_lane = jnp.zeros((slots, LANES), f32)
        for at in range(0, count, tile):
            cut = slice(at, at + tile)
            exps = jnp.exp(
                lax.dot_general(keys, tokens_ref[cut, :], cols_contract, preferred_element_type=f32)
            )
            exp_ref[:, cut] = exps
            row_ref[:, :, cut] = jnp.broadcast_to(
                jnp.sum(exps, axis=0, keepdims=True)[None], (copies, 1, tile)
            )
            for lanes in range(0, tile, LANES):
                by_lane = by_lane + exps[:, lanes : lanes + LANES]
        column_ref[...] = by_lane

    return pl.pallas_call(
        kernel,
        in_specs=[whole_in_vmem()] * 2,
        out_specs=[whole_in_vmem()] * 3,
        out_shape=[
            jax.ShapeDtypeStruct((slots, count), f32),
            jax.ShapeDtypeStruct((copies, 1, count), f32),
            jax.ShapeDtypeStruct((slots, LANES), f32),
        ],
        compiler_params=params(GRANT),
        cost_estimate=cost(2 * slots * features * count, 2 * features * count),
        name="own_logits",
    )(slot_keys, tokens)


def dispatch_part(exps, column, column_other, tokens):
    slots, count = exps.shape
    features = tokens.shape[1]

    def kernel(exp_ref, column_ref, other_ref, tokens_ref, out_ref, weights_ref):
        total = jnp.sum(column_ref[...] + other_ref[...], axis=1, keepdims=True)
        power, inverse = guarded(jnp.where(total > 0, total, 1.0))
        weights_ref[...] = ((exp_ref[...] * power) * inverse).astype(bf16)
        out_ref[...] = jnp.dot(
            weights_ref[...], tokens_ref[...], preferred_element_type=f32
        ).astype(bf16)

    return pl.pallas_call(
        kernel,
        in_specs=[whole_in_vmem()] * 4,
        out_specs=whole_in_vmem(),
        out_shape=jax.ShapeDtypeStruct((slots, features), bf16),
        scratch_shapes=[pltpu.VMEM((slots, count), bf16)],
        compiler_params=params(GRANT),
        cost_estimate=cost(2 * slots * features * count, 2 * features * count),
        name="dispatch_part",
    )(exps, column, column_other, tokens)


def combine_part(place, exps, row_parts, column, column_other, slot_in_part, out_grad, groups):
    slots, count = exps.shape
    features = out_grad.shape[1]
    half = features // 2
    block = slots // groups

    def kernel(
        place_ref, exp_ref, row_ref, column_ref, other_ref, in_ref, grad_ref,
        keep_ref, give_ref, weights_ref, total_ref,
    ):
        power, inverse = guarded(jnp.sum(row_ref[...], axis=0))
        weights_ref[...] = ((exp_ref[...] * power) * inverse).astype(bf16)
        total = jnp.sum(column_ref[...] + other_ref[...], axis=1, keepdims=True)
        shift, _unused = guarded(total)
        high, low = two_parts(total * shift)
        lanes = in_lanes(slots, (high, low, 1.0 / shift))
        total_ref[...] = jnp.dot(
            weights_ref[...], grad_ref[...], preferred_element_type=f32
        ).astype(bf16)
        here, there = halves(place_ref, half)
        for group in range(groups):
            rows = slice(group * block, (group + 1) * block)
            keep_ref[group, :, :half] = in_ref[rows, here]
            keep_ref[group, :, half:features] = total_ref[rows, here]
            keep_ref[group, :, features:] = lanes[rows]
            give_ref[group, :, :half] = in_ref[rows, there]
            give_ref[group, :, half:] = total_ref[rows, there]

    return pl.pallas_call(
        kernel,
        in_specs=[in_smem()] + [whole_in_vmem()] * 6,
        out_specs=[whole_in_vmem()] * 2,
        out_shape=[
            jax.ShapeDtypeStruct((groups, block, features + LANES), bf16),
            jax.ShapeDtypeStruct((groups, block, features), bf16),
        ],
        scratch_shapes=[
            pltpu.VMEM((slots, count), bf16),
            pltpu.VMEM((slots, features), bf16),
        ],
        compiler_params=params(GRANT),
        cost_estimate=cost(2 * slots * features * count, 2 * features * count),
        name="combine_part",
    )(place, exps, row_parts, column, column_other, slot_in_part, out_grad)


def pair_sum(keep, received):
    features = received.shape[2]

    def kernel(keep_ref, received_ref, out_ref):
        total = keep_ref[:, :, :features].astype(f32) + received_ref[...].astype(f32)
        out_ref[:, :, :features] = total.astype(bf16)
        if keep_ref.shape[2] > features:
            out_ref[:, :, features:] = keep_ref[:, :, features:]

    return pl.pallas_call(
        kernel,
        in_specs=[whole_in_vmem()] * 2,
        out_specs=whole_in_vmem(),
        out_shape=jax.ShapeDtypeStruct(keep.shape, bf16),
        compiler_params=params(GRANT),
        name="pair_sum",
    )(keep, received)


def sum_slots(parts, copies):
    sources, block, width = parts.shape
    features = width - LANES
    half = features // 2

    def kernel(parts_ref, sent_ref, in_ref, column_ref):
        lanes = parts_ref[:, :, features:].astype(f32)
        columns = (lanes[:, :, 0:1] + lanes[:, :, 1:2]) * lanes[:, :, 2:3]
        total = jnp.sum(columns, axis=0)
        power, inverse = guarded(total)
        share = (columns * power[None]) * inverse[None]
        slot_in = jnp.zeros((block, half), f32)
        slot_grad = jnp.zeros((block, half), f32)
        for source in range(sources):
            slot_in = slot_in + parts_ref[source, :, :half].astype(f32) * share[source]
            slot_grad = slot_grad + parts_ref[source, :, half:features].astype(f32)
        in_ref[...] = slot_in
        column_ref[...] = jnp.broadcast_to(total, (block, LANES))
        in_low = slot_in.astype(bf16)
        grad_low = slot_grad.astype(bf16)
        for copy in range(copies):
            sent_ref[copy, :, :half] = in_low
            sent_ref[copy, :, half:] = grad_low

    return pl.pallas_call(
        kernel,
        in_specs=[whole_in_vmem()],
        out_specs=[whole_in_vmem()] * 3,
        out_shape=[
            jax.ShapeDtypeStruct((copies, block, features), bf16),
            jax.ShapeDtypeStruct((block, half), f32),
            jax.ShapeDtypeStruct((block, LANES), f32),
        ],
        compiler_params=params(GRANT),
        name="sum_slots",
    )(parts)


def experts_part(place, mine, other, w_in, w_out):
    experts, hidden, features = w_in.shape
    block = mine.shape[1]
    half = features // 2

    def kernel(place_ref, mine_ref, other_ref, w_in_ref, w_out_ref, keep_ref, give_ref, act_hbm, pre_hbm, act_ref, pre_ref, sems):
        here, there = halves(place_ref, half)

        def inward(at, weights_ref, e):
            cut = slice(at * half, (at + 1) * half)
            near = lax.dot_general(
                mine_ref[e, :, cut], weights_ref[e, :, here], cols_contract, preferred_element_type=f32
            )
            far = lax.dot_general(
                other_ref[e, :, cut], weights_ref[e, :, there], cols_contract, preferred_element_type=f32
            )
            return near + far

        for e in range(experts):
            hidden_pre = inward(0, w_in_ref, e)
            act_grad = inward(1, w_out_ref, e)
            act = gelu_tanh(hidden_pre).astype(bf16)
            pre = (act_grad * gelu_slope(hidden_pre)).astype(bf16)
            for cut, out_ref in ((here, keep_ref), (there, give_ref)):
                out_ref[e, :, :half] = jnp.dot(
                    act, w_out_ref[e, :, cut], preferred_element_type=f32
                ).astype(bf16)
                out_ref[e, :, half:] = jnp.dot(
                    pre, w_in_ref[e, :, cut], preferred_element_type=f32
                ).astype(bf16)
            act_ref[e] = act
            pre_ref[e] = pre
        first = pltpu.make_async_copy(act_ref, act_hbm, sems.at[0])
        second = pltpu.make_async_copy(pre_ref, pre_hbm, sems.at[1])
        first.start()
        second.start()
        first.wait()
        second.wait()

    return pl.pallas_call(
        kernel,
        in_specs=[in_smem()] + [whole_in_vmem()] * 4,
        out_specs=[whole_in_vmem()] * 2 + [pl.BlockSpec(memory_space=pltpu.HBM)] * 2,
        out_shape=[
            jax.ShapeDtypeStruct((experts, block, features), bf16),
            jax.ShapeDtypeStruct((experts, block, features), bf16),
            jax.ShapeDtypeStruct((experts, block, hidden), bf16),
            jax.ShapeDtypeStruct((experts, block, hidden), bf16),
        ],
        scratch_shapes=[pltpu.VMEM((experts, block, hidden), bf16)] * 2 + [pltpu.SemaphoreType.DMA((2,))],
        compiler_params=params(GRANT),
        cost_estimate=cost(8 * experts * block * hidden * features, 4 * experts * hidden * features),
        name="experts_part",
    )(place, mine, other, w_in, w_out)


def weight_grads(place, mine, other, act, pre):
    experts, block, hidden = act.shape
    features = mine.shape[2]
    half = features // 2

    def kernel(place_ref, mine_ref, other_ref, act_ref, pre_ref, in_ref, out_ref):
        here, there = halves(place_ref, half)
        for cut, from_ref in ((here, mine_ref), (there, other_ref)):
            in_ref[0, :, cut] = lax.dot_general(
                pre_ref[0], from_ref[0, :, :half], rows_contract, preferred_element_type=f32
            ).astype(bf16)
            out_ref[0, :, cut] = lax.dot_general(
                act_ref[0], from_ref[0, :, half:], rows_contract, preferred_element_type=f32
            ).astype(bf16)

    return pl.pallas_call(
        kernel,
        grid=(experts,),
        in_specs=[
            in_smem(),
            pl.BlockSpec((1, block, features), lambda e: (e, 0, 0)),
            pl.BlockSpec((1, block, features), lambda e: (e, 0, 0)),
            pl.BlockSpec((1, block, hidden), lambda e: (e, 0, 0)),
            pl.BlockSpec((1, block, hidden), lambda e: (e, 0, 0)),
        ],
        out_specs=[pl.BlockSpec((1, hidden, features), lambda e: (e, 0, 0))] * 2,
        out_shape=[jax.ShapeDtypeStruct((experts, hidden, features), bf16)] * 2,
        compiler_params=params(GRANT),
        cost_estimate=cost(4 * experts * block * hidden * features, 4 * experts * hidden * features),
        name="weight_grads",
    )(place, mine, other, act, pre)


def sum_terms(terms, slot_in, column, copies):
    sources, block, features = terms.shape
    half = features // 2
    width = features + LANES

    def kernel(terms_ref, in_ref, column_ref, sent_ref):
        total = terms_ref[0].astype(f32)
        for source in range(1, sources):
            total = total + terms_ref[source].astype(f32)
        low = total.astype(bf16)
        inner = jnp.sum(in_ref[...] * low[:, half:].astype(f32), axis=1, keepdims=True)
        power, inverse = guarded(column_ref[:, 0:1])
        lanes = in_lanes(block, two_parts(inverse) + (power,) + two_parts(inner))
        for copy in range(copies):
            sent_ref[copy, :, :features] = low
            sent_ref[copy, :, features:] = lanes

    return pl.pallas_call(
        kernel,
        in_specs=[whole_in_vmem()] * 3,
        out_specs=whole_in_vmem(),
        out_shape=jax.ShapeDtypeStruct((copies, block, width), bf16),
        compiler_params=params(GRANT),
        name="sum_terms",
    )(terms, slot_in, column)


def all_exps(place, slot_keys, near_keys, far_keys, tokens, width, tile=256):
    features, block = slot_keys.shape
    count = tokens.shape[0]
    half = features // 2
    others = len(near_keys)
    slots = (others + 1) * block

    def kernel(place_ref, own_ref, *refs):
        near_refs, far_refs = refs[:others], refs[others : 2 * others]
        tokens_ref, exp_ref, rows_ref, turned_ref = refs[2 * others :]
        core, at_own = place_ref[0], place_ref[1]
        here, there = halves(place_ref, half)

        def spot(at):
            return pl.ds(pl.multiple_of(at * block, block), block)

        rows = pl.ds(pl.multiple_of(at_own * width, 16), width)
        turned_ref[spot(at_own), :] = own_ref[...].T
        for side in range(2):
            first = pl.multiple_of(at_own * width + side * half, 16)
            rows_ref[side, :, spot(at_own)] = own_ref[pl.ds(first, width), :]
        for at in range(others):
            place_at = spot(at_own ^ (at + 1))
            turned_ref[place_at, here] = near_refs[at][...].T
            turned_ref[place_at, there] = far_refs[at][...].T
            rows_ref[core, :, place_at] = near_refs[at][rows, :]
            rows_ref[1 - core, :, place_at] = far_refs[at][rows, :]
        for at in range(0, count, tile):
            exp_ref[:, at : at + tile] = jnp.exp(
                lax.dot_general(
                    turned_ref[...], tokens_ref[at : at + tile, :], cols_contract,
                    preferred_element_type=f32,
                )
            ).astype(bf16)

    return pl.pallas_call(
        kernel,
        in_specs=[in_smem()] + [whole_in_vmem()] * (2 * others + 2),
        out_specs=[whole_in_vmem()] * 2,
        out_shape=[
            jax.ShapeDtypeStruct((slots, count), bf16),
            jax.ShapeDtypeStruct((2, width, slots), bf16),
        ],
        scratch_shapes=[pltpu.VMEM((slots, features), bf16)],
        compiler_params=params(GRANT),
        cost_estimate=cost(2 * slots * features * count, 2 * features * count),
        name="all_exps",
    )(place, slot_keys, *near_keys, *far_keys, tokens)


def half_dot(place_ref, gathered_ref, ref, at, rows, own):
    blocks, block, _unused = gathered_ref.shape
    half = ref.shape[1] // 2
    here, there = halves(place_ref, half)
    return lax.dot_general(
        gathered_ref[:, :, at * half : (at + 1) * half].reshape(blocks * block, half),
        ref[rows, here if own else there],
        cols_contract,
        preferred_element_type=f32,
    )


def near_dots(place, out_grad, mine, slots, tile=256):
    count, features = out_grad.shape

    def kernel(place_ref, grad_ref, mine_ref, dot_ref):
        for at in range(0, count, tile):
            cut = slice(at, at + tile)
            dot_ref[:, cut] = half_dot(place_ref, mine_ref, grad_ref, 0, cut, True)

    return pl.pallas_call(
        kernel,
        in_specs=[in_smem()] + [whole_in_vmem()] * 2,
        out_specs=whole_in_vmem(),
        out_shape=jax.ShapeDtypeStruct((slots, count), f32),
        compiler_params=params(GRANT),
        cost_estimate=cost(slots * features * count, features * count),
        name="near_dots",
    )(place, out_grad, mine)


def comb_dots(place, exps, near, out_grad, row_parts, other, tile=256):
    slots, count = exps.shape
    features = out_grad.shape[1]

    def kernel(place_ref, exp_ref, near_ref, grad_ref, row_ref, other_ref, dot_ref, sum_ref):
        for at in range(0, count, tile):
            cut = slice(at, at + tile)
            power, inverse = guarded(jnp.sum(row_ref[:, :, cut], axis=0))
            dots = near_ref[:, cut] + half_dot(place_ref, other_ref, grad_ref, 0, cut, False)
            dot_ref[:, cut] = dots
            terms = (exp_ref[:, cut].astype(f32) * power) * dots
            sum_ref[:, cut] = jnp.sum(terms, axis=0, keepdims=True) * inverse

    return pl.pallas_call(
        kernel,
        in_specs=[in_smem()] + [whole_in_vmem()] * 5,
        out_specs=[whole_in_vmem()] * 2,
        out_shape=[
            jax.ShapeDtypeStruct((slots, count), f32),
            jax.ShapeDtypeStruct((1, count), f32),
        ],
        compiler_params=params(GRANT),
        cost_estimate=cost(slots * features * count, features * count),
        name="comb_dots",
    )(place, exps, near, out_grad, row_parts, other)


def disp_dots(place, exps, dots, tokens, row_parts, mine, other, width, tile=256):
    slots, count = exps.shape
    features = tokens.shape[1]
    half = features // 2

    def kernel(
        place_ref, exp_ref, dot_ref, tokens_ref, row_ref, mine_ref, other_ref,
        terms_ref, dispatch_ref, rows_ref, power_ref, inverse_ref, total_ref, turned_ref,
    ):
        lanes = mine_ref[:, :, features:].reshape(slots, LANES).astype(f32)
        apart = other_ref[:, :, features:].reshape(slots, LANES).astype(f32)
        inner = lanes[:, 3:4] + lanes[:, 4:5] + apart[:, 3:4] + apart[:, 4:5]
        power_ref[...] = jnp.broadcast_to(lanes[:, 2:3], (slots, tile))
        inverse_ref[...] = jnp.broadcast_to(lanes[:, 0:1] + lanes[:, 1:2], (slots, tile))
        total_ref[...] = jnp.broadcast_to(inner, (slots, tile))
        rows = pl.ds(pl.multiple_of(place_ref[1] * width, 16), width)
        for at, ref in enumerate((mine_ref, other_ref)):
            turned_ref[...] = ref[:, :, half:features].reshape(slots, half).T
            rows_ref[at] = turned_ref[rows, :]
        for at in range(0, count, tile):
            cut = slice(at, at + tile)
            power, inverse = guarded(jnp.sum(row_ref[:, :, cut], axis=0))
            exps_here = exp_ref[:, cut].astype(f32)
            dispatch = (exps_here * power_ref[...]) * inverse_ref[...]
            dispatch_ref[:, cut] = dispatch.astype(bf16)
            disp_dot = half_dot(place_ref, mine_ref, tokens_ref, 1, cut, True)
            disp_dot = disp_dot + half_dot(place_ref, other_ref, tokens_ref, 1, cut, False)
            combine = (exps_here * power) * inverse
            terms_ref[:, cut] = combine * dot_ref[:, cut] + dispatch * (disp_dot - total_ref[...])

    return pl.pallas_call(
        kernel,
        in_specs=[in_smem()] + [whole_in_vmem()] * 6,
        out_specs=[whole_in_vmem()] * 3,
        out_shape=[
            jax.ShapeDtypeStruct((slots, count), f32),
            jax.ShapeDtypeStruct((slots, count), bf16),
            jax.ShapeDtypeStruct((2, width, slots), bf16),
        ],
        scratch_shapes=[pltpu.VMEM((slots, tile), f32)] * 3 + [pltpu.VMEM((half, slots), bf16)],
        compiler_params=params(GRANT),
        cost_estimate=cost(2 * slots * features * count, 2 * features * count),
        name="disp_dots",
    )(place, exps, dots, tokens, row_parts, mine, other)


def columns_dot(place_ref, keys_rows_ref, grad_rows_ref, logit, dispatch, own):
    core, half_at = place_ref[0], place_ref[2]
    near = jnp.where(core == half_at, 0, 1)
    at_keys, at_grad = (half_at, near) if own else (1 - half_at, 1 - near)
    total = jnp.dot(keys_rows_ref[at_keys], logit, preferred_element_type=f32)
    return total + jnp.dot(grad_rows_ref[at_grad], dispatch, preferred_element_type=f32)


def logit_grads(place, exps, terms, dispatch, row_parts, row, row_other, keys_rows, grad_rows, tile=256):
    slots, count = exps.shape
    width = keys_rows.shape[1]

    def kernel(
        place_ref, exp_ref, terms_ref, dispatch_ref, row_ref, sum_ref, other_ref, keys_rows_ref, grad_rows_ref,
        logit_ref, sent_ref,
    ):
        for at in range(0, count, tile):
            cut = slice(at, at + tile)
            power, inverse = guarded(jnp.sum(row_ref[:, :, cut], axis=0))
            weight = (sum_ref[:, cut] + other_ref[:, cut]) * inverse
            exps_here = exp_ref[:, cut].astype(f32)
            logit_ref[:, cut] = (terms_ref[:, cut] - (exps_here * power) * weight).astype(bf16)
            sent_ref[:, cut] = columns_dot(
                place_ref, keys_rows_ref, grad_rows_ref, logit_ref[:, cut], dispatch_ref[:, cut], False
            ).astype(bf16)

    return pl.pallas_call(
        kernel,
        in_specs=[in_smem()] + [whole_in_vmem()] * 8,
        out_specs=[whole_in_vmem()] * 2,
        out_shape=[
            jax.ShapeDtypeStruct((slots, count), bf16),
            jax.ShapeDtypeStruct((width, count), bf16),
        ],
        compiler_params=params(GRANT),
        cost_estimate=cost(4 * slots * width * count, 4 * slots * count),
        name="logit_grads",
    )(place, exps, terms, dispatch, row_parts, row, row_other, keys_rows, grad_rows)


def own_parts(place, logit, dispatch, tokens, keys_rows, grad_rows, own_slots, tile=256):
    count, features = tokens.shape
    width = keys_rows.shape[1]

    def kernel(place_ref, logit_ref, dispatch_ref, tokens_ref, keys_rows_ref, grad_rows_ref, keys_ref, own_ref):
        own = pl.ds(pl.multiple_of(place_ref[1] * own_slots, own_slots), own_slots)
        total = jnp.dot(logit_ref[own, :], tokens_ref[...], preferred_element_type=f32)
        keys_ref[...] = total.T.astype(bf16)
        for at in range(0, count, tile):
            cut = slice(at, at + tile)
            own_ref[:, cut] = columns_dot(
                place_ref, keys_rows_ref, grad_rows_ref, logit_ref[:, cut], dispatch_ref[:, cut], True
            )

    return pl.pallas_call(
        kernel,
        in_specs=[in_smem()] + [whole_in_vmem()] * 5,
        out_specs=[whole_in_vmem()] * 2,
        out_shape=[
            jax.ShapeDtypeStruct((features, own_slots), bf16),
            jax.ShapeDtypeStruct((width, count), f32),
        ],
        compiler_params=params(GRANT),
        cost_estimate=cost(2 * own_slots * features * count, 2 * features * count),
        name="own_parts",
    )(place, logit, dispatch, tokens, keys_rows, grad_rows)


def per_device(tokens, slot_keys, w_in, w_out, out_grad):
    features = tokens.shape[1]
    own_slots = slot_keys.shape[1]
    slot_devices = lax.axis_size(SLOT)
    seq_devices = lax.axis_size(SEQ)
    groups = lax.axis_size(CHIPS)
    everyone = lax.axis_size(GATHERED)
    width = features // slot_devices
    swap = [(0, 1), (1, 0)]
    place = jnp.stack(
        [lax.axis_index("c"), lax.axis_index(KEYS), lax.axis_index("xa")]
    ).astype(jnp.int32)

    half = features // 2
    own_half = lax.dynamic_slice_in_dim(slot_keys, lax.axis_index("c") * half, half, 0)
    blocks = lax.axis_size(KEYS)
    near_keys = [
        lax.ppermute(own_half, KEYS, [(at, at ^ other) for at in range(blocks)])
        for other in range(1, blocks)
    ]
    exps, own_row, column = own_logits(slot_keys, tokens, slot_devices)
    own_row, near_keys = lax.optimization_barrier((own_row, near_keys))
    far_keys = [lax.ppermute(keys, "c", swap) for keys in near_keys]
    column_other = lax.ppermute(column, "c", swap)
    row_parts = lax.all_to_all(own_row, SLOT, 0, 0)
    slot_in_part = dispatch_part(exps, column, column_other, tokens)
    keep, give = combine_part(
        place, exps, row_parts, column, column_other, slot_in_part, out_grad, groups
    )
    parts = lax.all_to_all(pair_sum(keep, lax.ppermute(give, "c", swap)), CHIPS, 0, 0)
    sent, slot_in, column_total = sum_slots(parts, groups)
    mine = lax.all_to_all(sent, CHIPS, 0, 0)
    other = lax.ppermute(mine, "c", swap)

    keep, give, act, pre = experts_part(place, mine, other, w_in, w_out)
    sent = pair_sum(keep, lax.ppermute(give, "c", swap))
    sent, near_keys, far_keys = lax.optimization_barrier((sent, near_keys, far_keys))
    terms = lax.all_to_all(sent, CHIPS, 0, 0)
    all_exp, keys_rows = all_exps(place, slot_keys, near_keys, far_keys, tokens, width)
    terms, all_exp, act, pre = lax.optimization_barrier((terms, all_exp, act, pre))
    sent = sum_terms(terms, slot_in, column_total, everyone)
    gathered = lax.all_to_all(sent, GATHERED, 0, 0)
    grad_w_in, grad_w_out = weight_grads(place, mine, other, act, pre)
    gathered, grad_w_in, grad_w_out = lax.optimization_barrier((gathered, grad_w_in, grad_w_out))
    gathered_other = lax.ppermute(gathered, "c", swap)

    near = near_dots(place, out_grad, gathered, all_exp.shape[0])
    gathered_other, near = lax.optimization_barrier((gathered_other, near))
    dots, row = comb_dots(place, all_exp, near, out_grad, row_parts, gathered_other)
    row_other = lax.ppermute(row, "xa", swap)
    terms, dispatch, grad_rows = disp_dots(
        place, all_exp, dots, tokens, row_parts, gathered, gathered_other, width
    )
    logit, sent = logit_grads(
        place, all_exp, terms, dispatch, row_parts, row, row_other, keys_rows, grad_rows
    )
    received = lax.ppermute(sent, "xa", swap)
    keys_part, own_grads = own_parts(
        place, logit, dispatch, tokens, keys_rows, grad_rows, own_slots
    )
    keys_parts = lax.all_to_all(
        keys_part.reshape(seq_devices, features // seq_devices, own_slots), SEQ, 0, 0
    )
    grad_tokens = (own_grads + received.astype(f32)).astype(bf16).T
    grad_keys = jnp.sum(keys_parts.astype(f32), axis=0)
    return (grad_tokens, grad_keys, grad_w_in, grad_w_out)


def solution(mesh):
    fine = Mesh(mesh.devices.reshape(2, 4, 2, 2, 2, 2), ("zl", "y", "c", "xa", "xb", "zh"))
    placed = (
        P(SEQ, None),
        P(None, SLOT),
        P(SLOT, SEQ, None),
        P(SLOT, SEQ, None),
        P(SEQ, None),
    )
    return jax.shard_map(
        per_device,
        mesh=fine,
        in_specs=placed,
        out_specs=(
            P(SEQ, SLOT),
            P(SEQ, SLOT),
            P(SLOT, SEQ, None),
            P(SLOT, SEQ, None),
        ),
        check_vma=False,
    )
```

```python
import jax
import jax.numpy as jnp
from jax import lax
from jax.experimental import pallas as pl
from jax.experimental.pallas import tpu as pltpu
from jax.sharding import Mesh, PartitionSpec as P

gelu_scale = 0.7978845608
gelu_cubic = 0.044715
rows_contract = (((0,), (0,)), ((), ()))
cols_contract = (((1,), (1,)), ((), ()))

SEQ = ("zl", "y", "c")
SLOT = ("xa", "xb", "zh")
KEYS = ("xb", "zh")
CHIPS = ("zl", "y")
GATHERED = ("xb", "zh", "zl", "y")
f32 = jnp.float32
bf16 = jnp.bfloat16
LANES = 128
MIB = 1 << 20
GRANT = 16
SCALE = 1


def gelu_tanh(values):
    return (
        0.5
        * values
        * (1.0 + jnp.tanh(gelu_scale * (values + gelu_cubic * values * values * values)))
    )


def gelu_slope(values):
    bent = jnp.tanh(gelu_scale * (values + gelu_cubic * values * values * values))
    return 0.5 * (1.0 + bent) + 0.5 * values * (1.0 - bent * bent) * gelu_scale * (
        1.0 + 3.0 * gelu_cubic * values * values
    )


def guarded(total):
    power = jnp.where(total > 2.0**64, 2.0**-32, jnp.where(total < 2.0**-64, 2.0**32, 1.0))
    return power, 1.0 / (total * power)


def two_parts(values):
    high = values.astype(bf16).astype(f32)
    return high, values - high


def in_lanes(rows, columns):
    lane = lax.broadcasted_iota(jnp.int32, (rows, LANES), 1)
    laid = jnp.zeros((rows, LANES), f32)
    for at, column in enumerate(columns):
        laid = jnp.where(lane == at, column, laid)
    return laid.astype(bf16)


def params(mib):
    return pltpu.CompilerParams(vmem_limit_bytes=mib * MIB)


def cost(flops, nbytes):
    return pl.CostEstimate(flops=SCALE * flops, bytes_accessed=nbytes, transcendentals=0)


def whole_in_vmem():
    return pl.BlockSpec(memory_space=pltpu.VMEM)


def in_smem():
    return pl.BlockSpec(memory_space=pltpu.SMEM)


def halves(place_ref, half):
    core = place_ref[0]
    here = pl.ds(pl.multiple_of(core * half, LANES), half)
    there = pl.ds(pl.multiple_of((1 - core) * half, LANES), half)
    return here, there


def dispatch_part(exps, column, column_other, tokens):
    slots, count = exps.shape
    features = tokens.shape[1]

    def kernel(exp_ref, column_ref, other_ref, tokens_ref, out_ref, weights_ref):
        total = jnp.sum(column_ref[...] + other_ref[...], axis=1, keepdims=True)
        power, inverse = guarded(jnp.where(total > 0, total, 1.0))
        weights_ref[...] = ((exp_ref[...] * power) * inverse).astype(bf16)
        out_ref[...] = jnp.dot(
            weights_ref[...], tokens_ref[...], preferred_element_type=f32
        ).astype(bf16)

    return pl.pallas_call(
        kernel,
        in_specs=[whole_in_vmem()] * 4,
        out_specs=whole_in_vmem(),
        out_shape=jax.ShapeDtypeStruct((slots, features), bf16),
        scratch_shapes=[pltpu.VMEM((slots, count), bf16)],
        compiler_params=params(GRANT),
        cost_estimate=cost(2 * slots * features * count, 2 * features * count),
        name="dispatch_part",
    )(exps, column, column_other, tokens)


def combine_part(place, exps, row, row_other, column, column_other, slot_in_part, out_grad, groups):
    slots, count = exps.shape
    features = out_grad.shape[1]
    half = features // 2
    block = slots // groups

    def kernel(
        place_ref, exp_ref, row_ref, row_other_ref, column_ref, other_ref, in_ref, grad_ref,
        keep_ref, give_ref, row_total_ref, weights_ref, total_ref,
    ):
        row_total_ref[...] = row_ref[...] + row_other_ref[...]
        power, inverse = guarded(row_total_ref[...])
        weights_ref[...] = ((exp_ref[...] * power) * inverse).astype(bf16)
        total = jnp.sum(column_ref[...] + other_ref[...], axis=1, keepdims=True)
        shift, _unused = guarded(total)
        high, low = two_parts(total * shift)
        lanes = in_lanes(slots, (high, low, 1.0 / shift))
        total_ref[...] = jnp.dot(
            weights_ref[...], grad_ref[...], preferred_element_type=f32
        ).astype(bf16)
        here, there = halves(place_ref, half)
        for group in range(groups):
            rows = slice(group * block, (group + 1) * block)
            keep_ref[group, :, :half] = in_ref[rows, here]
            keep_ref[group, :, half:features] = total_ref[rows, here]
            keep_ref[group, :, features:] = lanes[rows]
            give_ref[group, :, :half] = in_ref[rows, there]
            give_ref[group, :, half:] = total_ref[rows, there]

    return pl.pallas_call(
        kernel,
        in_specs=[in_smem()] + [whole_in_vmem()] * 7,
        out_specs=[whole_in_vmem()] * 3,
        out_shape=[
            jax.ShapeDtypeStruct((groups, block, features + LANES), bf16),
            jax.ShapeDtypeStruct((groups, block, features), bf16),
            jax.ShapeDtypeStruct((1, count), f32),
        ],
        scratch_shapes=[
            pltpu.VMEM((slots, count), bf16),
            pltpu.VMEM((slots, features), bf16),
        ],
        compiler_params=params(GRANT),
        cost_estimate=cost(2 * slots * features * count, 2 * features * count),
        name="combine_part",
    )(place, exps, row, row_other, column, column_other, slot_in_part, out_grad)


def pair_sum(keep, received):
    features = received.shape[2]

    def kernel(keep_ref, received_ref, out_ref):
        total = keep_ref[:, :, :features].astype(f32) + received_ref[...].astype(f32)
        out_ref[:, :, :features] = total.astype(bf16)
        if keep_ref.shape[2] > features:
            out_ref[:, :, features:] = keep_ref[:, :, features:]

    return pl.pallas_call(
        kernel,
        in_specs=[whole_in_vmem()] * 2,
        out_specs=whole_in_vmem(),
        out_shape=jax.ShapeDtypeStruct(keep.shape, bf16),
        compiler_params=params(GRANT),
        name="pair_sum",
    )(keep, received)


def sum_slots(parts, copies):
    sources, block, width = parts.shape
    features = width - LANES
    half = features // 2

    def kernel(parts_ref, sent_ref, in_ref, column_ref):
        lanes = parts_ref[:, :, features:].astype(f32)
        columns = (lanes[:, :, 0:1] + lanes[:, :, 1:2]) * lanes[:, :, 2:3]
        total = jnp.sum(columns, axis=0)
        power, inverse = guarded(total)
        share = (columns * power[None]) * inverse[None]
        slot_in = jnp.zeros((block, half), f32)
        slot_grad = jnp.zeros((block, half), f32)
        for source in range(sources):
            slot_in = slot_in + parts_ref[source, :, :half].astype(f32) * share[source]
            slot_grad = slot_grad + parts_ref[source, :, half:features].astype(f32)
        in_ref[...] = slot_in
        column_ref[...] = jnp.broadcast_to(total, (block, LANES))
        in_low = slot_in.astype(bf16)
        grad_low = slot_grad.astype(bf16)
        for copy in range(copies):
            sent_ref[copy, :, :half] = in_low
            sent_ref[copy, :, half:] = grad_low

    return pl.pallas_call(
        kernel,
        in_specs=[whole_in_vmem()],
        out_specs=[whole_in_vmem()] * 3,
        out_shape=[
            jax.ShapeDtypeStruct((copies, block, features), bf16),
            jax.ShapeDtypeStruct((block, half), f32),
            jax.ShapeDtypeStruct((block, LANES), f32),
        ],
        compiler_params=params(GRANT),
        name="sum_slots",
    )(parts)


def experts_part(place, mine, other, w_in, w_out):
    experts, hidden, features = w_in.shape
    block = mine.shape[1]
    half = features // 2

    def kernel(place_ref, mine_ref, other_ref, w_in_ref, w_out_ref, keep_ref, give_ref, act_hbm, pre_hbm, act_ref, pre_ref, sems):
        here, there = halves(place_ref, half)

        def inward(at, weights_ref, e):
            cut = slice(at * half, (at + 1) * half)
            near = lax.dot_general(
                mine_ref[e, :, cut], weights_ref[e, :, here], cols_contract, preferred_element_type=f32
            )
            far = lax.dot_general(
                other_ref[e, :, cut], weights_ref[e, :, there], cols_contract, preferred_element_type=f32
            )
            return near + far

        for e in range(experts):
            hidden_pre = inward(0, w_in_ref, e)
            act_grad = inward(1, w_out_ref, e)
            act = gelu_tanh(hidden_pre).astype(bf16)
            pre = (act_grad * gelu_slope(hidden_pre)).astype(bf16)
            for cut, out_ref in ((here, keep_ref), (there, give_ref)):
                out_ref[e, :, :half] = jnp.dot(
                    act, w_out_ref[e, :, cut], preferred_element_type=f32
                ).astype(bf16)
                out_ref[e, :, half:] = jnp.dot(
                    pre, w_in_ref[e, :, cut], preferred_element_type=f32
                ).astype(bf16)
            act_ref[e] = act
            pre_ref[e] = pre
        first = pltpu.make_async_copy(act_ref, act_hbm, sems.at[0])
        second = pltpu.make_async_copy(pre_ref, pre_hbm, sems.at[1])
        first.start()
        second.start()
        first.wait()
        second.wait()

    return pl.pallas_call(
        kernel,
        in_specs=[in_smem()] + [whole_in_vmem()] * 4,
        out_specs=[whole_in_vmem()] * 2 + [pl.BlockSpec(memory_space=pltpu.HBM)] * 2,
        out_shape=[
            jax.ShapeDtypeStruct((experts, block, features), bf16),
            jax.ShapeDtypeStruct((experts, block, features), bf16),
            jax.ShapeDtypeStruct((experts, block, hidden), bf16),
            jax.ShapeDtypeStruct((experts, block, hidden), bf16),
        ],
        scratch_shapes=[pltpu.VMEM((experts, block, hidden), bf16)] * 2 + [pltpu.SemaphoreType.DMA((2,))],
        compiler_params=params(GRANT),
        cost_estimate=cost(8 * experts * block * hidden * features, 4 * experts * hidden * features),
        name="experts_part",
    )(place, mine, other, w_in, w_out)


def weight_grads(place, mine, other, act, pre):
    experts, block, hidden = act.shape
    features = mine.shape[2]
    half = features // 2

    def kernel(place_ref, mine_ref, other_ref, act_ref, pre_ref, in_ref, out_ref):
        here, there = halves(place_ref, half)
        for cut, from_ref in ((here, mine_ref), (there, other_ref)):
            in_ref[0, :, cut] = lax.dot_general(
                pre_ref[0], from_ref[0, :, :half], rows_contract, preferred_element_type=f32
            ).astype(bf16)
            out_ref[0, :, cut] = lax.dot_general(
                act_ref[0], from_ref[0, :, half:], rows_contract, preferred_element_type=f32
            ).astype(bf16)

    return pl.pallas_call(
        kernel,
        grid=(experts,),
        in_specs=[
            in_smem(),
            pl.BlockSpec((1, block, features), lambda e: (e, 0, 0)),
            pl.BlockSpec((1, block, features), lambda e: (e, 0, 0)),
            pl.BlockSpec((1, block, hidden), lambda e: (e, 0, 0)),
            pl.BlockSpec((1, block, hidden), lambda e: (e, 0, 0)),
        ],
        out_specs=[pl.BlockSpec((1, hidden, features), lambda e: (e, 0, 0))] * 2,
        out_shape=[jax.ShapeDtypeStruct((experts, hidden, features), bf16)] * 2,
        compiler_params=params(GRANT),
        cost_estimate=cost(4 * experts * block * hidden * features, 4 * experts * hidden * features),
        name="weight_grads",
    )(place, mine, other, act, pre)


def sum_terms(terms, slot_in, column, copies):
    sources, block, features = terms.shape
    half = features // 2
    width = features + LANES

    def kernel(terms_ref, in_ref, column_ref, sent_ref):
        total = terms_ref[0].astype(f32)
        for source in range(1, sources):
            total = total + terms_ref[source].astype(f32)
        low = total.astype(bf16)
        inner = jnp.sum(in_ref[...] * low[:, half:].astype(f32), axis=1, keepdims=True)
        power, inverse = guarded(column_ref[:, 0:1])
        lanes = in_lanes(block, two_parts(inverse) + (power,) + two_parts(inner))
        for copy in range(copies):
            sent_ref[copy, :, :features] = low
            sent_ref[copy, :, features:] = lanes

    return pl.pallas_call(
        kernel,
        in_specs=[whole_in_vmem()] * 3,
        out_specs=whole_in_vmem(),
        out_shape=jax.ShapeDtypeStruct((copies, block, width), bf16),
        compiler_params=params(GRANT),
        name="sum_terms",
    )(terms, slot_in, column)


def all_exps(place, slot_keys, near_keys, far_keys, tokens, width, tile=256):
    features, block = slot_keys.shape
    count = tokens.shape[0]
    half = features // 2
    others = len(near_keys)
    slots = (others + 1) * block

    def kernel(place_ref, *refs):
        blocks_hbm = refs[: 2 * others + 1]
        tokens_ref, all_ref, own_ref, row_ref, column_ref, rows_ref = refs[2 * others + 1 : 2 * others + 7]
        turned_ref, found_ref, keys_ref, *block_refs = refs[2 * others + 7 : -1]
        sems = refs[-1]
        started = []
        for at, target in enumerate([keys_ref] + block_refs):
            started.append(pltpu.make_async_copy(blocks_hbm[at], target, sems.at[at]))
            started[at].start()
        near_refs, far_refs = block_refs[:others], block_refs[others:]
        for copy in started:
            copy.wait()
        core, at_own = place_ref[0], place_ref[1]
        here, there = halves(place_ref, half)

        def spot(at):
            return pl.ds(pl.multiple_of(at * block, block), block)

        own = spot(at_own)
        rows = pl.ds(pl.multiple_of(at_own * width, 16), width)
        turned_ref[own, :] = keys_ref[...].T
        for side in range(2):
            first = pl.multiple_of(at_own * width + side * half, 16)
            rows_ref[side, :, own] = keys_ref[pl.ds(first, width), :]
        for at in range(others):
            place_at = spot(at_own ^ (at + 1))
            turned_ref[place_at, here] = near_refs[at][...].T
            turned_ref[place_at, there] = far_refs[at][...].T
            rows_ref[core, :, place_at] = near_refs[at][rows, :]
            rows_ref[1 - core, :, place_at] = far_refs[at][rows, :]
        by_lane = jnp.zeros((block, LANES), f32)
        for at in range(0, count, tile):
            cut = slice(at, at + tile)
            found = jnp.exp(
                lax.dot_general(
                    turned_ref[...], tokens_ref[cut, :], cols_contract, preferred_element_type=f32
                )
            )
            found_ref[:, cut] = found
            all_ref[:, cut] = found.astype(bf16)
            row_ref[:, cut] = jnp.sum(found, axis=0, keepdims=True)
            exps = found_ref[own, cut]
            own_ref[:, cut] = exps
            for lanes in range(0, tile, LANES):
                by_lane = by_lane + exps[:, lanes : lanes + LANES]
        column_ref[...] = by_lane

    return pl.pallas_call(
        kernel,
        in_specs=[in_smem()]
        + [pl.BlockSpec(memory_space=pltpu.HBM)] * (2 * others + 1)
        + [whole_in_vmem()],
        out_specs=[whole_in_vmem()] * 5,
        out_shape=[
            jax.ShapeDtypeStruct((slots, count), bf16),
            jax.ShapeDtypeStruct((block, count), f32),
            jax.ShapeDtypeStruct((1, count), f32),
            jax.ShapeDtypeStruct((block, LANES), f32),
            jax.ShapeDtypeStruct((2, width, slots), bf16),
        ],
        scratch_shapes=[
            pltpu.VMEM((slots, features), bf16),
            pltpu.VMEM((slots, count), f32),
            pltpu.VMEM((features, block), bf16),
        ]
        + [pltpu.VMEM((half, block), bf16)] * (2 * others)
        + [pltpu.SemaphoreType.DMA((2 * others + 1,))],
        compiler_params=params(GRANT),
        cost_estimate=cost(2 * slots * features * count, 2 * features * count),
        name="all_exps",
    )(place, slot_keys, *near_keys, *far_keys, tokens)


def half_dot(place_ref, gathered_ref, ref, at, rows, own):
    blocks, block, _unused = gathered_ref.shape
    half = ref.shape[1] // 2
    here, there = halves(place_ref, half)
    return lax.dot_general(
        gathered_ref[:, :, at * half : (at + 1) * half].reshape(blocks * block, half),
        ref[rows, here if own else there],
        cols_contract,
        preferred_element_type=f32,
    )


def near_dots(place, out_grad, mine, slots, tile=256):
    count, features = out_grad.shape
    half = features // 2

    def kernel(place_ref, grad_ref, mine_ref, dot_ref, far_ref):
        _unused, there = halves(place_ref, half)
        far_ref[...] = grad_ref[:, there]
        for at in range(0, count, tile):
            cut = slice(at, at + tile)
            dot_ref[:, cut] = half_dot(place_ref, mine_ref, grad_ref, 0, cut, True)

    return pl.pallas_call(
        kernel,
        in_specs=[in_smem()] + [whole_in_vmem()] * 2,
        out_specs=[whole_in_vmem()] * 2,
        out_shape=[
            jax.ShapeDtypeStruct((slots, count), f32),
            jax.ShapeDtypeStruct((count, half), bf16),
        ],
        compiler_params=params(GRANT),
        cost_estimate=cost(slots * features * count, features * count),
        name="near_dots",
    )(place, out_grad, mine)


def comb_dots(exps, near, grad_far, row_parts, other, tile=256):
    slots, count = exps.shape
    half = grad_far.shape[1]

    def kernel(exp_ref, near_ref, grad_ref, row_ref, other_ref, dot_ref, sum_ref):
        slot_out = other_ref[:, :, :half].reshape(slots, half)
        for at in range(0, count, tile):
            cut = slice(at, at + tile)
            power, inverse = guarded(row_ref[:, cut])
            dots = near_ref[:, cut] + lax.dot_general(
                slot_out, grad_ref[cut, :], cols_contract, preferred_element_type=f32
            )
            dot_ref[:, cut] = dots
            terms = (exp_ref[:, cut].astype(f32) * power) * dots
            sum_ref[:, cut] = jnp.sum(terms, axis=0, keepdims=True) * inverse

    return pl.pallas_call(
        kernel,
        in_specs=[whole_in_vmem()] * 5,
        out_specs=[whole_in_vmem()] * 2,
        out_shape=[
            jax.ShapeDtypeStruct((slots, count), f32),
            jax.ShapeDtypeStruct((1, count), f32),
        ],
        compiler_params=params(GRANT),
        cost_estimate=cost(2 * slots * half * count, 2 * half * count),
        name="comb_dots",
    )(exps, near, grad_far, row_parts, other)


def disp_dots(place, exps, dots, tokens, row_parts, mine, other, width, tile=256):
    slots, count = exps.shape
    features = tokens.shape[1]
    half = features // 2

    def kernel(
        place_ref, exp_ref, dot_ref, tokens_ref, row_ref, mine_ref, other_ref,
        terms_ref, dispatch_ref, rows_ref, power_ref, inverse_ref, total_ref, turned_ref,
    ):
        lanes = mine_ref[:, :, features:].reshape(slots, LANES).astype(f32)
        apart = other_ref[:, :, features:].reshape(slots, LANES).astype(f32)
        inner = lanes[:, 3:4] + lanes[:, 4:5] + apart[:, 3:4] + apart[:, 4:5]
        power_ref[...] = jnp.broadcast_to(lanes[:, 2:3], (slots, tile))
        inverse_ref[...] = jnp.broadcast_to(lanes[:, 0:1] + lanes[:, 1:2], (slots, tile))
        total_ref[...] = jnp.broadcast_to(inner, (slots, tile))
        rows = pl.ds(pl.multiple_of(place_ref[1] * width, 16), width)
        for at, ref in enumerate((mine_ref, other_ref)):
            turned_ref[...] = ref[:, :, half:features].reshape(slots, half).T
            rows_ref[at] = turned_ref[rows, :]
        for at in range(0, count, tile):
            cut = slice(at, at + tile)
            power, inverse = guarded(row_ref[:, cut])
            exps_here = exp_ref[:, cut].astype(f32)
            dispatch = (exps_here * power_ref[...]) * inverse_ref[...]
            dispatch_ref[:, cut] = dispatch.astype(bf16)
            disp_dot = half_dot(place_ref, mine_ref, tokens_ref, 1, cut, True)
            disp_dot = disp_dot + half_dot(place_ref, other_ref, tokens_ref, 1, cut, False)
            combine = (exps_here * power) * inverse
            terms_ref[:, cut] = combine * dot_ref[:, cut] + dispatch * (disp_dot - total_ref[...])

    return pl.pallas_call(
        kernel,
        in_specs=[in_smem()] + [whole_in_vmem()] * 6,
        out_specs=[whole_in_vmem()] * 3,
        out_shape=[
            jax.ShapeDtypeStruct((slots, count), f32),
            jax.ShapeDtypeStruct((slots, count), bf16),
            jax.ShapeDtypeStruct((2, width, slots), bf16),
        ],
        scratch_shapes=[pltpu.VMEM((slots, tile), f32)] * 3 + [pltpu.VMEM((half, slots), bf16)],
        compiler_params=params(GRANT),
        cost_estimate=cost(2 * slots * features * count, 2 * features * count),
        name="disp_dots",
    )(place, exps, dots, tokens, row_parts, mine, other)


def columns_dot(place_ref, keys_rows_ref, grad_rows_ref, logit, dispatch, own):
    core, half_at = place_ref[0], place_ref[2]
    near = jnp.where(core == half_at, 0, 1)
    at_keys, at_grad = (half_at, near) if own else (1 - half_at, 1 - near)
    total = jnp.dot(keys_rows_ref[at_keys], logit, preferred_element_type=f32)
    return total + jnp.dot(grad_rows_ref[at_grad], dispatch, preferred_element_type=f32)


def logit_grads(place, exps, terms, dispatch, row_parts, row, row_other, keys_rows, grad_rows, tile=256):
    slots, count = exps.shape
    width = keys_rows.shape[1]

    def kernel(
        place_ref, exp_ref, terms_ref, dispatch_ref, row_ref, sum_ref, other_ref, keys_rows_ref, grad_rows_ref,
        logit_ref, sent_ref,
    ):
        for at in range(0, count, tile):
            cut = slice(at, at + tile)
            power, inverse = guarded(row_ref[:, cut])
            weight = (sum_ref[:, cut] + other_ref[:, cut]) * inverse
            exps_here = exp_ref[:, cut].astype(f32)
            logit_ref[:, cut] = (terms_ref[:, cut] - (exps_here * power) * weight).astype(bf16)
            sent_ref[:, cut] = columns_dot(
                place_ref, keys_rows_ref, grad_rows_ref, logit_ref[:, cut], dispatch_ref[:, cut], False
            ).astype(bf16)

    return pl.pallas_call(
        kernel,
        in_specs=[in_smem()] + [whole_in_vmem()] * 8,
        out_specs=[whole_in_vmem()] * 2,
        out_shape=[
            jax.ShapeDtypeStruct((slots, count), bf16),
            jax.ShapeDtypeStruct((width, count), bf16),
        ],
        compiler_params=params(GRANT),
        cost_estimate=cost(4 * slots * width * count, 4 * slots * count),
        name="logit_grads",
    )(place, exps, terms, dispatch, row_parts, row, row_other, keys_rows, grad_rows)


def own_parts(place, logit, dispatch, tokens, keys_rows, grad_rows, own_slots, tile=256):
    count, features = tokens.shape
    width = keys_rows.shape[1]

    def kernel(place_ref, logit_ref, dispatch_ref, tokens_ref, keys_rows_ref, grad_rows_ref, keys_ref, own_ref):
        own = pl.ds(pl.multiple_of(place_ref[1] * own_slots, own_slots), own_slots)
        total = jnp.dot(logit_ref[own, :], tokens_ref[...], preferred_element_type=f32)
        keys_ref[...] = total.T.astype(bf16)
        for at in range(0, count, tile):
            cut = slice(at, at + tile)
            own_ref[:, cut] = columns_dot(
                place_ref, keys_rows_ref, grad_rows_ref, logit_ref[:, cut], dispatch_ref[:, cut], True
            )

    return pl.pallas_call(
        kernel,
        in_specs=[in_smem()] + [whole_in_vmem()] * 5,
        out_specs=[whole_in_vmem()] * 2,
        out_shape=[
            jax.ShapeDtypeStruct((features, own_slots), bf16),
            jax.ShapeDtypeStruct((width, count), f32),
        ],
        compiler_params=params(GRANT),
        cost_estimate=cost(2 * own_slots * features * count, 2 * features * count),
        name="own_parts",
    )(place, logit, dispatch, tokens, keys_rows, grad_rows)


def per_device(tokens, slot_keys, w_in, w_out, out_grad):
    features = tokens.shape[1]
    own_slots = slot_keys.shape[1]
    slot_devices = lax.axis_size(SLOT)
    seq_devices = lax.axis_size(SEQ)
    groups = lax.axis_size(CHIPS)
    everyone = lax.axis_size(GATHERED)
    width = features // slot_devices
    swap = [(0, 1), (1, 0)]
    place = jnp.stack(
        [lax.axis_index("c"), lax.axis_index(KEYS), lax.axis_index("xa")]
    ).astype(jnp.int32)

    half = features // 2
    own_half = lax.dynamic_slice_in_dim(slot_keys, lax.axis_index("c") * half, half, 0)
    blocks = lax.axis_size(KEYS)
    near_keys = [
        lax.ppermute(own_half, KEYS, [(at, at ^ other) for at in range(blocks)])
        for other in range(1, blocks)
    ]
    far_keys = [lax.ppermute(keys, "c", swap) for keys in near_keys]
    all_exp, exps, row_sum, column, keys_rows = all_exps(
        place, slot_keys, near_keys, far_keys, tokens, width
    )
    column_other = lax.ppermute(column, "c", swap)
    row_sum_other = lax.ppermute(row_sum, "xa", swap)
    slot_in_part = dispatch_part(exps, column, column_other, tokens)
    keep, give, row_parts = combine_part(
        place, exps, row_sum, row_sum_other, column, column_other, slot_in_part, out_grad, groups
    )
    parts = lax.all_to_all(pair_sum(keep, lax.ppermute(give, "c", swap)), CHIPS, 0, 0)
    sent, slot_in, column_total = sum_slots(parts, groups)
    mine = lax.all_to_all(sent, CHIPS, 0, 0)
    other = lax.ppermute(mine, "c", swap)

    keep, give, act, pre = experts_part(place, mine, other, w_in, w_out)
    sent = pair_sum(keep, lax.ppermute(give, "c", swap))
    terms = lax.all_to_all(sent, CHIPS, 0, 0)
    terms, act, pre = lax.optimization_barrier((terms, act, pre))
    sent = sum_terms(terms, slot_in, column_total, everyone)
    gathered = lax.all_to_all(sent, GATHERED, 0, 0)
    grad_w_in, grad_w_out = weight_grads(place, mine, other, act, pre)
    gathered, grad_w_in, grad_w_out = lax.optimization_barrier((gathered, grad_w_in, grad_w_out))
    gathered_other = lax.ppermute(gathered, "c", swap)

    near, grad_far = near_dots(place, out_grad, gathered, all_exp.shape[0])
    gathered_other, near = lax.optimization_barrier((gathered_other, near))
    dots, row = comb_dots(all_exp, near, grad_far, row_parts, gathered_other)
    row_other = lax.ppermute(row, "xa", swap)
    terms, dispatch, grad_rows = disp_dots(
        place, all_exp, dots, tokens, row_parts, gathered, gathered_other, width
    )
    logit, sent = logit_grads(
        place, all_exp, terms, dispatch, row_parts, row, row_other, keys_rows, grad_rows
    )
    received = lax.ppermute(sent, "xa", swap)
    keys_part, own_grads = own_parts(
        place, logit, dispatch, tokens, keys_rows, grad_rows, own_slots
    )
    keys_parts = lax.all_to_all(
        keys_part.reshape(seq_devices, features // seq_devices, own_slots), SEQ, 0, 0
    )
    grad_tokens = (own_grads + received.astype(f32)).astype(bf16).T
    grad_keys = jnp.sum(keys_parts.astype(f32), axis=0)
    return (grad_tokens, grad_keys, grad_w_in, grad_w_out)


def solution(mesh):
    fine = Mesh(mesh.devices.reshape(2, 4, 2, 2, 2, 2), ("zl", "y", "c", "xa", "xb", "zh"))
    placed = (
        P(SEQ, None),
        P(None, SLOT),
        P(SLOT, SEQ, None),
        P(SLOT, SEQ, None),
        P(SEQ, None),
    )
    return jax.shard_map(
        per_device,
        mesh=fine,
        in_specs=placed,
        out_specs=(
            P(SEQ, SLOT),
            P(SEQ, SLOT),
            P(SLOT, SEQ, None),
            P(SLOT, SEQ, None),
        ),
        check_vma=False,
    )
```

```python
import jax
import jax.numpy as jnp
from jax import lax
from jax.experimental import pallas as pl
from jax.experimental.pallas import tpu as pltpu
from jax.sharding import Mesh, PartitionSpec as P

gelu_scale = 0.7978845608
gelu_cubic = 0.044715
rows_contract = (((0,), (0,)), ((), ()))
cols_contract = (((1,), (1,)), ((), ()))

SEQ = ("zl", "y", "c")
SLOT = ("xa", "xb", "zh")
KEYS = ("xb", "zh")
CHIPS = ("zl", "y")
GATHERED = ("xb", "zh", "zl", "y")
f32 = jnp.float32
bf16 = jnp.bfloat16
LANES = 128
MIB = 1 << 20
GRANT = 16
SCALE = 1


def gelu_tanh(values):
    return (
        0.5
        * values
        * (1.0 + jnp.tanh(gelu_scale * (values + gelu_cubic * values * values * values)))
    )


def gelu_slope(values):
    bent = jnp.tanh(gelu_scale * (values + gelu_cubic * values * values * values))
    return 0.5 * (1.0 + bent) + 0.5 * values * (1.0 - bent * bent) * gelu_scale * (
        1.0 + 3.0 * gelu_cubic * values * values
    )


def guarded(total):
    power = jnp.where(total > 2.0**64, 2.0**-32, jnp.where(total < 2.0**-64, 2.0**32, 1.0))
    return power, 1.0 / (total * power)


def two_parts(values):
    high = values.astype(bf16).astype(f32)
    return high, values - high


def in_lanes(rows, columns):
    lane = lax.broadcasted_iota(jnp.int32, (rows, LANES), 1)
    laid = jnp.zeros((rows, LANES), f32)
    for at, column in enumerate(columns):
        laid = jnp.where(lane == at, column, laid)
    return laid.astype(bf16)


def params(mib):
    return pltpu.CompilerParams(vmem_limit_bytes=mib * MIB)


def cost(flops, nbytes):
    return pl.CostEstimate(flops=SCALE * flops, bytes_accessed=nbytes, transcendentals=0)


def whole_in_vmem():
    return pl.BlockSpec(memory_space=pltpu.VMEM)


def in_smem():
    return pl.BlockSpec(memory_space=pltpu.SMEM)


def halves(place_ref, half):
    core = place_ref[0]
    here = pl.ds(pl.multiple_of(core * half, LANES), half)
    there = pl.ds(pl.multiple_of((1 - core) * half, LANES), half)
    return here, there


def dispatch_part(exps, column, column_other, tokens):
    slots, count = exps.shape
    features = tokens.shape[1]

    def kernel(exp_ref, column_ref, other_ref, tokens_ref, out_ref, weights_ref):
        total = jnp.sum(column_ref[...] + other_ref[...], axis=1, keepdims=True)
        power, inverse = guarded(jnp.where(total > 0, total, 1.0))
        weights_ref[...] = ((exp_ref[...] * power) * inverse).astype(bf16)
        out_ref[...] = jnp.dot(
            weights_ref[...], tokens_ref[...], preferred_element_type=f32
        ).astype(bf16)

    return pl.pallas_call(
        kernel,
        in_specs=[whole_in_vmem()] * 4,
        out_specs=whole_in_vmem(),
        out_shape=jax.ShapeDtypeStruct((slots, features), bf16),
        scratch_shapes=[pltpu.VMEM((slots, count), bf16)],
        compiler_params=params(GRANT),
        cost_estimate=cost(2 * slots * features * count, 2 * features * count),
        name="dispatch_part",
    )(exps, column, column_other, tokens)


def combine_part(place, exps, row, row_other, column, column_other, slot_in_part, out_grad, groups):
    slots, count = exps.shape
    features = out_grad.shape[1]
    half = features // 2
    block = slots // groups

    def kernel(
        place_ref, exp_ref, row_ref, row_other_ref, column_ref, other_ref, in_ref, grad_ref,
        keep_ref, give_ref, row_total_ref, weights_ref, total_ref,
    ):
        row_total_ref[...] = row_ref[...] + row_other_ref[...]
        power, inverse = guarded(row_total_ref[...])
        weights_ref[...] = ((exp_ref[...] * power) * inverse).astype(bf16)
        total = jnp.sum(column_ref[...] + other_ref[...], axis=1, keepdims=True)
        shift, _unused = guarded(total)
        high, low = two_parts(total * shift)
        lanes = in_lanes(slots, (high, low, 1.0 / shift))
        total_ref[...] = jnp.dot(
            weights_ref[...], grad_ref[...], preferred_element_type=f32
        ).astype(bf16)
        here, there = halves(place_ref, half)
        for group in range(groups):
            rows = slice(group * block, (group + 1) * block)
            keep_ref[group, :, :half] = in_ref[rows, here]
            keep_ref[group, :, half:features] = total_ref[rows, here]
            keep_ref[group, :, features:] = lanes[rows]
            give_ref[group, :, :half] = in_ref[rows, there]
            give_ref[group, :, half:] = total_ref[rows, there]

    return pl.pallas_call(
        kernel,
        in_specs=[in_smem()] + [whole_in_vmem()] * 7,
        out_specs=[whole_in_vmem()] * 3,
        out_shape=[
            jax.ShapeDtypeStruct((groups, block, features + LANES), bf16),
            jax.ShapeDtypeStruct((groups, block, features), bf16),
            jax.ShapeDtypeStruct((1, count), f32),
        ],
        scratch_shapes=[
            pltpu.VMEM((slots, count), bf16),
            pltpu.VMEM((slots, features), bf16),
        ],
        compiler_params=params(GRANT),
        cost_estimate=cost(2 * slots * features * count, 2 * features * count),
        name="combine_part",
    )(place, exps, row, row_other, column, column_other, slot_in_part, out_grad)


def pair_sum(keep, received):
    features = received.shape[2]

    def kernel(keep_ref, received_ref, out_ref):
        total = keep_ref[:, :, :features].astype(f32) + received_ref[...].astype(f32)
        out_ref[:, :, :features] = total.astype(bf16)
        if keep_ref.shape[2] > features:
            out_ref[:, :, features:] = keep_ref[:, :, features:]

    return pl.pallas_call(
        kernel,
        in_specs=[whole_in_vmem()] * 2,
        out_specs=whole_in_vmem(),
        out_shape=jax.ShapeDtypeStruct(keep.shape, bf16),
        compiler_params=params(GRANT),
        name="pair_sum",
    )(keep, received)


def sum_slots(parts, copies):
    sources, block, width = parts.shape
    features = width - LANES
    half = features // 2

    def kernel(parts_ref, sent_ref, in_ref, column_ref):
        lanes = parts_ref[:, :, features:].astype(f32)
        columns = (lanes[:, :, 0:1] + lanes[:, :, 1:2]) * lanes[:, :, 2:3]
        total = jnp.sum(columns, axis=0)
        power, inverse = guarded(total)
        share = (columns * power[None]) * inverse[None]
        slot_in = jnp.zeros((block, half), f32)
        slot_grad = jnp.zeros((block, half), f32)
        for source in range(sources):
            slot_in = slot_in + parts_ref[source, :, :half].astype(f32) * share[source]
            slot_grad = slot_grad + parts_ref[source, :, half:features].astype(f32)
        in_ref[...] = slot_in
        column_ref[...] = jnp.broadcast_to(total, (block, LANES))
        in_low = slot_in.astype(bf16)
        grad_low = slot_grad.astype(bf16)
        for copy in range(copies):
            sent_ref[copy, :, :half] = in_low
            sent_ref[copy, :, half:] = grad_low

    return pl.pallas_call(
        kernel,
        in_specs=[whole_in_vmem()],
        out_specs=[whole_in_vmem()] * 3,
        out_shape=[
            jax.ShapeDtypeStruct((copies, block, features), bf16),
            jax.ShapeDtypeStruct((block, half), f32),
            jax.ShapeDtypeStruct((block, LANES), f32),
        ],
        compiler_params=params(GRANT),
        name="sum_slots",
    )(parts)


def experts_part(place, mine, other, w_in, w_out):
    experts, hidden, features = w_in.shape
    block = mine.shape[1]
    half = features // 2

    def kernel(place_ref, mine_ref, other_ref, w_in_ref, w_out_ref, keep_ref, give_ref, act_hbm, pre_hbm, act_ref, pre_ref, whole_ref, out_ref, sems):
        here, there = halves(place_ref, half)

        def inward(at, weights_ref, e):
            cut = slice(at * half, (at + 1) * half)
            whole_ref[e, at, :, here] = mine_ref[e, :, cut]
            whole_ref[e, at, :, there] = other_ref[e, :, cut]
            return lax.dot_general(
                whole_ref[e, at], weights_ref[e], cols_contract, preferred_element_type=f32
            )

        for e in range(experts):
            hidden_pre = inward(0, w_in_ref, e)
            act_grad = inward(1, w_out_ref, e)
            act = gelu_tanh(hidden_pre).astype(bf16)
            pre = (act_grad * gelu_slope(hidden_pre)).astype(bf16)
            out_ref[e, 0] = jnp.dot(act, w_out_ref[e], preferred_element_type=f32).astype(bf16)
            out_ref[e, 1] = jnp.dot(pre, w_in_ref[e], preferred_element_type=f32).astype(bf16)
            for cut, sent_ref in ((here, keep_ref), (there, give_ref)):
                sent_ref[e, :, :half] = out_ref[e, 0, :, cut]
                sent_ref[e, :, half:] = out_ref[e, 1, :, cut]
            act_ref[e] = act
            pre_ref[e] = pre
        first = pltpu.make_async_copy(act_ref, act_hbm, sems.at[0])
        second = pltpu.make_async_copy(pre_ref, pre_hbm, sems.at[1])
        first.start()
        second.start()
        first.wait()
        second.wait()

    return pl.pallas_call(
        kernel,
        in_specs=[in_smem()] + [whole_in_vmem()] * 4,
        out_specs=[whole_in_vmem()] * 2 + [pl.BlockSpec(memory_space=pltpu.HBM)] * 2,
        out_shape=[
            jax.ShapeDtypeStruct((experts, block, features), bf16),
            jax.ShapeDtypeStruct((experts, block, features), bf16),
            jax.ShapeDtypeStruct((experts, block, hidden), bf16),
            jax.ShapeDtypeStruct((experts, block, hidden), bf16),
        ],
        scratch_shapes=[pltpu.VMEM((experts, block, hidden), bf16)] * 2
        + [pltpu.VMEM((experts, 2, block, features), bf16)] * 2
        + [pltpu.SemaphoreType.DMA((2,))],
        compiler_params=params(GRANT),
        cost_estimate=cost(8 * experts * block * hidden * features, 4 * experts * hidden * features),
        name="experts_part",
    )(place, mine, other, w_in, w_out)


def weight_grads(place, mine, other, act, pre):
    experts, block, hidden = act.shape
    features = mine.shape[2]
    half = features // 2

    def kernel(place_ref, mine_ref, other_ref, act_ref, pre_ref, in_ref, out_ref):
        here, there = halves(place_ref, half)
        for cut, from_ref in ((here, mine_ref), (there, other_ref)):
            in_ref[0, :, cut] = lax.dot_general(
                pre_ref[0], from_ref[0, :, :half], rows_contract, preferred_element_type=f32
            ).astype(bf16)
            out_ref[0, :, cut] = lax.dot_general(
                act_ref[0], from_ref[0, :, half:], rows_contract, preferred_element_type=f32
            ).astype(bf16)

    return pl.pallas_call(
        kernel,
        grid=(experts,),
        in_specs=[
            in_smem(),
            pl.BlockSpec((1, block, features), lambda e: (e, 0, 0)),
            pl.BlockSpec((1, block, features), lambda e: (e, 0, 0)),
            pl.BlockSpec((1, block, hidden), lambda e: (e, 0, 0)),
            pl.BlockSpec((1, block, hidden), lambda e: (e, 0, 0)),
        ],
        out_specs=[pl.BlockSpec((1, hidden, features), lambda e: (e, 0, 0))] * 2,
        out_shape=[jax.ShapeDtypeStruct((experts, hidden, features), bf16)] * 2,
        compiler_params=params(GRANT),
        cost_estimate=cost(4 * experts * block * hidden * features, 4 * experts * hidden * features),
        name="weight_grads",
    )(place, mine, other, act, pre)


def sum_terms(terms, slot_in, column, copies):
    sources, block, features = terms.shape
    half = features // 2
    width = features + LANES

    def kernel(terms_ref, in_ref, column_ref, sent_ref):
        total = terms_ref[0].astype(f32)
        for source in range(1, sources):
            total = total + terms_ref[source].astype(f32)
        low = total.astype(bf16)
        inner = jnp.sum(in_ref[...] * low[:, half:].astype(f32), axis=1, keepdims=True)
        power, inverse = guarded(column_ref[:, 0:1])
        lanes = in_lanes(block, two_parts(inverse) + (power,) + two_parts(inner))
        for copy in range(copies):
            sent_ref[copy, :, :features] = low
            sent_ref[copy, :, features:] = lanes

    return pl.pallas_call(
        kernel,
        in_specs=[whole_in_vmem()] * 3,
        out_specs=whole_in_vmem(),
        out_shape=jax.ShapeDtypeStruct((copies, block, width), bf16),
        compiler_params=params(GRANT),
        name="sum_terms",
    )(terms, slot_in, column)


def all_exps(place, slot_keys, near_keys, far_keys, tokens, width, tile=256):
    features, block = slot_keys.shape
    count = tokens.shape[0]
    half = features // 2
    others = len(near_keys)
    slots = (others + 1) * block

    def kernel(place_ref, keys_ref, *refs):
        near_refs, far_refs = refs[:others], refs[others : 2 * others]
        (
            tokens_ref, all_ref, own_ref, row_ref, column_ref, rows_ref, turned_ref, found_ref
        ) = refs[2 * others :]
        core, at_own = place_ref[0], place_ref[1]
        here, there = halves(place_ref, half)

        def spot(at):
            return pl.ds(pl.multiple_of(at * block, block), block)

        own = spot(at_own)
        rows = pl.ds(pl.multiple_of(at_own * width, 16), width)
        turned_ref[own, :] = keys_ref[...].T
        for side in range(2):
            first = pl.multiple_of(at_own * width + side * half, 16)
            rows_ref[side, :, own] = keys_ref[pl.ds(first, width), :]
        for at in range(others):
            place_at = spot(at_own ^ (at + 1))
            turned_ref[place_at, here] = near_refs[at][...].T
            turned_ref[place_at, there] = far_refs[at][...].T
            rows_ref[core, :, place_at] = near_refs[at][rows, :]
            rows_ref[1 - core, :, place_at] = far_refs[at][rows, :]
        by_lane = jnp.zeros((block, LANES), f32)
        for at in range(0, count, tile):
            cut = slice(at, at + tile)
            found = jnp.exp(
                lax.dot_general(
                    turned_ref[...], tokens_ref[cut, :], cols_contract, preferred_element_type=f32
                )
            )
            found_ref[:, cut] = found
            all_ref[:, cut] = found.astype(bf16)
            row_ref[:, cut] = jnp.sum(found, axis=0, keepdims=True)
            exps = found_ref[own, cut]
            own_ref[:, cut] = exps
            for lanes in range(0, tile, LANES):
                by_lane = by_lane + exps[:, lanes : lanes + LANES]
        column_ref[...] = by_lane

    return pl.pallas_call(
        kernel,
        in_specs=[in_smem()] + [whole_in_vmem()] * (2 * others + 2),
        out_specs=[whole_in_vmem()] * 5,
        out_shape=[
            jax.ShapeDtypeStruct((slots, count), bf16),
            jax.ShapeDtypeStruct((block, count), f32),
            jax.ShapeDtypeStruct((1, count), f32),
            jax.ShapeDtypeStruct((block, LANES), f32),
            jax.ShapeDtypeStruct((2, width, slots), bf16),
        ],
        scratch_shapes=[
            pltpu.VMEM((slots, features), bf16),
            pltpu.VMEM((slots, count), f32),
        ],
        compiler_params=params(GRANT),
        cost_estimate=cost(2 * slots * features * count, 2 * features * count),
        name="all_exps",
    )(place, slot_keys, *near_keys, *far_keys, tokens)


def half_dot(place_ref, gathered_ref, ref, at, rows, own):
    blocks, block, _unused = gathered_ref.shape
    half = ref.shape[1] // 2
    here, there = halves(place_ref, half)
    return lax.dot_general(
        gathered_ref[:, :, at * half : (at + 1) * half].reshape(blocks * block, half),
        ref[rows, here if own else there],
        cols_contract,
        preferred_element_type=f32,
    )


def near_dots(place, out_grad, mine, slots, tile=256):
    count, features = out_grad.shape
    half = features // 2

    def kernel(place_ref, grad_ref, mine_ref, dot_ref, far_ref):
        _unused, there = halves(place_ref, half)
        far_ref[...] = grad_ref[:, there]
        for at in range(0, count, tile):
            cut = slice(at, at + tile)
            dot_ref[:, cut] = half_dot(place_ref, mine_ref, grad_ref, 0, cut, True)

    return pl.pallas_call(
        kernel,
        in_specs=[in_smem()] + [whole_in_vmem()] * 2,
        out_specs=[whole_in_vmem()] * 2,
        out_shape=[
            jax.ShapeDtypeStruct((slots, count), f32),
            jax.ShapeDtypeStruct((count, half), bf16),
        ],
        compiler_params=params(GRANT),
        cost_estimate=cost(slots * features * count, features * count),
        name="near_dots",
    )(place, out_grad, mine)


def comb_dots(exps, near, grad_far, row_parts, other, tile=256):
    slots, count = exps.shape
    half = grad_far.shape[1]

    def kernel(exp_ref, near_ref, grad_ref, row_ref, other_ref, dot_ref, sum_ref):
        slot_out = other_ref[:, :, :half].reshape(slots, half)
        for at in range(0, count, tile):
            cut = slice(at, at + tile)
            power, inverse = guarded(row_ref[:, cut])
            dots = near_ref[:, cut] + lax.dot_general(
                slot_out, grad_ref[cut, :], cols_contract, preferred_element_type=f32
            )
            dot_ref[:, cut] = dots
            terms = (exp_ref[:, cut].astype(f32) * power) * dots
            sum_ref[:, cut] = jnp.sum(terms, axis=0, keepdims=True) * inverse

    return pl.pallas_call(
        kernel,
        in_specs=[whole_in_vmem()] * 5,
        out_specs=[whole_in_vmem()] * 2,
        out_shape=[
            jax.ShapeDtypeStruct((slots, count), f32),
            jax.ShapeDtypeStruct((1, count), f32),
        ],
        compiler_params=params(GRANT),
        cost_estimate=cost(2 * slots * half * count, 2 * half * count),
        name="comb_dots",
    )(exps, near, grad_far, row_parts, other)


def disp_dots(place, exps, dots, tokens, row_parts, mine, other, width, tile=256):
    slots, count = exps.shape
    features = tokens.shape[1]
    half = features // 2

    def kernel(
        place_ref, exp_ref, dot_ref, tokens_ref, row_ref, mine_ref, other_ref,
        terms_ref, dispatch_ref, rows_ref, power_ref, inverse_ref, total_ref, turned_ref,
    ):
        lanes = mine_ref[:, :, features:].reshape(slots, LANES).astype(f32)
        apart = other_ref[:, :, features:].reshape(slots, LANES).astype(f32)
        inner = lanes[:, 3:4] + lanes[:, 4:5] + apart[:, 3:4] + apart[:, 4:5]
        power_ref[...] = jnp.broadcast_to(lanes[:, 2:3], (slots, tile))
        inverse_ref[...] = jnp.broadcast_to(lanes[:, 0:1] + lanes[:, 1:2], (slots, tile))
        total_ref[...] = jnp.broadcast_to(inner, (slots, tile))
        rows = pl.ds(pl.multiple_of(place_ref[1] * width, 16), width)
        for at, ref in enumerate((mine_ref, other_ref)):
            turned_ref[...] = ref[:, :, half:features].reshape(slots, half).T
            rows_ref[at] = turned_ref[rows, :]
        for at in range(0, count, tile):
            cut = slice(at, at + tile)
            power, inverse = guarded(row_ref[:, cut])
            exps_here = exp_ref[:, cut].astype(f32)
            dispatch = (exps_here * power_ref[...]) * inverse_ref[...]
            dispatch_ref[:, cut] = dispatch.astype(bf16)
            disp_dot = half_dot(place_ref, mine_ref, tokens_ref, 1, cut, True)
            disp_dot = disp_dot + half_dot(place_ref, other_ref, tokens_ref, 1, cut, False)
            combine = (exps_here * power) * inverse
            terms_ref[:, cut] = combine * dot_ref[:, cut] + dispatch * (disp_dot - total_ref[...])

    return pl.pallas_call(
        kernel,
        in_specs=[in_smem()] + [whole_in_vmem()] * 6,
        out_specs=[whole_in_vmem()] * 3,
        out_shape=[
            jax.ShapeDtypeStruct((slots, count), f32),
            jax.ShapeDtypeStruct((slots, count), bf16),
            jax.ShapeDtypeStruct((2, width, slots), bf16),
        ],
        scratch_shapes=[pltpu.VMEM((slots, tile), f32)] * 3 + [pltpu.VMEM((half, slots), bf16)],
        compiler_params=params(GRANT),
        cost_estimate=cost(2 * slots * features * count, 2 * features * count),
        name="disp_dots",
    )(place, exps, dots, tokens, row_parts, mine, other)


def columns_dot(place_ref, keys_rows_ref, grad_rows_ref, logit, dispatch, own):
    core, half_at = place_ref[0], place_ref[2]
    near = jnp.where(core == half_at, 0, 1)
    at_keys, at_grad = (half_at, near) if own else (1 - half_at, 1 - near)
    total = jnp.dot(keys_rows_ref[at_keys], logit, preferred_element_type=f32)
    return total + jnp.dot(grad_rows_ref[at_grad], dispatch, preferred_element_type=f32)


def logit_grads(place, exps, terms, dispatch, row_parts, row, row_other, keys_rows, grad_rows, tile=256):
    slots, count = exps.shape
    width = keys_rows.shape[1]

    def kernel(
        place_ref, exp_ref, terms_ref, dispatch_ref, row_ref, sum_ref, other_ref, keys_rows_ref, grad_rows_ref,
        logit_ref, sent_ref,
    ):
        for at in range(0, count, tile):
            cut = slice(at, at + tile)
            power, inverse = guarded(row_ref[:, cut])
            weight = (sum_ref[:, cut] + other_ref[:, cut]) * inverse
            exps_here = exp_ref[:, cut].astype(f32)
            logit_ref[:, cut] = (terms_ref[:, cut] - (exps_here * power) * weight).astype(bf16)
            sent_ref[:, cut] = columns_dot(
                place_ref, keys_rows_ref, grad_rows_ref, logit_ref[:, cut], dispatch_ref[:, cut], False
            ).astype(bf16)

    return pl.pallas_call(
        kernel,
        in_specs=[in_smem()] + [whole_in_vmem()] * 8,
        out_specs=[whole_in_vmem()] * 2,
        out_shape=[
            jax.ShapeDtypeStruct((slots, count), bf16),
            jax.ShapeDtypeStruct((width, count), bf16),
        ],
        compiler_params=params(GRANT),
        cost_estimate=cost(4 * slots * width * count, 4 * slots * count),
        name="logit_grads",
    )(place, exps, terms, dispatch, row_parts, row, row_other, keys_rows, grad_rows)


def own_parts(place, logit, dispatch, tokens, keys_rows, grad_rows, own_slots, chips, tile=256):
    count, features = tokens.shape
    width = keys_rows.shape[1]
    rows = features // (2 * chips)

    def kernel(place_ref, logit_ref, dispatch_ref, tokens_ref, keys_rows_ref, grad_rows_ref, keep_ref, give_ref, own_ref, keys_ref):
        own = pl.ds(pl.multiple_of(place_ref[1] * own_slots, own_slots), own_slots)
        total = jnp.dot(logit_ref[own, :], tokens_ref[...], preferred_element_type=f32)
        keys_ref[...] = total.T.astype(bf16)
        for chip in range(chips):
            for core, out_ref in ((place_ref[0], keep_ref), (1 - place_ref[0], give_ref)):
                first = pl.multiple_of(chip * 2 * rows + core * rows, 16)
                out_ref[chip] = keys_ref[pl.ds(first, rows), :]
        for at in range(0, count, tile):
            cut = slice(at, at + tile)
            own_ref[:, cut] = columns_dot(
                place_ref, keys_rows_ref, grad_rows_ref, logit_ref[:, cut], dispatch_ref[:, cut], True
            )

    return pl.pallas_call(
        kernel,
        in_specs=[in_smem()] + [whole_in_vmem()] * 5,
        out_specs=[whole_in_vmem()] * 3,
        out_shape=[
            jax.ShapeDtypeStruct((chips, rows, own_slots), bf16),
            jax.ShapeDtypeStruct((chips, rows, own_slots), bf16),
            jax.ShapeDtypeStruct((width, count), f32),
        ],
        scratch_shapes=[pltpu.VMEM((features, own_slots), bf16)],
        compiler_params=params(GRANT),
        cost_estimate=cost(2 * own_slots * features * count, 2 * features * count),
        name="own_parts",
    )(place, logit, dispatch, tokens, keys_rows, grad_rows)


def per_device(tokens, slot_keys, w_in, w_out, out_grad):
    features = tokens.shape[1]
    own_slots = slot_keys.shape[1]
    slot_devices = lax.axis_size(SLOT)
    groups = lax.axis_size(CHIPS)
    everyone = lax.axis_size(GATHERED)
    width = features // slot_devices
    swap = [(0, 1), (1, 0)]
    place = jnp.stack(
        [lax.axis_index("c"), lax.axis_index(KEYS), lax.axis_index("xa")]
    ).astype(jnp.int32)

    half = features // 2
    own_half = lax.dynamic_slice_in_dim(slot_keys, lax.axis_index("c") * half, half, 0)
    blocks = lax.axis_size(KEYS)
    near_keys = [
        lax.ppermute(own_half, KEYS, [(at, at ^ other) for at in range(blocks)])
        for other in range(1, blocks)
    ]
    far_keys = [lax.ppermute(keys, "c", swap) for keys in near_keys]
    all_exp, exps, row_sum, column, keys_rows = all_exps(
        place, slot_keys, near_keys, far_keys, tokens, width
    )
    column_other = lax.ppermute(column, "c", swap)
    row_sum_other = lax.ppermute(row_sum, "xa", swap)
    slot_in_part = dispatch_part(exps, column, column_other, tokens)
    keep, give, row_parts = combine_part(
        place, exps, row_sum, row_sum_other, column, column_other, slot_in_part, out_grad, groups
    )
    parts = lax.all_to_all(pair_sum(keep, lax.ppermute(give, "c", swap)), CHIPS, 0, 0)
    sent, slot_in, column_total = sum_slots(parts, groups)
    mine = lax.all_to_all(sent, CHIPS, 0, 0)
    other = lax.ppermute(mine, "c", swap)

    keep, give, act, pre = experts_part(place, mine, other, w_in, w_out)
    sent = pair_sum(keep, lax.ppermute(give, "c", swap))
    terms = lax.all_to_all(sent, CHIPS, 0, 0)
    terms, act, pre = lax.optimization_barrier((terms, act, pre))
    sent = sum_terms(terms, slot_in, column_total, everyone)
    gathered = lax.all_to_all(sent, GATHERED, 0, 0)
    grad_w_in, grad_w_out = weight_grads(place, mine, other, act, pre)
    gathered, grad_w_in, grad_w_out = lax.optimization_barrier((gathered, grad_w_in, grad_w_out))
    gathered_other = lax.ppermute(gathered, "c", swap)

    near, grad_far = near_dots(place, out_grad, gathered, all_exp.shape[0])
    gathered_other, near = lax.optimization_barrier((gathered_other, near))
    dots, row = comb_dots(all_exp, near, grad_far, row_parts, gathered_other)
    row_other = lax.ppermute(row, "xa", swap)
    terms, dispatch, grad_rows = disp_dots(
        place, all_exp, dots, tokens, row_parts, gathered, gathered_other, width
    )
    logit, sent = logit_grads(
        place, all_exp, terms, dispatch, row_parts, row, row_other, keys_rows, grad_rows
    )
    received = lax.ppermute(sent, "xa", swap)
    keep, give, own_grads = own_parts(
        place, logit, dispatch, tokens, keys_rows, grad_rows, own_slots, groups
    )
    keys_parts = lax.all_to_all(
        pair_sum(keep, lax.ppermute(give, "c", swap)), CHIPS, 0, 0
    )
    grad_tokens = (own_grads + received.astype(f32)).astype(bf16).T
    grad_keys = jnp.sum(keys_parts.astype(f32), axis=0)
    return (grad_tokens, grad_keys, grad_w_in, grad_w_out)


def solution(mesh):
    fine = Mesh(mesh.devices.reshape(2, 4, 2, 2, 2, 2), ("zl", "y", "c", "xa", "xb", "zh"))
    placed = (
        P(SEQ, None),
        P(None, SLOT),
        P(SLOT, SEQ, None),
        P(SLOT, SEQ, None),
        P(SEQ, None),
    )
    return jax.shard_map(
        per_device,
        mesh=fine,
        in_specs=placed,
        out_specs=(
            P(SEQ, SLOT),
            P(SEQ, SLOT),
            P(SLOT, SEQ, None),
            P(SLOT, SEQ, None),
        ),
        check_vma=False,
    )
```

```python
import jax
import jax.numpy as jnp
from jax import lax
from jax.experimental import pallas as pl
from jax.experimental.pallas import tpu as pltpu
from jax.sharding import Mesh, PartitionSpec as P

gelu_scale = 0.7978845608
gelu_cubic = 0.044715
rows_contract = (((0,), (0,)), ((), ()))
cols_contract = (((1,), (1,)), ((), ()))

SEQ = ("zl", "y", "c")
SLOT = ("xb", "xa", "zh")
KEYS = ("xb", "zh")
CHIPS = ("zl", "y")
GATHERED = ("xb", "xa", "zh", "zl", "y")
f32 = jnp.float32
bf16 = jnp.bfloat16
LANES = 128
MIB = 1 << 20
GRANT = 16
SCALE = 1


def gelu_tanh(values):
    return (
        0.5
        * values
        * (1.0 + jnp.tanh(gelu_scale * (values + gelu_cubic * values * values * values)))
    )


def gelu_slope(values):
    bent = jnp.tanh(gelu_scale * (values + gelu_cubic * values * values * values))
    return 0.5 * (1.0 + bent) + 0.5 * values * (1.0 - bent * bent) * gelu_scale * (
        1.0 + 3.0 * gelu_cubic * values * values
    )


def guarded(total):
    power = jnp.where(total > 2.0**64, 2.0**-32, jnp.where(total < 2.0**-64, 2.0**32, 1.0))
    return power, 1.0 / (total * power)


def two_parts(values):
    high = values.astype(bf16).astype(f32)
    return high, values - high


def in_lanes(rows, columns):
    lane = lax.broadcasted_iota(jnp.int32, (rows, LANES), 1)
    laid = jnp.zeros((rows, LANES), f32)
    for at, column in enumerate(columns):
        laid = jnp.where(lane == at, column, laid)
    return laid.astype(bf16)


def params(mib):
    return pltpu.CompilerParams(vmem_limit_bytes=mib * MIB)


def cost(flops, nbytes):
    return pl.CostEstimate(flops=SCALE * flops, bytes_accessed=nbytes, transcendentals=0)


def whole_in_vmem():
    return pl.BlockSpec(memory_space=pltpu.VMEM)


def in_smem():
    return pl.BlockSpec(memory_space=pltpu.SMEM)


def halves(place_ref, half):
    core = place_ref[0]
    here = pl.ds(pl.multiple_of(core * half, LANES), half)
    there = pl.ds(pl.multiple_of((1 - core) * half, LANES), half)
    return here, there


def dispatch_part(exps, column, column_other, tokens):
    slots, count = exps.shape
    features = tokens.shape[1]

    def kernel(exp_ref, column_ref, other_ref, tokens_ref, out_ref, weights_ref):
        total = jnp.sum(column_ref[...] + other_ref[...], axis=1, keepdims=True)
        power, inverse = guarded(jnp.where(total > 0, total, 1.0))
        weights_ref[...] = ((exp_ref[...] * power) * inverse).astype(bf16)
        out_ref[...] = jnp.dot(
            weights_ref[...], tokens_ref[...], preferred_element_type=f32
        ).astype(bf16)

    return pl.pallas_call(
        kernel,
        in_specs=[whole_in_vmem()] * 4,
        out_specs=whole_in_vmem(),
        out_shape=jax.ShapeDtypeStruct((slots, features), bf16),
        scratch_shapes=[pltpu.VMEM((slots, count), bf16)],
        compiler_params=params(GRANT),
        cost_estimate=cost(2 * slots * features * count, 2 * features * count),
        name="dispatch_part",
    )(exps, column, column_other, tokens)


def combine_part(place, exps, row, row_other, column, column_other, slot_in_part, out_grad, groups):
    slots, count = exps.shape
    features = out_grad.shape[1]
    half = features // 2
    block = slots // groups

    def kernel(
        place_ref, exp_ref, row_ref, row_other_ref, column_ref, other_ref, in_ref, grad_ref,
        keep_ref, give_ref, row_total_ref, weights_ref, total_ref,
    ):
        row_total_ref[...] = row_ref[...] + row_other_ref[...]
        power, inverse = guarded(row_total_ref[...])
        weights_ref[...] = ((exp_ref[...] * power) * inverse).astype(bf16)
        total = jnp.sum(column_ref[...] + other_ref[...], axis=1, keepdims=True)
        shift, _unused = guarded(total)
        high, low = two_parts(total * shift)
        lanes = in_lanes(slots, (high, low, 1.0 / shift))
        total_ref[...] = jnp.dot(
            weights_ref[...], grad_ref[...], preferred_element_type=f32
        ).astype(bf16)
        here, there = halves(place_ref, half)
        for group in range(groups):
            rows = slice(group * block, (group + 1) * block)
            keep_ref[group, :, :half] = in_ref[rows, here]
            keep_ref[group, :, half:features] = total_ref[rows, here]
            keep_ref[group, :, features:] = lanes[rows]
            give_ref[group, :, :half] = in_ref[rows, there]
            give_ref[group, :, half:] = total_ref[rows, there]

    return pl.pallas_call(
        kernel,
        in_specs=[in_smem()] + [whole_in_vmem()] * 7,
        out_specs=[whole_in_vmem()] * 3,
        out_shape=[
            jax.ShapeDtypeStruct((groups, block, features + LANES), bf16),
            jax.ShapeDtypeStruct((groups, block, features), bf16),
            jax.ShapeDtypeStruct((1, count), f32),
        ],
        scratch_shapes=[
            pltpu.VMEM((slots, count), bf16),
            pltpu.VMEM((slots, features), bf16),
        ],
        compiler_params=params(GRANT),
        cost_estimate=cost(2 * slots * features * count, 2 * features * count),
        name="combine_part",
    )(place, exps, row, row_other, column, column_other, slot_in_part, out_grad)


def pair_sum(keep, received):
    features = received.shape[2]

    def kernel(keep_ref, received_ref, out_ref):
        total = keep_ref[:, :, :features].astype(f32) + received_ref[...].astype(f32)
        out_ref[:, :, :features] = total.astype(bf16)
        if keep_ref.shape[2] > features:
            out_ref[:, :, features:] = keep_ref[:, :, features:]

    return pl.pallas_call(
        kernel,
        in_specs=[whole_in_vmem()] * 2,
        out_specs=whole_in_vmem(),
        out_shape=jax.ShapeDtypeStruct(keep.shape, bf16),
        compiler_params=params(GRANT),
        name="pair_sum",
    )(keep, received)


def sum_slots(parts, copies):
    sources, block, width = parts.shape
    features = width - LANES
    half = features // 2

    def kernel(parts_ref, sent_ref, in_ref, column_ref):
        lanes = parts_ref[:, :, features:].astype(f32)
        columns = (lanes[:, :, 0:1] + lanes[:, :, 1:2]) * lanes[:, :, 2:3]
        total = jnp.sum(columns, axis=0)
        power, inverse = guarded(total)
        share = (columns * power[None]) * inverse[None]
        slot_in = jnp.zeros((block, half), f32)
        slot_grad = jnp.zeros((block, half), f32)
        for source in range(sources):
            slot_in = slot_in + parts_ref[source, :, :half].astype(f32) * share[source]
            slot_grad = slot_grad + parts_ref[source, :, half:features].astype(f32)
        in_ref[...] = slot_in
        column_ref[...] = jnp.broadcast_to(total, (block, LANES))
        in_low = slot_in.astype(bf16)
        grad_low = slot_grad.astype(bf16)
        for copy in range(copies):
            sent_ref[copy, :, :half] = in_low
            sent_ref[copy, :, half:] = grad_low

    return pl.pallas_call(
        kernel,
        in_specs=[whole_in_vmem()],
        out_specs=[whole_in_vmem()] * 3,
        out_shape=[
            jax.ShapeDtypeStruct((copies, block, features), bf16),
            jax.ShapeDtypeStruct((block, half), f32),
            jax.ShapeDtypeStruct((block, LANES), f32),
        ],
        compiler_params=params(GRANT),
        name="sum_slots",
    )(parts)


def experts_part(place, mine, other, w_in, w_out):
    experts, hidden, features = w_in.shape
    block = mine.shape[1]
    half = features // 2

    def kernel(place_ref, mine_ref, other_ref, w_in_ref, w_out_ref, keep_ref, give_ref, act_hbm, pre_hbm, act_ref, pre_ref, whole_ref, out_ref, sems):
        here, there = halves(place_ref, half)

        def inward(at, weights_ref, e):
            cut = slice(at * half, (at + 1) * half)
            whole_ref[e, at, :, here] = mine_ref[e, :, cut]
            whole_ref[e, at, :, there] = other_ref[e, :, cut]
            return lax.dot_general(
                whole_ref[e, at], weights_ref[e], cols_contract, preferred_element_type=f32
            )

        for e in range(experts):
            hidden_pre = inward(0, w_in_ref, e)
            act_grad = inward(1, w_out_ref, e)
            act = gelu_tanh(hidden_pre).astype(bf16)
            pre = (act_grad * gelu_slope(hidden_pre)).astype(bf16)
            out_ref[e, 0] = jnp.dot(act, w_out_ref[e], preferred_element_type=f32).astype(bf16)
            out_ref[e, 1] = jnp.dot(pre, w_in_ref[e], preferred_element_type=f32).astype(bf16)
            for cut, sent_ref in ((here, keep_ref), (there, give_ref)):
                sent_ref[e, :, :half] = out_ref[e, 0, :, cut]
                sent_ref[e, :, half:] = out_ref[e, 1, :, cut]
            act_ref[e] = act
            pre_ref[e] = pre
        first = pltpu.make_async_copy(act_ref, act_hbm, sems.at[0])
        second = pltpu.make_async_copy(pre_ref, pre_hbm, sems.at[1])
        first.start()
        second.start()
        first.wait()
        second.wait()

    return pl.pallas_call(
        kernel,
        in_specs=[in_smem()] + [whole_in_vmem()] * 4,
        out_specs=[whole_in_vmem()] * 2 + [pl.BlockSpec(memory_space=pltpu.HBM)] * 2,
        out_shape=[
            jax.ShapeDtypeStruct((experts, block, features), bf16),
            jax.ShapeDtypeStruct((experts, block, features), bf16),
            jax.ShapeDtypeStruct((experts, block, hidden), bf16),
            jax.ShapeDtypeStruct((experts, block, hidden), bf16),
        ],
        scratch_shapes=[pltpu.VMEM((experts, block, hidden), bf16)] * 2
        + [pltpu.VMEM((experts, 2, block, features), bf16)] * 2
        + [pltpu.SemaphoreType.DMA((2,))],
        compiler_params=params(GRANT),
        cost_estimate=cost(8 * experts * block * hidden * features, 4 * experts * hidden * features),
        name="experts_part",
    )(place, mine, other, w_in, w_out)


def weight_grads(place, mine, other, act, pre):
    experts, block, hidden = act.shape
    features = mine.shape[2]
    half = features // 2

    def kernel(place_ref, mine_ref, other_ref, act_ref, pre_ref, in_ref, out_ref):
        here, there = halves(place_ref, half)
        for cut, from_ref in ((here, mine_ref), (there, other_ref)):
            in_ref[0, :, cut] = lax.dot_general(
                pre_ref[0], from_ref[0, :, :half], rows_contract, preferred_element_type=f32
            ).astype(bf16)
            out_ref[0, :, cut] = lax.dot_general(
                act_ref[0], from_ref[0, :, half:], rows_contract, preferred_element_type=f32
            ).astype(bf16)

    return pl.pallas_call(
        kernel,
        grid=(experts,),
        in_specs=[
            in_smem(),
            pl.BlockSpec((1, block, features), lambda e: (e, 0, 0)),
            pl.BlockSpec((1, block, features), lambda e: (e, 0, 0)),
            pl.BlockSpec((1, block, hidden), lambda e: (e, 0, 0)),
            pl.BlockSpec((1, block, hidden), lambda e: (e, 0, 0)),
        ],
        out_specs=[pl.BlockSpec((1, hidden, features), lambda e: (e, 0, 0))] * 2,
        out_shape=[jax.ShapeDtypeStruct((experts, hidden, features), bf16)] * 2,
        compiler_params=params(GRANT),
        cost_estimate=cost(4 * experts * block * hidden * features, 4 * experts * hidden * features),
        name="weight_grads",
    )(place, mine, other, act, pre)


def sum_terms(terms, slot_in, column, copies):
    sources, block, features = terms.shape
    half = features // 2
    width = features + LANES

    def kernel(terms_ref, in_ref, column_ref, sent_ref):
        total = terms_ref[0].astype(f32)
        for source in range(1, sources):
            total = total + terms_ref[source].astype(f32)
        low = total.astype(bf16)
        inner = jnp.sum(in_ref[...] * low[:, half:].astype(f32), axis=1, keepdims=True)
        power, inverse = guarded(column_ref[:, 0:1])
        lanes = in_lanes(block, two_parts(inverse) + (power,) + two_parts(inner))
        for copy in range(copies):
            sent_ref[copy, :, :features] = low
            sent_ref[copy, :, features:] = lanes

    return pl.pallas_call(
        kernel,
        in_specs=[whole_in_vmem()] * 3,
        out_specs=whole_in_vmem(),
        out_shape=jax.ShapeDtypeStruct((copies, block, width), bf16),
        compiler_params=params(GRANT),
        name="sum_terms",
    )(terms, slot_in, column)


def all_exps(place, slot_keys, near_keys, far_keys, tokens, width, tile=256):
    features, block = slot_keys.shape
    count = tokens.shape[0]
    half = features // 2
    others = len(near_keys)
    slots = (others + 1) * block

    def kernel(place_ref, keys_ref, *refs):
        near_refs, far_refs = refs[:others], refs[others : 2 * others]
        (
            tokens_ref, all_ref, own_ref, row_ref, column_ref, rows_ref, turned_ref, found_ref
        ) = refs[2 * others :]
        core, at_own = place_ref[0], place_ref[1]
        here, there = halves(place_ref, half)

        def spot(at):
            return pl.ds(pl.multiple_of(at * block, block), block)

        own = spot(at_own)
        near_here = core == place_ref[2]
        firsts = [pl.multiple_of(place_ref[3 + whose] * width, 16) for whose in range(2)]
        turned_ref[own, :] = keys_ref[...].T
        for whose, first in enumerate(firsts):
            first = pl.multiple_of(place_ref[2] * half + first, 16)
            rows_ref[whose, :, own] = keys_ref[pl.ds(first, width), :]
        for at in range(others):
            place_at = spot(at_own ^ (at + 1))
            turned_ref[place_at, here] = near_refs[at][...].T
            turned_ref[place_at, there] = far_refs[at][...].T
            for whose, first in enumerate(firsts):
                rows = pl.ds(first, width)
                rows_ref[whose, :, place_at] = jnp.where(
                    near_here, near_refs[at][rows, :], far_refs[at][rows, :]
                )
        by_lane = jnp.zeros((block, LANES), f32)
        for at in range(0, count, tile):
            cut = slice(at, at + tile)
            found = jnp.exp(
                lax.dot_general(
                    turned_ref[...], tokens_ref[cut, :], cols_contract, preferred_element_type=f32
                )
            )
            found_ref[:, cut] = found
            all_ref[:, cut] = found.astype(bf16)
            row_ref[:, cut] = jnp.sum(found, axis=0, keepdims=True)
            exps = found_ref[own, cut]
            own_ref[:, cut] = exps
            for lanes in range(0, tile, LANES):
                by_lane = by_lane + exps[:, lanes : lanes + LANES]
        column_ref[...] = by_lane

    return pl.pallas_call(
        kernel,
        in_specs=[in_smem()] + [whole_in_vmem()] * (2 * others + 2),
        out_specs=[whole_in_vmem()] * 5,
        out_shape=[
            jax.ShapeDtypeStruct((slots, count), bf16),
            jax.ShapeDtypeStruct((block, count), f32),
            jax.ShapeDtypeStruct((1, count), f32),
            jax.ShapeDtypeStruct((block, LANES), f32),
            jax.ShapeDtypeStruct((2, width, slots), bf16),
        ],
        scratch_shapes=[
            pltpu.VMEM((slots, features), bf16),
            pltpu.VMEM((slots, count), f32),
        ],
        compiler_params=params(GRANT),
        cost_estimate=cost(2 * slots * features * count, 2 * features * count),
        name="all_exps",
    )(place, slot_keys, *near_keys, *far_keys, tokens)


def half_dot(place_ref, gathered_ref, ref, at, rows, own):
    blocks, block, _unused = gathered_ref.shape
    half = ref.shape[1] // 2
    here, there = halves(place_ref, half)
    return lax.dot_general(
        gathered_ref[:, :, at * half : (at + 1) * half].reshape(blocks * block, half),
        ref[rows, here if own else there],
        cols_contract,
        preferred_element_type=f32,
    )


def near_dots(place, out_grad, mine, slots, tile=256):
    count, features = out_grad.shape
    half = features // 2

    def kernel(place_ref, grad_ref, mine_ref, dot_ref, far_ref):
        _unused, there = halves(place_ref, half)
        far_ref[...] = grad_ref[:, there]
        for at in range(0, count, tile):
            cut = slice(at, at + tile)
            dot_ref[:, cut] = half_dot(place_ref, mine_ref, grad_ref, 0, cut, True)

    return pl.pallas_call(
        kernel,
        in_specs=[in_smem()] + [whole_in_vmem()] * 2,
        out_specs=[whole_in_vmem()] * 2,
        out_shape=[
            jax.ShapeDtypeStruct((slots, count), f32),
            jax.ShapeDtypeStruct((count, half), bf16),
        ],
        compiler_params=params(GRANT),
        cost_estimate=cost(slots * features * count, features * count),
        name="near_dots",
    )(place, out_grad, mine)


def comb_dots(exps, near, grad_far, row_parts, other, tile=256):
    slots, count = exps.shape
    half = grad_far.shape[1]

    def kernel(exp_ref, near_ref, grad_ref, row_ref, other_ref, dot_ref, sum_ref):
        slot_out = other_ref[:, :, :half].reshape(slots, half)
        for at in range(0, count, tile):
            cut = slice(at, at + tile)
            power, inverse = guarded(row_ref[:, cut])
            dots = near_ref[:, cut] + lax.dot_general(
                slot_out, grad_ref[cut, :], cols_contract, preferred_element_type=f32
            )
            dot_ref[:, cut] = dots
            terms = (exp_ref[:, cut].astype(f32) * power) * dots
            sum_ref[:, cut] = jnp.sum(terms, axis=0, keepdims=True) * inverse

    return pl.pallas_call(
        kernel,
        in_specs=[whole_in_vmem()] * 5,
        out_specs=[whole_in_vmem()] * 2,
        out_shape=[
            jax.ShapeDtypeStruct((slots, count), f32),
            jax.ShapeDtypeStruct((1, count), f32),
        ],
        compiler_params=params(GRANT),
        cost_estimate=cost(2 * slots * half * count, 2 * half * count),
        name="comb_dots",
    )(exps, near, grad_far, row_parts, other)


def disp_dots(place, exps, dots, tokens, row_parts, mine, other, width, tile=256):
    slots, count = exps.shape
    features = tokens.shape[1]
    half = features // 2

    def kernel(
        place_ref, exp_ref, dot_ref, tokens_ref, row_ref, mine_ref, other_ref,
        terms_ref, dispatch_ref, rows_ref, power_ref, inverse_ref, total_ref, turned_ref,
    ):
        lanes = mine_ref[:, :, features:].reshape(slots, LANES).astype(f32)
        apart = other_ref[:, :, features:].reshape(slots, LANES).astype(f32)
        inner = lanes[:, 3:4] + lanes[:, 4:5] + apart[:, 3:4] + apart[:, 4:5]
        power_ref[...] = jnp.broadcast_to(lanes[:, 2:3], (slots, tile))
        inverse_ref[...] = jnp.broadcast_to(lanes[:, 0:1] + lanes[:, 1:2], (slots, tile))
        total_ref[...] = jnp.broadcast_to(inner, (slots, tile))
        turned_ref[...] = jnp.where(
            place_ref[0] == place_ref[2], mine_ref[:, :, half:features], other_ref[:, :, half:features]
        ).reshape(slots, half).T
        for whose in range(2):
            first = pl.multiple_of(place_ref[3 + whose] * width, 16)
            rows_ref[whose] = turned_ref[pl.ds(first, width), :]
        for at in range(0, count, tile):
            cut = slice(at, at + tile)
            power, inverse = guarded(row_ref[:, cut])
            exps_here = exp_ref[:, cut].astype(f32)
            dispatch = (exps_here * power_ref[...]) * inverse_ref[...]
            dispatch_ref[:, cut] = dispatch.astype(bf16)
            disp_dot = half_dot(place_ref, mine_ref, tokens_ref, 1, cut, True)
            disp_dot = disp_dot + half_dot(place_ref, other_ref, tokens_ref, 1, cut, False)
            combine = (exps_here * power) * inverse
            terms_ref[:, cut] = combine * dot_ref[:, cut] + dispatch * (disp_dot - total_ref[...])

    return pl.pallas_call(
        kernel,
        in_specs=[in_smem()] + [whole_in_vmem()] * 6,
        out_specs=[whole_in_vmem()] * 3,
        out_shape=[
            jax.ShapeDtypeStruct((slots, count), f32),
            jax.ShapeDtypeStruct((slots, count), bf16),
            jax.ShapeDtypeStruct((2, width, slots), bf16),
        ],
        scratch_shapes=[pltpu.VMEM((slots, tile), f32)] * 3 + [pltpu.VMEM((half, slots), bf16)],
        compiler_params=params(GRANT),
        cost_estimate=cost(2 * slots * features * count, 2 * features * count),
        name="disp_dots",
    )(place, exps, dots, tokens, row_parts, mine, other)


def columns_dot(keys_rows_ref, grad_rows_ref, logit, dispatch, own):
    whose = 0 if own else 1
    total = jnp.dot(keys_rows_ref[whose], logit, preferred_element_type=f32)
    return total + jnp.dot(grad_rows_ref[whose], dispatch, preferred_element_type=f32)


def logit_grads(place, exps, terms, dispatch, row_parts, row, row_other, keys_rows, grad_rows, tile=256):
    slots, count = exps.shape
    width = keys_rows.shape[1]

    def kernel(
        place_ref, exp_ref, terms_ref, dispatch_ref, row_ref, sum_ref, other_ref, keys_rows_ref, grad_rows_ref,
        logit_ref, sent_ref,
    ):
        for at in range(0, count, tile):
            cut = slice(at, at + tile)
            power, inverse = guarded(row_ref[:, cut])
            weight = (sum_ref[:, cut] + other_ref[:, cut]) * inverse
            exps_here = exp_ref[:, cut].astype(f32)
            logit_ref[:, cut] = (terms_ref[:, cut] - (exps_here * power) * weight).astype(bf16)
            sent_ref[:, cut] = columns_dot(
                keys_rows_ref, grad_rows_ref, logit_ref[:, cut], dispatch_ref[:, cut], False
            ).astype(bf16)

    return pl.pallas_call(
        kernel,
        in_specs=[in_smem()] + [whole_in_vmem()] * 8,
        out_specs=[whole_in_vmem()] * 2,
        out_shape=[
            jax.ShapeDtypeStruct((slots, count), bf16),
            jax.ShapeDtypeStruct((width, count), bf16),
        ],
        compiler_params=params(GRANT),
        cost_estimate=cost(4 * slots * width * count, 4 * slots * count),
        name="logit_grads",
    )(place, exps, terms, dispatch, row_parts, row, row_other, keys_rows, grad_rows)


def own_parts(place, logit, dispatch, tokens, keys_rows, grad_rows, own_slots, chips, tile=256):
    count, features = tokens.shape
    width = keys_rows.shape[1]
    rows = features // (2 * chips)

    def kernel(place_ref, logit_ref, dispatch_ref, tokens_ref, keys_rows_ref, grad_rows_ref, keep_ref, give_ref, own_ref, keys_ref):
        own = pl.ds(pl.multiple_of(place_ref[1] * own_slots, own_slots), own_slots)
        total = jnp.dot(logit_ref[own, :], tokens_ref[...], preferred_element_type=f32)
        keys_ref[...] = total.T.astype(bf16)
        for chip in range(chips):
            for core, out_ref in ((place_ref[0], keep_ref), (1 - place_ref[0], give_ref)):
                first = pl.multiple_of(chip * 2 * rows + core * rows, 16)
                out_ref[chip] = keys_ref[pl.ds(first, rows), :]
        for at in range(0, count, tile):
            cut = slice(at, at + tile)
            own_ref[:, cut] = columns_dot(
                keys_rows_ref, grad_rows_ref, logit_ref[:, cut], dispatch_ref[:, cut], True
            )

    return pl.pallas_call(
        kernel,
        in_specs=[in_smem()] + [whole_in_vmem()] * 5,
        out_specs=[whole_in_vmem()] * 3,
        out_shape=[
            jax.ShapeDtypeStruct((chips, rows, own_slots), bf16),
            jax.ShapeDtypeStruct((chips, rows, own_slots), bf16),
            jax.ShapeDtypeStruct((width, count), f32),
        ],
        scratch_shapes=[pltpu.VMEM((features, own_slots), bf16)],
        compiler_params=params(GRANT),
        cost_estimate=cost(2 * own_slots * features * count, 2 * features * count),
        name="own_parts",
    )(place, logit, dispatch, tokens, keys_rows, grad_rows)


def per_device(tokens, slot_keys, w_in, w_out, out_grad):
    features = tokens.shape[1]
    own_slots = slot_keys.shape[1]
    slot_devices = lax.axis_size(SLOT)
    groups = lax.axis_size(CHIPS)
    everyone = lax.axis_size(GATHERED) // 2
    quarter = everyone // 2
    across = [
        [*range(first, first + quarter), *range(4 * quarter - first - quarter, 4 * quarter - first)]
        for first in (0, quarter)
    ]
    width = features // slot_devices
    swap = [(0, 1), (1, 0)]
    pair_at, depth_at = lax.axis_index("xa"), lax.axis_index("zh")
    place = jnp.stack(
        [
            lax.axis_index("c"),
            lax.axis_index(KEYS),
            lax.axis_index("xb"),
            2 * pair_at + depth_at,
            2 * (1 - pair_at) + depth_at,
        ]
    ).astype(jnp.int32)

    half = features // 2
    own_half = lax.dynamic_slice_in_dim(slot_keys, lax.axis_index("c") * half, half, 0)
    blocks = lax.axis_size(KEYS)
    near_keys = [
        lax.ppermute(own_half, SLOT, [(at, at ^ other) for at in range(slot_devices)])
        for other in (1, 6, 7)
    ]
    far_keys = [lax.ppermute(keys, "c", swap) for keys in near_keys]
    all_exp, exps, row_sum, column, keys_rows = all_exps(
        place, slot_keys, near_keys, far_keys, tokens, width
    )
    column_other = lax.ppermute(column, "c", swap)
    row_sum_other = lax.ppermute(row_sum, "xa", swap)
    slot_in_part = dispatch_part(exps, column, column_other, tokens)
    keep, give, row_parts = combine_part(
        place, exps, row_sum, row_sum_other, column, column_other, slot_in_part, out_grad, groups
    )
    parts = lax.all_to_all(pair_sum(keep, lax.ppermute(give, "c", swap)), CHIPS, 0, 0)
    sent, slot_in, column_total = sum_slots(parts, groups)
    mine = lax.all_to_all(sent, CHIPS, 0, 0)
    other = lax.ppermute(mine, "c", swap)

    keep, give, act, pre = experts_part(place, mine, other, w_in, w_out)
    sent = pair_sum(keep, lax.ppermute(give, "c", swap))
    terms = lax.all_to_all(sent, CHIPS, 0, 0)
    terms, act, pre = lax.optimization_barrier((terms, act, pre))
    sent = sum_terms(terms, slot_in, column_total, everyone)
    gathered = lax.all_to_all(sent, GATHERED, 0, 0, axis_index_groups=across)
    grad_w_in, grad_w_out = weight_grads(place, mine, other, act, pre)
    gathered, grad_w_in, grad_w_out = lax.optimization_barrier((gathered, grad_w_in, grad_w_out))
    gathered_other = lax.ppermute(gathered, "c", swap)

    near, grad_far = near_dots(place, out_grad, gathered, all_exp.shape[0])
    gathered_other, near = lax.optimization_barrier((gathered_other, near))
    dots, row = comb_dots(all_exp, near, grad_far, row_parts, gathered_other)
    row_other = lax.ppermute(row, "xa", swap)
    terms, dispatch, grad_rows = disp_dots(
        place, all_exp, dots, tokens, row_parts, gathered, gathered_other, width
    )
    logit, sent = logit_grads(
        place, all_exp, terms, dispatch, row_parts, row, row_other, keys_rows, grad_rows
    )
    received = lax.ppermute(sent, "xa", swap)
    keep, give, own_grads = own_parts(
        place, logit, dispatch, tokens, keys_rows, grad_rows, own_slots, groups
    )
    keys_parts = lax.all_to_all(
        pair_sum(keep, lax.ppermute(give, "c", swap)), CHIPS, 0, 0
    )
    grad_tokens = (own_grads + received.astype(f32)).astype(bf16).T
    grad_keys = jnp.sum(keys_parts.astype(f32), axis=0)
    return (grad_tokens, grad_keys, grad_w_in, grad_w_out)


def solution(mesh):
    fine = Mesh(mesh.devices.reshape(2, 4, 2, 2, 2, 2), ("zl", "y", "c", "xb", "xa", "zh"))
    placed = (
        P(SEQ, None),
        P(None, SLOT),
        P(SLOT, SEQ, None),
        P(SLOT, SEQ, None),
        P(SEQ, None),
    )
    return jax.shard_map(
        per_device,
        mesh=fine,
        in_specs=placed,
        out_specs=(
            P(SEQ, SLOT),
            P(SEQ, SLOT),
            P(SLOT, SEQ, None),
            P(SLOT, SEQ, None),
        ),
        check_vma=False,
    )
```

```python
import jax
import jax.numpy as jnp
from jax import lax
from jax.experimental import pallas as pl
from jax.experimental.pallas import tpu as pltpu
from jax.sharding import Mesh, PartitionSpec as P

gelu_scale = 0.7978845608
gelu_cubic = 0.044715
rows_contract = (((0,), (0,)), ((), ()))
cols_contract = (((1,), (1,)), ((), ()))

SEQ = ("zl", "y", "c")
SLOT = ("xb", "xa", "zh")
KEYS = ("xb", "zh")
CHIPS = ("zl", "y")
GATHERED = ("xb", "xa", "zh", "zl", "y")
f32 = jnp.float32
bf16 = jnp.bfloat16
LANES = 128
MIB = 1 << 20
GRANT = 16
SCALE = 1


def gelu_tanh(values):
    return (
        0.5
        * values
        * (1.0 + jnp.tanh(gelu_scale * (values + gelu_cubic * values * values * values)))
    )


def gelu_slope(values):
    bent = jnp.tanh(gelu_scale * (values + gelu_cubic * values * values * values))
    return 0.5 * (1.0 + bent) + 0.5 * values * (1.0 - bent * bent) * gelu_scale * (
        1.0 + 3.0 * gelu_cubic * values * values
    )


def guarded(total):
    power = jnp.where(total > 2.0**64, 2.0**-32, jnp.where(total < 2.0**-64, 2.0**32, 1.0))
    return power, 1.0 / (total * power)


def two_parts(values):
    high = values.astype(bf16).astype(f32)
    return high, values - high


def in_lanes(rows, columns):
    lane = lax.broadcasted_iota(jnp.int32, (rows, LANES), 1)
    laid = jnp.zeros((rows, LANES), f32)
    for at, column in enumerate(columns):
        laid = jnp.where(lane == at, column, laid)
    return laid.astype(bf16)


def params(mib):
    return pltpu.CompilerParams(vmem_limit_bytes=mib * MIB)


def cost(flops, nbytes):
    return pl.CostEstimate(flops=SCALE * flops, bytes_accessed=nbytes, transcendentals=0)


def whole_in_vmem():
    return pl.BlockSpec(memory_space=pltpu.VMEM)


def in_smem():
    return pl.BlockSpec(memory_space=pltpu.SMEM)


def halves(place_ref, half):
    core = place_ref[0]
    here = pl.ds(pl.multiple_of(core * half, LANES), half)
    there = pl.ds(pl.multiple_of((1 - core) * half, LANES), half)
    return here, there


def dispatch_part(exps, column, column_other, tokens):
    slots, count = exps.shape
    features = tokens.shape[1]

    def kernel(exp_ref, column_ref, other_ref, tokens_ref, out_ref, weights_ref):
        total = jnp.sum(column_ref[...] + other_ref[...], axis=1, keepdims=True)
        power, inverse = guarded(jnp.where(total > 0, total, 1.0))
        weights_ref[...] = ((exp_ref[...] * power) * inverse).astype(bf16)
        out_ref[...] = jnp.dot(
            weights_ref[...], tokens_ref[...], preferred_element_type=f32
        ).astype(bf16)

    return pl.pallas_call(
        kernel,
        in_specs=[whole_in_vmem()] * 4,
        out_specs=whole_in_vmem(),
        out_shape=jax.ShapeDtypeStruct((slots, features), bf16),
        scratch_shapes=[pltpu.VMEM((slots, count), bf16)],
        compiler_params=params(GRANT),
        cost_estimate=cost(2 * slots * features * count, 2 * features * count),
        name="dispatch_part",
    )(exps, column, column_other, tokens)


def combine_part(place, exps, row, row_other, column, column_other, slot_in_part, out_grad, groups):
    slots, count = exps.shape
    features = out_grad.shape[1]
    half = features // 2
    block = slots // groups

    def kernel(
        place_ref, exp_ref, row_ref, row_other_ref, column_ref, other_ref, in_ref, grad_ref,
        keep_ref, give_ref, row_total_ref, weights_ref, total_ref,
    ):
        row_total_ref[...] = row_ref[...] + row_other_ref[...]
        power, inverse = guarded(row_total_ref[...])
        weights_ref[...] = ((exp_ref[...] * power) * inverse).astype(bf16)
        total = jnp.sum(column_ref[...] + other_ref[...], axis=1, keepdims=True)
        shift, _unused = guarded(total)
        high, low = two_parts(total * shift)
        lanes = in_lanes(slots, (high, low, 1.0 / shift))
        total_ref[...] = jnp.dot(
            weights_ref[...], grad_ref[...], preferred_element_type=f32
        ).astype(bf16)
        here, there = halves(place_ref, half)
        for group in range(groups):
            rows = slice(group * block, (group + 1) * block)
            keep_ref[group, :, :half] = in_ref[rows, here]
            keep_ref[group, :, half:features] = total_ref[rows, here]
            keep_ref[group, :, features:] = lanes[rows]
            give_ref[group, :, :half] = in_ref[rows, there]
            give_ref[group, :, half:] = total_ref[rows, there]

    return pl.pallas_call(
        kernel,
        in_specs=[in_smem()] + [whole_in_vmem()] * 7,
        out_specs=[whole_in_vmem()] * 3,
        out_shape=[
            jax.ShapeDtypeStruct((groups, block, features + LANES), bf16),
            jax.ShapeDtypeStruct((groups, block, features), bf16),
            jax.ShapeDtypeStruct((1, count), f32),
        ],
        scratch_shapes=[
            pltpu.VMEM((slots, count), bf16),
            pltpu.VMEM((slots, features), bf16),
        ],
        compiler_params=params(GRANT),
        cost_estimate=cost(2 * slots * features * count, 2 * features * count),
        name="combine_part",
    )(place, exps, row, row_other, column, column_other, slot_in_part, out_grad)


def pair_sum(keep, received):
    features = received.shape[2]

    def kernel(keep_ref, received_ref, out_ref):
        total = keep_ref[:, :, :features].astype(f32) + received_ref[...].astype(f32)
        out_ref[:, :, :features] = total.astype(bf16)
        if keep_ref.shape[2] > features:
            out_ref[:, :, features:] = keep_ref[:, :, features:]

    return pl.pallas_call(
        kernel,
        in_specs=[whole_in_vmem()] * 2,
        out_specs=whole_in_vmem(),
        out_shape=jax.ShapeDtypeStruct(keep.shape, bf16),
        compiler_params=params(GRANT),
        name="pair_sum",
    )(keep, received)


def sum_slots(parts, copies):
    sources, block, width = parts.shape
    features = width - LANES
    half = features // 2

    def kernel(parts_ref, sent_ref, in_ref, column_ref):
        lanes = parts_ref[:, :, features:].astype(f32)
        columns = (lanes[:, :, 0:1] + lanes[:, :, 1:2]) * lanes[:, :, 2:3]
        total = jnp.sum(columns, axis=0)
        power, inverse = guarded(total)
        share = (columns * power[None]) * inverse[None]
        slot_in = jnp.zeros((block, half), f32)
        slot_grad = jnp.zeros((block, half), f32)
        for source in range(sources):
            slot_in = slot_in + parts_ref[source, :, :half].astype(f32) * share[source]
            slot_grad = slot_grad + parts_ref[source, :, half:features].astype(f32)
        in_ref[...] = slot_in
        column_ref[...] = jnp.broadcast_to(total, (block, LANES))
        in_low = slot_in.astype(bf16)
        grad_low = slot_grad.astype(bf16)
        for copy in range(copies):
            sent_ref[copy, :, :half] = in_low
            sent_ref[copy, :, half:] = grad_low

    return pl.pallas_call(
        kernel,
        in_specs=[whole_in_vmem()],
        out_specs=[whole_in_vmem()] * 3,
        out_shape=[
            jax.ShapeDtypeStruct((copies, block, features), bf16),
            jax.ShapeDtypeStruct((block, half), f32),
            jax.ShapeDtypeStruct((block, LANES), f32),
        ],
        compiler_params=params(GRANT),
        name="sum_slots",
    )(parts)


def experts_part(place, mine, other, w_in, w_out):
    experts, hidden, features = w_in.shape
    block = mine.shape[1]
    half = features // 2

    def kernel(place_ref, mine_ref, other_ref, w_in_ref, w_out_ref, keep_ref, give_ref, act_hbm, pre_hbm, act_ref, pre_ref, whole_ref, out_ref, sems):
        here, there = halves(place_ref, half)

        def inward(at, weights_ref, e):
            cut = slice(at * half, (at + 1) * half)
            whole_ref[e, at, :, here] = mine_ref[e, :, cut]
            whole_ref[e, at, :, there] = other_ref[e, :, cut]
            return lax.dot_general(
                whole_ref[e, at], weights_ref[e], cols_contract, preferred_element_type=f32
            )

        for e in range(experts):
            hidden_pre = inward(0, w_in_ref, e)
            act_grad = inward(1, w_out_ref, e)
            act = gelu_tanh(hidden_pre).astype(bf16)
            pre = (act_grad * gelu_slope(hidden_pre)).astype(bf16)
            out_ref[e, 0] = jnp.dot(act, w_out_ref[e], preferred_element_type=f32).astype(bf16)
            out_ref[e, 1] = jnp.dot(pre, w_in_ref[e], preferred_element_type=f32).astype(bf16)
            for cut, sent_ref in ((here, keep_ref), (there, give_ref)):
                sent_ref[e, :, :half] = out_ref[e, 0, :, cut]
                sent_ref[e, :, half:] = out_ref[e, 1, :, cut]
            act_ref[e] = act
            pre_ref[e] = pre
        first = pltpu.make_async_copy(act_ref, act_hbm, sems.at[0])
        second = pltpu.make_async_copy(pre_ref, pre_hbm, sems.at[1])
        first.start()
        second.start()
        first.wait()
        second.wait()

    return pl.pallas_call(
        kernel,
        in_specs=[in_smem()] + [whole_in_vmem()] * 4,
        out_specs=[whole_in_vmem()] * 2 + [pl.BlockSpec(memory_space=pltpu.HBM)] * 2,
        out_shape=[
            jax.ShapeDtypeStruct((experts, block, features), bf16),
            jax.ShapeDtypeStruct((experts, block, features), bf16),
            jax.ShapeDtypeStruct((experts, block, hidden), bf16),
            jax.ShapeDtypeStruct((experts, block, hidden), bf16),
        ],
        scratch_shapes=[pltpu.VMEM((experts, block, hidden), bf16)] * 2
        + [pltpu.VMEM((experts, 2, block, features), bf16)] * 2
        + [pltpu.SemaphoreType.DMA((2,))],
        compiler_params=params(GRANT),
        cost_estimate=cost(8 * experts * block * hidden * features, 4 * experts * hidden * features),
        name="experts_part",
    )(place, mine, other, w_in, w_out)


def weight_grads(place, mine, other, act, pre):
    experts, block, hidden = act.shape
    features = mine.shape[2]
    half = features // 2

    def kernel(place_ref, mine_ref, other_ref, act_ref, pre_ref, in_ref, out_ref):
        here, there = halves(place_ref, half)
        for cut, from_ref in ((here, mine_ref), (there, other_ref)):
            in_ref[0, :, cut] = lax.dot_general(
                pre_ref[0], from_ref[0, :, :half], rows_contract, preferred_element_type=f32
            ).astype(bf16)
            out_ref[0, :, cut] = lax.dot_general(
                act_ref[0], from_ref[0, :, half:], rows_contract, preferred_element_type=f32
            ).astype(bf16)

    return pl.pallas_call(
        kernel,
        grid=(experts,),
        in_specs=[
            in_smem(),
            pl.BlockSpec((1, block, features), lambda e: (e, 0, 0)),
            pl.BlockSpec((1, block, features), lambda e: (e, 0, 0)),
            pl.BlockSpec((1, block, hidden), lambda e: (e, 0, 0)),
            pl.BlockSpec((1, block, hidden), lambda e: (e, 0, 0)),
        ],
        out_specs=[pl.BlockSpec((1, hidden, features), lambda e: (e, 0, 0))] * 2,
        out_shape=[jax.ShapeDtypeStruct((experts, hidden, features), bf16)] * 2,
        compiler_params=params(GRANT),
        cost_estimate=cost(4 * experts * block * hidden * features, 4 * experts * hidden * features),
        name="weight_grads",
    )(place, mine, other, act, pre)


def sum_terms(terms, slot_in, column, copies):
    sources, block, features = terms.shape
    half = features // 2
    width = features + LANES

    def kernel(terms_ref, in_ref, column_ref, sent_ref):
        total = terms_ref[0].astype(f32)
        for source in range(1, sources):
            total = total + terms_ref[source].astype(f32)
        low = total.astype(bf16)
        inner = jnp.sum(in_ref[...] * low[:, half:].astype(f32), axis=1, keepdims=True)
        power, inverse = guarded(column_ref[:, 0:1])
        lanes = in_lanes(block, two_parts(inverse) + (power,) + two_parts(inner))
        for copy in range(copies):
            sent_ref[copy, :, :features] = low
            sent_ref[copy, :, features:] = lanes

    return pl.pallas_call(
        kernel,
        in_specs=[whole_in_vmem()] * 3,
        out_specs=whole_in_vmem(),
        out_shape=jax.ShapeDtypeStruct((copies, block, width), bf16),
        compiler_params=params(GRANT),
        name="sum_terms",
    )(terms, slot_in, column)


def all_exps(place, slot_keys, near_keys, far_keys, tokens, width, tile=256):
    features, block = slot_keys.shape
    count = tokens.shape[0]
    half = features // 2
    others = len(near_keys)
    slots = (others + 1) * block

    def kernel(place_ref, keys_ref, *refs):
        near_refs, far_refs = refs[:others], refs[others : 2 * others]
        (
            tokens_ref, all_ref, own_ref, row_ref, column_ref, rows_ref, turned_ref, found_ref
        ) = refs[2 * others :]
        core, at_own = place_ref[0], place_ref[1]
        here, there = halves(place_ref, half)

        def spot(at):
            return pl.ds(pl.multiple_of(at * block, block), block)

        own = spot(at_own)
        near_here = core == place_ref[2]
        firsts = [pl.multiple_of(place_ref[3 + whose] * width, 16) for whose in range(2)]
        turned_ref[own, :] = keys_ref[...].T
        for whose, first in enumerate(firsts):
            first = pl.multiple_of(place_ref[2] * half + first, 16)
            rows_ref[whose, :, own] = keys_ref[pl.ds(first, width), :]
        for at in range(others):
            place_at = spot(at_own ^ (at + 1))
            turned_ref[place_at, here] = near_refs[at][...].T
            turned_ref[place_at, there] = far_refs[at][...].T
            for whose, first in enumerate(firsts):
                rows = pl.ds(first, width)
                rows_ref[whose, :, place_at] = jnp.where(
                    near_here, near_refs[at][rows, :], far_refs[at][rows, :]
                )
        by_lane = jnp.zeros((block, LANES), f32)
        for at in range(0, count, tile):
            cut = slice(at, at + tile)
            found = jnp.exp(
                lax.dot_general(
                    turned_ref[...], tokens_ref[cut, :], cols_contract, preferred_element_type=f32
                )
            )
            found_ref[:, cut] = found
            all_ref[:, cut] = found.astype(bf16)
            row_ref[:, cut] = jnp.sum(found, axis=0, keepdims=True)
            exps = found_ref[own, cut]
            own_ref[:, cut] = exps
            for lanes in range(0, tile, LANES):
                by_lane = by_lane + exps[:, lanes : lanes + LANES]
        column_ref[...] = by_lane

    return pl.pallas_call(
        kernel,
        in_specs=[in_smem()] + [whole_in_vmem()] * (2 * others + 2),
        out_specs=[whole_in_vmem()] * 5,
        out_shape=[
            jax.ShapeDtypeStruct((slots, count), bf16),
            jax.ShapeDtypeStruct((block, count), f32),
            jax.ShapeDtypeStruct((1, count), f32),
            jax.ShapeDtypeStruct((block, LANES), f32),
            jax.ShapeDtypeStruct((2, width, slots), bf16),
        ],
        scratch_shapes=[
            pltpu.VMEM((slots, features), bf16),
            pltpu.VMEM((slots, count), f32),
        ],
        compiler_params=params(GRANT),
        cost_estimate=cost(2 * slots * features * count, 2 * features * count),
        name="all_exps",
    )(place, slot_keys, *near_keys, *far_keys, tokens)


def half_dot(place_ref, gathered_ref, ref, at, rows, own):
    blocks, block, _unused = gathered_ref.shape
    half = ref.shape[1] // 2
    here, there = halves(place_ref, half)
    return lax.dot_general(
        gathered_ref[:, :, at * half : (at + 1) * half].reshape(blocks * block, half),
        ref[rows, here if own else there],
        cols_contract,
        preferred_element_type=f32,
    )


def near_dots(place, out_grad, mine, slots, tile=256):
    count, features = out_grad.shape
    half = features // 2

    def kernel(place_ref, grad_ref, mine_ref, dot_ref, far_ref):
        _unused, there = halves(place_ref, half)
        far_ref[...] = grad_ref[:, there]
        for at in range(0, count, tile):
            cut = slice(at, at + tile)
            dot_ref[:, cut] = half_dot(place_ref, mine_ref, grad_ref, 0, cut, True)

    return pl.pallas_call(
        kernel,
        in_specs=[in_smem()] + [whole_in_vmem()] * 2,
        out_specs=[whole_in_vmem()] * 2,
        out_shape=[
            jax.ShapeDtypeStruct((slots, count), f32),
            jax.ShapeDtypeStruct((count, half), bf16),
        ],
        compiler_params=params(GRANT),
        cost_estimate=cost(slots * features * count, features * count),
        name="near_dots",
    )(place, out_grad, mine)


def comb_dots(exps, near, grad_far, row_parts, other, tile=256):
    slots, count = exps.shape
    half = grad_far.shape[1]

    def kernel(exp_ref, near_ref, grad_ref, row_ref, other_ref, dot_ref, sum_ref):
        slot_out = other_ref[:, :, :half].reshape(slots, half)
        for at in range(0, count, tile):
            cut = slice(at, at + tile)
            power, inverse = guarded(row_ref[:, cut])
            dots = near_ref[:, cut] + lax.dot_general(
                slot_out, grad_ref[cut, :], cols_contract, preferred_element_type=f32
            )
            terms = ((exp_ref[:, cut].astype(f32) * power) * inverse) * dots
            dot_ref[:, cut] = terms
            sum_ref[:, cut] = jnp.sum(terms, axis=0, keepdims=True)

    return pl.pallas_call(
        kernel,
        in_specs=[whole_in_vmem()] * 5,
        out_specs=[whole_in_vmem()] * 2,
        out_shape=[
            jax.ShapeDtypeStruct((slots, count), f32),
            jax.ShapeDtypeStruct((1, count), f32),
        ],
        compiler_params=params(GRANT),
        cost_estimate=cost(2 * slots * half * count, 2 * half * count),
        name="comb_dots",
    )(exps, near, grad_far, row_parts, other)


def disp_dots(place, exps, dots, tokens, mine, other, width, tile=256):
    slots, count = exps.shape
    features = tokens.shape[1]
    half = features // 2

    def kernel(
        place_ref, exp_ref, dot_ref, tokens_ref, mine_ref, other_ref,
        terms_ref, dispatch_ref, rows_ref, power_ref, inverse_ref, total_ref, turned_ref,
    ):
        lanes = mine_ref[:, :, features:].reshape(slots, LANES).astype(f32)
        apart = other_ref[:, :, features:].reshape(slots, LANES).astype(f32)
        inner = lanes[:, 3:4] + lanes[:, 4:5] + apart[:, 3:4] + apart[:, 4:5]
        power_ref[...] = jnp.broadcast_to(lanes[:, 2:3], (slots, tile))
        inverse_ref[...] = jnp.broadcast_to(lanes[:, 0:1] + lanes[:, 1:2], (slots, tile))
        total_ref[...] = jnp.broadcast_to(inner, (slots, tile))
        turned_ref[...] = jnp.where(
            place_ref[0] == place_ref[2], mine_ref[:, :, half:features], other_ref[:, :, half:features]
        ).reshape(slots, half).T
        for whose in range(2):
            first = pl.multiple_of(place_ref[3 + whose] * width, 16)
            rows_ref[whose] = turned_ref[pl.ds(first, width), :]
        for at in range(0, count, tile):
            cut = slice(at, at + tile)
            exps_here = exp_ref[:, cut].astype(f32)
            dispatch = (exps_here * power_ref[...]) * inverse_ref[...]
            dispatch_ref[:, cut] = dispatch.astype(bf16)
            disp_dot = half_dot(place_ref, mine_ref, tokens_ref, 1, cut, True)
            disp_dot = disp_dot + half_dot(place_ref, other_ref, tokens_ref, 1, cut, False)
            terms_ref[:, cut] = dot_ref[:, cut] + dispatch * (disp_dot - total_ref[...])

    return pl.pallas_call(
        kernel,
        in_specs=[in_smem()] + [whole_in_vmem()] * 5,
        out_specs=[whole_in_vmem()] * 3,
        out_shape=[
            jax.ShapeDtypeStruct((slots, count), f32),
            jax.ShapeDtypeStruct((slots, count), bf16),
            jax.ShapeDtypeStruct((2, width, slots), bf16),
        ],
        scratch_shapes=[pltpu.VMEM((slots, tile), f32)] * 3 + [pltpu.VMEM((half, slots), bf16)],
        compiler_params=params(GRANT),
        cost_estimate=cost(2 * slots * features * count, 2 * features * count),
        name="disp_dots",
    )(place, exps, dots, tokens, mine, other)


def columns_dot(keys_rows_ref, grad_rows_ref, logit, dispatch, own):
    whose = 0 if own else 1
    total = jnp.dot(keys_rows_ref[whose], logit, preferred_element_type=f32)
    return total + jnp.dot(grad_rows_ref[whose], dispatch, preferred_element_type=f32)


def logit_grads(place, exps, terms, dispatch, row_parts, row, row_other, keys_rows, grad_rows, tile=256):
    slots, count = exps.shape
    width = keys_rows.shape[1]

    def kernel(
        place_ref, exp_ref, terms_ref, dispatch_ref, row_ref, sum_ref, other_ref, keys_rows_ref, grad_rows_ref,
        logit_ref, sent_ref,
    ):
        for at in range(0, count, tile):
            cut = slice(at, at + tile)
            power, inverse = guarded(row_ref[:, cut])
            weight = (sum_ref[:, cut] + other_ref[:, cut]) * inverse
            exps_here = exp_ref[:, cut].astype(f32)
            logit_ref[:, cut] = (terms_ref[:, cut] - (exps_here * power) * weight).astype(bf16)
            sent_ref[:, cut] = columns_dot(
                keys_rows_ref, grad_rows_ref, logit_ref[:, cut], dispatch_ref[:, cut], False
            ).astype(bf16)

    return pl.pallas_call(
        kernel,
        in_specs=[in_smem()] + [whole_in_vmem()] * 8,
        out_specs=[whole_in_vmem()] * 2,
        out_shape=[
            jax.ShapeDtypeStruct((slots, count), bf16),
            jax.ShapeDtypeStruct((width, count), bf16),
        ],
        compiler_params=params(GRANT),
        cost_estimate=cost(4 * slots * width * count, 4 * slots * count),
        name="logit_grads",
    )(place, exps, terms, dispatch, row_parts, row, row_other, keys_rows, grad_rows)


def own_parts(place, logit, dispatch, tokens, keys_rows, grad_rows, own_slots, chips, tile=256):
    count, features = tokens.shape
    width = keys_rows.shape[1]
    rows = features // (2 * chips)

    def kernel(place_ref, logit_ref, dispatch_ref, tokens_ref, keys_rows_ref, grad_rows_ref, keep_ref, give_ref, own_ref, keys_ref):
        own = pl.ds(pl.multiple_of(place_ref[1] * own_slots, own_slots), own_slots)
        total = jnp.dot(logit_ref[own, :], tokens_ref[...], preferred_element_type=f32)
        keys_ref[...] = total.T.astype(bf16)
        for chip in range(chips):
            for core, out_ref in ((place_ref[0], keep_ref), (1 - place_ref[0], give_ref)):
                first = pl.multiple_of(chip * 2 * rows + core * rows, 16)
                out_ref[chip] = keys_ref[pl.ds(first, rows), :]
        for at in range(0, count, tile):
            cut = slice(at, at + tile)
            own_ref[:, cut] = columns_dot(
                keys_rows_ref, grad_rows_ref, logit_ref[:, cut], dispatch_ref[:, cut], True
            )

    return pl.pallas_call(
        kernel,
        in_specs=[in_smem()] + [whole_in_vmem()] * 5,
        out_specs=[whole_in_vmem()] * 3,
        out_shape=[
            jax.ShapeDtypeStruct((chips, rows, own_slots), bf16),
            jax.ShapeDtypeStruct((chips, rows, own_slots), bf16),
            jax.ShapeDtypeStruct((width, count), f32),
        ],
        scratch_shapes=[pltpu.VMEM((features, own_slots), bf16)],
        compiler_params=params(GRANT),
        cost_estimate=cost(2 * own_slots * features * count, 2 * features * count),
        name="own_parts",
    )(place, logit, dispatch, tokens, keys_rows, grad_rows)


def per_device(tokens, slot_keys, w_in, w_out, out_grad):
    features = tokens.shape[1]
    own_slots = slot_keys.shape[1]
    slot_devices = lax.axis_size(SLOT)
    groups = lax.axis_size(CHIPS)
    everyone = lax.axis_size(GATHERED) // 2
    quarter = everyone // 2
    across = [
        [*range(first, first + quarter), *range(4 * quarter - first - quarter, 4 * quarter - first)]
        for first in (0, quarter)
    ]
    width = features // slot_devices
    swap = [(0, 1), (1, 0)]
    pair_at, depth_at = lax.axis_index("xa"), lax.axis_index("zh")
    place = jnp.stack(
        [
            lax.axis_index("c"),
            lax.axis_index(KEYS),
            lax.axis_index("xb"),
            2 * pair_at + depth_at,
            2 * (1 - pair_at) + depth_at,
        ]
    ).astype(jnp.int32)

    half = features // 2
    own_half = lax.dynamic_slice_in_dim(slot_keys, lax.axis_index("c") * half, half, 0)
    blocks = lax.axis_size(KEYS)
    near_keys = [
        lax.ppermute(own_half, SLOT, [(at, at ^ other) for at in range(slot_devices)])
        for other in (1, 6, 7)
    ]
    far_keys = [lax.ppermute(keys, "c", swap) for keys in near_keys]
    all_exp, exps, row_sum, column, keys_rows = all_exps(
        place, slot_keys, near_keys, far_keys, tokens, width
    )
    column_other = lax.ppermute(column, "c", swap)
    row_sum_other = lax.ppermute(row_sum, "xa", swap)
    slot_in_part = dispatch_part(exps, column, column_other, tokens)
    keep, give, row_parts = combine_part(
        place, exps, row_sum, row_sum_other, column, column_other, slot_in_part, out_grad, groups
    )
    parts = lax.all_to_all(pair_sum(keep, lax.ppermute(give, "c", swap)), CHIPS, 0, 0)
    sent, slot_in, column_total = sum_slots(parts, groups)
    mine = lax.all_to_all(sent, CHIPS, 0, 0)
    other = lax.ppermute(mine, "c", swap)

    keep, give, act, pre = experts_part(place, mine, other, w_in, w_out)
    sent = pair_sum(keep, lax.ppermute(give, "c", swap))
    terms = lax.all_to_all(sent, CHIPS, 0, 0)
    terms, act, pre = lax.optimization_barrier((terms, act, pre))
    sent = sum_terms(terms, slot_in, column_total, everyone)
    gathered = lax.all_to_all(sent, GATHERED, 0, 0, axis_index_groups=across)
    grad_w_in, grad_w_out = weight_grads(place, mine, other, act, pre)
    gathered, grad_w_in, grad_w_out = lax.optimization_barrier((gathered, grad_w_in, grad_w_out))
    gathered_other = lax.ppermute(gathered, "c", swap)

    near, grad_far = near_dots(place, out_grad, gathered, all_exp.shape[0])
    gathered_other, near = lax.optimization_barrier((gathered_other, near))
    dots, row = comb_dots(all_exp, near, grad_far, row_parts, gathered_other)
    row_other = lax.ppermute(row, "xa", swap)
    terms, dispatch, grad_rows = disp_dots(
        place, all_exp, dots, tokens, gathered, gathered_other, width
    )
    logit, sent = logit_grads(
        place, all_exp, terms, dispatch, row_parts, row, row_other, keys_rows, grad_rows
    )
    received = lax.ppermute(sent, "xa", swap)
    keep, give, own_grads = own_parts(
        place, logit, dispatch, tokens, keys_rows, grad_rows, own_slots, groups
    )
    keys_parts = lax.all_to_all(
        pair_sum(keep, lax.ppermute(give, "c", swap)), CHIPS, 0, 0
    )
    grad_tokens = (own_grads + received.astype(f32)).astype(bf16).T
    grad_keys = jnp.sum(keys_parts.astype(f32), axis=0)
    return (grad_tokens, grad_keys, grad_w_in, grad_w_out)


def solution(mesh):
    fine = Mesh(mesh.devices.reshape(2, 4, 2, 2, 2, 2), ("zl", "y", "c", "xb", "xa", "zh"))
    placed = (
        P(SEQ, None),
        P(None, SLOT),
        P(SLOT, SEQ, None),
        P(SLOT, SEQ, None),
        P(SEQ, None),
    )
    return jax.shard_map(
        per_device,
        mesh=fine,
        in_specs=placed,
        out_specs=(
            P(SEQ, SLOT),
            P(SEQ, SLOT),
            P(SLOT, SEQ, None),
            P(SLOT, SEQ, None),
        ),
        check_vma=False,
    )
```
